512 devices in a mesh: var: 8 (over z_lo), lat: 64 (over z_hi, x, y, core).
Axes of the slice: x: 4, y: 4, z: 16 (z_hi: 2, z_lo: 8; z = z_hi * 8 + z_lo), core: 2. Of those that a mesh axis runs over, the one named last changes fastest.
Arguments:
- fields: bfloat16 [64, 1536, 384], P('var', 'lat'), may hold values from -6 to 6
- field_ids: int32 [64], replicated, may hold values from 0 to 63, each once
- embed_w: bfloat16 [64, 16, 512], replicated, may hold values from -1.5 to 1.5
- lat_query: bfloat16 [4, 512], replicated, may hold values from -3 to 3
- perc_wk: bfloat16 [512, 512], replicated, may hold values from -10 to 10
- perc_wv: bfloat16 [512, 512], replicated, may hold values from -0.25 to 0.25
- swin_qkv: bfloat16 [512, 1536], replicated, may hold values from -12 to 12
- swin_wo: bfloat16 [512, 512], replicated, may hold values from -0.25 to 0.25
- row_window: int32 [384], replicated, may hold values from 0 to 127, never falling along the last dimension, each value on 1 to 6 neighbouring positions
- lon_shift: int32 [2], replicated, may hold values from 1 to 11, as said below
Outputs:
- encoded: bfloat16 [4, 384, 96, 512], P(None, 'lat', 'var')
The draws below stay inside these ranges and needn't reach their ends.
Inputs may be any that keep to these rules, and one draw needn't show every extreme that they name: `row_window`: window ids never fall along the rows, and one id covers at most 6 consecutive rows; some id covers exactly 6. `lon_shift`: the shifts are distinct, and the largest is exactly 11.
All inputs are finite; a program needn't handle non-finite values.
Results may differ from the reference program's by a relative error of at most 0.019.
The reference program's roundings to bfloat16 on the way count: a program that leaves them out, or rounds other values in their place, can miss the bound.
Values may be sent and summed in bfloat16 or wider, within the bound.
A program may use at most 64 MiB of HBM per device.

```python
import math
import jax
import jax.numpy as jnp
import numpy as np
from jax import lax

D = 512
HEADS = 16
HEAD = 32
LEVELS = 4
PATCH = 4
WIN_LEV = 2
WIN_LAT = 6
WIN_LON = 12
FIELDS = 64
NROWS = 384
NLON = 96


def draw_perc_wk(key, part):
    key = jax.random.fold_in(key, 11)
    entries = jax.random.normal(jax.random.fold_in(key, 3), (D, D), jnp.float32)
    return jnp.clip(entries * (6.0 / math.sqrt(D)), -10.0, 10.0).astype(jnp.bfloat16)


def draw_swin_qkv(key, part):
    key = jax.random.fold_in(key, 23)
    base_scale = 1.5 / math.sqrt(D)
    query_part = jax.random.normal(jax.random.fold_in(key, 1), (D, HEADS, HEAD), jnp.float32) * base_scale
    key_free = jax.random.normal(jax.random.fold_in(key, 2), (D, HEADS, HEAD), jnp.float32) * base_scale
    value_part = jax.random.normal(jax.random.fold_in(key, 3), (D, D), jnp.float32) / math.sqrt(D)
    key_part = key_free
    merged = jnp.concatenate([query_part.reshape(D, D), key_part.reshape(D, D), value_part], axis=1)
    return jnp.clip(merged, -12.0, 12.0).astype(jnp.bfloat16)


def draw_lon_shift(key, part):
    key = jax.random.fold_in(key, 37)
    shuffled = jax.random.permutation(key, WIN_LON - 1).astype(jnp.int32) + 1
    taken = shuffled[:LEVELS // WIN_LEV]
    lifted = taken + (WIN_LON - 1 - jnp.max(taken))
    return lifted.astype(jnp.int32)


def levels(key, extent, cuts, smallest, high):
    def one(position, blocks):
        heights = jax.random.uniform(jax.random.fold_in(jax.random.fold_in(key, 6), position), (blocks,), jnp.float32, smallest / len(cuts), high / len(cuts))
        return jnp.repeat(jnp.exp(heights), extent[position] // blocks).reshape((-1,) + (1,) * (len(extent) - position - 1))

    factor_of = one(*cuts[0])
    for cut in cuts[1:]:
        factor_of = factor_of * one(*cut)
    return factor_of


def length_profile(number_of, total, most, slope):
    portions = [(1 << 20) // math.isqrt(grade ** slope) + 1 for grade in range(2, number_of + 1)]
    surplus, holding = total - most - (number_of - 1), [1] * (number_of - 1)
    while surplus > 0:
        free = [i for i in range(number_of - 1) if holding[i] < most]
        mass, budget = sum([portions[i] for i in free]), surplus
        for i in free:
            extra = min(most - holding[i], max(1, budget * portions[i] // mass), surplus)
            holding[i] = holding[i] + extra
            surplus = surplus - extra
    return np.array([most] + holding)


def uneven(key, number_of, total, reach, slope):
    if number_of == 2:
        one = jax.random.randint(key, (), max(1, total - reach), min(reach, total - 1) + 1)
        return jnp.stack([one, total - one])
    sizes = jnp.asarray(length_profile(number_of, total, reach, slope), jnp.int32)
    pairs = (number_of - 1) // 2
    giver, taker = sizes[1:1 + 2 * pairs:2], sizes[2:2 + 2 * pairs:2]
    slack = jnp.minimum(giver - 1, reach - taker)
    passed = jax.random.randint(jax.random.fold_in(key, 1), (pairs,), 0, 1 << 20) % (slack + 1)
    sizes = sizes.at[1:1 + 2 * pairs:2].set(giver - passed).at[2:2 + 2 * pairs:2].set(taker + passed)
    return sizes[jax.random.permutation(jax.random.fold_in(key, 2), number_of)]


def bell_draw(rng, dims, width, most, cuts=(), kind=jnp.bfloat16):
    array = jax.random.normal(rng, dims, jnp.float32) * width
    if len(cuts) > 0:
        array = levels(rng, dims, cuts, -0.22, 0.18) * array
    return jnp.clip(array, min=-most, max=most).astype(kind)


def setup_inputs(seed: int = 0) -> dict:
    streams_of = jax.random.split(jax.random.key(seed), 11)
    return {
        "fields": bell_draw(streams_of[0], (FIELDS, NROWS * PATCH, NLON * PATCH), 1.0, 6.0, ((0, 8), (1, 64))),
        "field_ids": jax.random.permutation(streams_of[1], FIELDS).astype(jnp.int32),
        "embed_w": bell_draw(streams_of[2], (FIELDS, PATCH * PATCH, D), (PATCH * PATCH) ** -0.5, 1.5),
        "lat_query": bell_draw(streams_of[3], (LEVELS, D), 0.5, 3.0),
        "perc_wk": draw_perc_wk(jax.random.fold_in(streams_of[10], 71), 0),
        "perc_wv": bell_draw(streams_of[5], (D, D), D ** -0.5, 0.25),
        "swin_qkv": draw_swin_qkv(jax.random.fold_in(streams_of[10], 71), 0),
        "swin_wo": bell_draw(streams_of[7], (D, D), D ** -0.5, 0.25),
        "row_window": jnp.searchsorted(jnp.cumsum(uneven(streams_of[8], NROWS // 3, NROWS, WIN_LAT, 0)), jnp.arange(NROWS), side="right").astype(jnp.int32),
        "lon_shift": draw_lon_shift(jax.random.fold_in(streams_of[10], 71), 0),
    }


EPSILON = 1e-05
MASKED = -1e+30

def layer_norm(values):
    row_mean = lax.optimization_barrier(jnp.mean(values, axis=-1, keepdims=True))
    centred = values - row_mean
    variance = lax.optimization_barrier(jnp.mean(centred * centred, axis=-1, keepdims=True))
    return centred * lax.rsqrt(variance + EPSILON)

def softmax_last(scores):
    row_top = lax.optimization_barrier(jnp.max(scores, axis=-1, keepdims=True))
    lifted = jnp.exp(scores - row_top)
    return lifted / lax.optimization_barrier(jnp.sum(lifted, axis=-1, keepdims=True))

def absorb(perc_wk, lat_query):
    weight_heads = perc_wk.astype(jnp.float32).reshape(D, HEADS, HEAD)
    query_heads = lat_query.astype(jnp.float32).reshape(LEVELS, HEADS, HEAD)
    merged = jnp.einsum('ehj,lhj->lhe', weight_heads, query_heads)
    return merged.astype(jnp.bfloat16).reshape(LEVELS * HEADS, D)

def perceive_row(pixels, chosen, query_keys, lat_query, perc_wv):
    field_count = pixels.shape[0]
    col_count = pixels.shape[2] // PATCH
    blocks = pixels.reshape(field_count, PATCH, col_count, PATCH).astype(jnp.float32)
    tokens = jnp.einsum('ficj,fijd->fcd', blocks, chosen.astype(jnp.float32)).astype(jnp.bfloat16)
    normed = layer_norm(tokens.astype(jnp.float32)).astype(jnp.bfloat16)
    scores = jnp.einsum('fcd,kd->ckf', normed.astype(jnp.float32), query_keys.astype(jnp.float32)) / math.sqrt(HEAD)
    weights = softmax_last(scores).astype(jnp.bfloat16)
    pooled = jnp.einsum('ckf,fcd->ckd', weights.astype(jnp.float32), normed.astype(jnp.float32)).astype(jnp.bfloat16)
    pooled = pooled.reshape(col_count, LEVELS, HEADS, D)
    value_heads = perc_wv.astype(jnp.float32).reshape(D, HEADS, HEAD)
    projected = jnp.einsum('clhe,ehj->clhj', pooled.astype(jnp.float32), value_heads)
    latent = projected.reshape(col_count, LEVELS, D) + lat_query.astype(jnp.float32)[None]
    return jnp.transpose(latent.astype(jnp.bfloat16), (1, 0, 2))

def attend(query_part, key_part, value_part, query_ids, key_ids, col_valid):
    lev_count, query_span, col_count, feat_count = query_part.shape
    key_span = key_part.shape[1]
    windows = col_count // WIN_LON

    def to_windows(tensor):
        span = tensor.shape[1]
        shaped = tensor.reshape(lev_count, span, windows, WIN_LON, HEADS, HEAD)
        return jnp.transpose(shaped, (2, 4, 0, 1, 3, 5)).reshape(windows, HEADS, lev_count * span * WIN_LON, HEAD)
    query_win = to_windows(query_part).astype(jnp.float32)
    key_win = to_windows(key_part).astype(jnp.float32)
    value_win = to_windows(value_part).astype(jnp.float32)
    scores = jnp.einsum('whqd,whkd->whqk', query_win, key_win) / math.sqrt(HEAD)
    same_window = query_ids[:, None] == key_ids[None, :]
    row_mask = jnp.broadcast_to(same_window[None, :, None, None, :, None], (lev_count, query_span, WIN_LON, lev_count, key_span, WIN_LON))
    row_mask = row_mask.reshape(lev_count * query_span * WIN_LON, lev_count * key_span * WIN_LON)
    col_mask = jnp.broadcast_to(col_valid[:, None, None, :], (windows, lev_count, key_span, WIN_LON)).reshape(windows, lev_count * key_span * WIN_LON)
    full_mask = row_mask[None] & col_mask[:, None, :]
    scores = jnp.where(full_mask[:, None], scores, MASKED)
    weights = softmax_last(scores).astype(jnp.bfloat16)
    mixed_heads = jnp.einsum('whqk,whkd->whqd', weights.astype(jnp.float32), value_win).astype(jnp.bfloat16)
    restored = mixed_heads.reshape(windows, HEADS, lev_count, query_span, WIN_LON, HEAD)
    return jnp.transpose(restored, (2, 3, 0, 4, 1, 5)).reshape(lev_count, query_span, col_count, feat_count)

def reference(fields, field_ids, embed_w, lat_query, perc_wk, perc_wv, swin_qkv, swin_wo, row_window, lon_shift):
    field_count = fields.shape[0]
    chosen = jnp.take(embed_w, field_ids, axis=0).reshape(field_count, PATCH, PATCH, D)
    query_keys = absorb(perc_wk, lat_query)
    row_major = jnp.moveaxis(fields.reshape(field_count, NROWS, PATCH, NLON * PATCH), 1, 0)
    per_row = lax.map(lambda one_row: perceive_row(one_row, chosen, query_keys, lat_query, perc_wv), row_major)
    latents = jnp.transpose(per_row, (1, 0, 2, 3))
    halo_rows = WIN_LAT - 1
    key_span = 3 * WIN_LAT - 2
    slab_width = NLON + WIN_LON
    padded = jnp.pad(latents, ((0, 0), (halo_rows, halo_rows), (0, 0), (0, 0)))
    padded_ids = jnp.pad(row_window, (halo_rows, halo_rows), constant_values=-1)

    def widen(tensor):
        return jnp.pad(tensor, ((0, 0), (0, 0), (WIN_LON, WIN_LON), (0, 0)))

    def one_block(block_index):
        row_start = block_index * WIN_LAT
        slab = lax.dynamic_slice_in_dim(padded, row_start, key_span, axis=1)
        slab_normed = layer_norm(slab.astype(jnp.float32)).astype(jnp.bfloat16)
        projected = jnp.einsum('lrcd,de->lrce', slab_normed.astype(jnp.float32), swin_qkv.astype(jnp.float32))
        queries = projected[:, halo_rows:halo_rows + WIN_LAT, :, :D].astype(jnp.bfloat16)
        keys = projected[..., D:2 * D].astype(jnp.bfloat16)
        values = projected[..., 2 * D:].astype(jnp.bfloat16)
        query_ids = lax.dynamic_slice_in_dim(row_window, row_start, WIN_LAT)
        key_ids = lax.dynamic_slice_in_dim(padded_ids, row_start, key_span)
        pieces = []
        for pair_index in range(LEVELS // WIN_LEV):
            offset = lon_shift[pair_index]
            lev_lo = pair_index * WIN_LEV
            slab_q = lax.dynamic_slice_in_dim(widen(queries[lev_lo:lev_lo + WIN_LEV]), offset, slab_width, axis=2)
            slab_k = lax.dynamic_slice_in_dim(widen(keys[lev_lo:lev_lo + WIN_LEV]), offset, slab_width, axis=2)
            slab_v = lax.dynamic_slice_in_dim(widen(values[lev_lo:lev_lo + WIN_LEV]), offset, slab_width, axis=2)
            global_cols = jnp.arange(slab_width, dtype=jnp.int32) + offset - WIN_LON
            col_valid = ((global_cols >= 0) & (global_cols < NLON)).reshape(slab_width // WIN_LON, WIN_LON)
            mixed = attend(slab_q, slab_k, slab_v, query_ids, key_ids, col_valid)
            pieces.append(lax.dynamic_slice_in_dim(mixed, WIN_LON - offset, NLON, axis=2))
        mixed_all = jnp.concatenate(pieces, axis=0)
        update = jnp.einsum('lrcd,de->lrce', mixed_all.astype(jnp.float32), swin_wo.astype(jnp.float32))
        own_rows = lax.dynamic_slice_in_dim(latents, row_start, WIN_LAT, axis=1)
        return (own_rows.astype(jnp.float32) + update).astype(jnp.bfloat16)
    blocks_out = lax.map(one_block, jnp.arange(NROWS // WIN_LAT, dtype=jnp.int32))
    return jnp.transpose(blocks_out, (1, 0, 2, 3, 4)).reshape(LEVELS, NROWS, NLON, D)
```

```python
import math

import jax
import jax.numpy as jnp
from jax import lax
from jax.experimental import pallas as pl
from jax.experimental.pallas import tpu as pltpu
from jax.sharding import PartitionSpec as P

D = 512
HEADS = 16
HEAD = 32
LEVELS = 4
PATCH = 4
WIN_LAT = 6
WIN_LON = 12
FIELDS = 64
ROWS = 6
COLS = 12
PIX = PATCH * PATCH
GROUP = 4
QUADS = COLS // GROUP
LINE = 2 * COLS
OWN = ROWS * LINE
HALO = 128
KEYS = 384
EDGE = 120

EPSILON = 1e-05
MASKED = -1e30
EXP2_SCALE = math.log2(math.e) / math.sqrt(HEAD)
F32 = jnp.float32
BF16 = jnp.bfloat16
NT = (((1,), (1,)), ((), ()))


def dot(a, b):
    return jnp.dot(a, b, preferred_element_type=F32)


def iota(shape, dim):
    return lax.broadcasted_iota(jnp.int32, shape, dim)


def layer_norm(values):
    row_mean = jnp.sum(values, axis=-1, keepdims=True) * (1.0 / D)
    centred = values - row_mean
    variance = jnp.sum(centred * centred, axis=-1, keepdims=True) * (1.0 / D)
    return centred * lax.rsqrt(variance + EPSILON)


def softmax_rows(scores):
    row_top = jnp.max(scores, axis=-1, keepdims=True)
    lifted = jnp.exp2(scores - row_top)
    return lifted * (1.0 / jnp.sum(lifted, axis=-1, keepdims=True))


def encode_kernel(
    ids_ref, shift_ref, pix_ref, embed_ref, query_ref, wk_ref, wv_ref, out_ref,
    slot_w, keys_scr, bias_scr, normed_scr, pooled_scr, query_scr,
):
    step = pl.program_id(0)

    @pl.when(step == 0)
    def _():
        def place(slot, carry):
            start = pl.multiple_of(slot * PIX, PIX)
            slot_w[pl.ds(start, PIX), :] = embed_ref[ids_ref[slot]]
            return carry

        lax.fori_loop(0, FIELDS, place, 0)
        swap = shift_ref[1] > shift_ref[0]
        query = query_ref[...].astype(F32)
        swapped = jnp.concatenate([query[2:], query[:2]], axis=0)
        query = jnp.where(swap, swapped, query)
        row = iota((256, D), 0)
        level = (row // GROUP) % LEVELS
        spread = jnp.zeros((256, D), F32)
        for lev in range(LEVELS):
            spread = jnp.where(level == lev, query[lev : lev + 1, :], spread)
        query_scr[...] = spread[:16]
        own_head = iota((256, D), 1) // HEAD == row // 16
        masked = jnp.where(own_head, spread, 0.0).astype(BF16)
        keys_scr[...] = lax.dot_general(
            masked, wk_ref[...], NT, preferred_element_type=F32
        ).astype(BF16)
        same = iota((256, 256), 1) // FIELDS == iota((256, 256), 0) % GROUP
        bias_scr[...] = jnp.where(same, 0.0, MASKED)

    own_slot = iota((1, 16, 256), 2) // PIX == iota((1, 16, 256), 1)
    for part in range(4):
        pixels = jnp.concatenate(
            [pix_ref[2 * part, 0], pix_ref[2 * part + 1, 0]], axis=-1
        ).astype(F32)
        spread = jnp.where(own_slot, pixels[:, None, :], 0.0).astype(BF16)
        tokens = dot(spread.reshape(COLS * 16, 256), slot_w[256 * part : 256 * part + 256, :])
        normed = layer_norm(tokens.astype(BF16).astype(F32)).astype(BF16)
        normed_scr[:, 16 * part : 16 * part + 16, :] = normed.reshape(COLS, 16, D)
    for quad in range(QUADS):
        normed = normed_scr[GROUP * quad : GROUP * quad + GROUP].reshape(GROUP * FIELDS, D)
        scores = lax.dot_general(keys_scr[...], normed, NT, preferred_element_type=F32)
        weights = softmax_rows(scores * EXP2_SCALE + bias_scr[...]).astype(BF16)
        pooled = dot(weights, normed).astype(BF16)
        start = pl.multiple_of(step * 48 + quad * 16, 16)
        pooled_scr[:, pl.ds(start, 16), :] = pooled.reshape(HEADS, 16, D)

    @pl.when(step == ROWS - 1)
    def _():
        halves = []
        for half in range(2):
            lane_head = iota((D, 256), 1) // HEAD
            value_w = wv_ref[:, 256 * half : 256 * half + 256].astype(F32)
            total = jnp.zeros((2 * OWN, 256), F32)
            for head in range(8):
                masked = jnp.where(lane_head == head, value_w, 0.0).astype(BF16)
                total = total + dot(pooled_scr[8 * half + head], masked)
            halves.append(total)
        projected = jnp.concatenate(halves, axis=-1).reshape(ROWS * QUADS, 16, D)
        latents = projected + query_scr[...][None]
        for pair in range(2):
            out_ref[pair] = latents[:, 8 * pair : 8 * pair + 8].reshape(OWN, D).astype(BF16)


def encode(ids, shift, pixels, embed_w, lat_query, wk, wv):
    vmem = pl.BlockSpec(memory_space=pltpu.VMEM)
    smem = pl.BlockSpec(memory_space=pltpu.SMEM)
    return pl.pallas_call(
        encode_kernel,
        out_shape=jax.ShapeDtypeStruct((2, OWN, D), BF16),
        grid=(ROWS,),
        in_specs=[
            smem, smem,
            pl.BlockSpec((8, 1, COLS, 128), lambda r: (0, r, 0, 0)),
            vmem, vmem, vmem, vmem,
        ],
        out_specs=vmem,
        scratch_shapes=[
            pltpu.VMEM((FIELDS * PIX, D), BF16),
            pltpu.VMEM((256, D), BF16),
            pltpu.VMEM((256, 256), F32),
            pltpu.VMEM((COLS, FIELDS, D), BF16),
            pltpu.VMEM((HEADS, 2 * OWN, D), BF16),
            pltpu.VMEM((16, D), F32),
        ],
        compiler_params=pltpu.CompilerParams(vmem_limit_bytes=48 << 20),
        name="encode",
    )(ids, shift, pixels, embed_w, lat_query, wk, wv)


def column_of(token):
    return (token % LINE) // 8 * GROUP + token % GROUP


def attend_kernel(window_ref, shift_ref, own_ref, up_ref, down_ref, qkv_ref, wo_ref, out_ref):
    sector = lax.axis_index("var")
    sectors = lax.axis_size("var")
    first = lax.axis_index("lat") * ROWS - (WIN_LAT - 1)
    total_rows = window_ref.shape[0]
    shift = jnp.minimum(shift_ref[0], shift_ref[1])
    key_token = iota((1, KEYS), 1)
    query_token = iota((OWN, 1), 0)
    key_row = jnp.full((1, KEYS), -1, jnp.int32)
    query_row = jnp.full((OWN, 1), -1, jnp.int32)
    for k in range(ROWS + 2 * (WIN_LAT - 1)):
        row = first + k
        inside = (row >= 0) & (row < total_rows)
        ident = jnp.where(inside, window_ref[jnp.clip(row, 0, total_rows - 1)], -1)
        key_row = jnp.where(key_token // LINE == k, ident, key_row)
        if 0 <= k - (WIN_LAT - 1) < ROWS:
            query_row = jnp.where(query_token // LINE == k - (WIN_LAT - 1), ident, query_row)

    for pair in range(2):
        def wrapped(token):
            column = column_of(token)
            if pair == 0:
                return jnp.where((column == COLS - 1) & (sector == 0), 1, 0)
            return jnp.where((column < shift) & (sector == sectors - 1), 1, 0)

        same = (query_row * 2 + wrapped(query_token)) == (key_row * 2 + wrapped(key_token))
        bias = jnp.where(same, 0.0, MASKED)
        own = own_ref[pair].astype(F32)
        up = up_ref[pair].astype(F32)[HALO - EDGE :]
        down = down_ref[pair].astype(F32)[:EDGE]
        normed = layer_norm(jnp.concatenate([up, own, down], axis=0))
        queries = dot(normed[EDGE : EDGE + OWN].astype(BF16), qkv_ref[:, :D])
        normed = normed.astype(BF16)
        keys = dot(normed, qkv_ref[:, D : 2 * D]).astype(BF16)
        values = dot(normed, qkv_ref[:, 2 * D :]).astype(BF16)
        halves = []
        lane_head = iota((OWN, 256), 1) // HEAD
        for half in range(2):
            cut = slice(256 * half, 256 * half + 256)
            part = queries[:, cut]
            stacked = jnp.concatenate(
                [jnp.where(lane_head == h, part, 0.0).astype(BF16) for h in range(8)], axis=0
            )
            scores = lax.dot_general(stacked, keys[:, cut], NT, preferred_element_type=F32)
            scores = scores.reshape(8, OWN, KEYS) * EXP2_SCALE + bias[None]
            weights = softmax_rows(scores).astype(BF16).reshape(8 * OWN, KEYS)
            mixed = dot(weights, values[:, cut]).reshape(8, OWN, 256)
            total = jnp.zeros((OWN, 256), F32)
            for h in range(8):
                total = jnp.where(lane_head == h, mixed[h], total)
            halves.append(total.astype(BF16))
        update = dot(jnp.concatenate(halves, axis=-1), wo_ref[...])
        out_ref[pair] = (own + update).astype(BF16)


def attend(window, shift, own, up, down, qkv, wo):
    vmem = pl.BlockSpec(memory_space=pltpu.VMEM)
    smem = pl.BlockSpec(memory_space=pltpu.SMEM)
    return pl.pallas_call(
        attend_kernel,
        out_shape=jax.ShapeDtypeStruct((2, OWN, D), BF16),
        in_specs=[smem, smem] + [vmem] * 5,
        out_specs=vmem,
        compiler_params=pltpu.CompilerParams(vmem_limit_bytes=48 << 20),
        name="attend",
    )(window, shift, own, up, down, qkv, wo)


def shards(
    fields, field_ids, embed_w, lat_query, perc_wk, perc_wv, swin_qkv, swin_wo, row_window, lon_shift
):
    sectors = lax.axis_size("var")
    bands = lax.axis_size("lat")
    blocks = fields.reshape(8, ROWS, PATCH, sectors, COLS, PATCH)
    blocks = jnp.transpose(blocks, (3, 1, 4, 0, 2, 5)).reshape(sectors, ROWS, COLS, 128)
    pixels = lax.all_to_all(blocks, "var", split_axis=0, concat_axis=0, tiled=True)
    latents = encode(field_ids, lon_shift, pixels, embed_w, lat_query, perc_wk, perc_wv)

    shift = jnp.minimum(lon_shift[0], lon_shift[1])
    split = latents.reshape(2, ROWS, QUADS, 2, GROUP, D)
    rightward = [(i, (i + 1) % sectors) for i in range(sectors)]
    leftward = [((i + 1) % sectors, i) for i in range(sectors)]
    from_left = lax.ppermute(split[0, :, 2:], "var", rightward)
    from_right = lax.ppermute(split[1], "var", leftward)
    column = (
        lax.broadcasted_iota(jnp.int32, (1, QUADS, 1, GROUP, 1), 1) * GROUP
        + lax.broadcasted_iota(jnp.int32, (1, QUADS, 1, GROUP, 1), 3)
    )
    from_left = jnp.broadcast_to(from_left, split[0].shape)
    slab = jnp.stack(
        [
            jnp.where(column == COLS - 1, from_left, split[0]),
            jnp.where(column < shift, from_right, split[1]),
        ]
    ).reshape(2, OWN, D)

    downward = [(i, i + 1) for i in range(bands - 1)]
    upward = [(i + 1, i) for i in range(bands - 1)]
    up = lax.ppermute(slab[:, OWN - HALO :], "lat", downward)
    down = lax.ppermute(slab[:, :HALO], "lat", upward)
    encoded = attend(row_window, lon_shift, slab, up, down, swin_qkv, swin_wo)

    split = encoded.reshape(2, ROWS, QUADS, 2, GROUP, D)
    back_left = lax.ppermute(split[0, :, 2:], "var", leftward)
    back_right = lax.ppermute(split[1], "var", rightward)
    back_left = jnp.broadcast_to(back_left, split[0].shape)
    pairs = jnp.stack(
        [
            jnp.where(column == COLS - 1, back_left, split[0]),
            jnp.where(column < shift, back_right, split[1]),
        ]
    )
    pairs = jnp.where(lon_shift[1] > lon_shift[0], pairs[::-1], pairs)
    return jnp.transpose(pairs, (0, 3, 1, 2, 4, 5)).reshape(LEVELS, ROWS, COLS, D)


def solution(mesh):
    in_specs = (P("var", "lat", None), P(), P(), P(), P(), P(), P(), P(), P(), P())
    out_specs = P(None, "lat", "var", None)
    return jax.shard_map(shards, mesh=mesh, in_specs=in_specs, out_specs=out_specs, check_vma=False)
```

```python
import math

import jax
import jax.numpy as jnp
from jax import lax
from jax.experimental import pallas as pl
from jax.experimental.pallas import tpu as pltpu
from jax.sharding import PartitionSpec as P

D = 512
HEADS = 16
HEAD = 32
LEVELS = 4
PATCH = 4
WIN_LAT = 6
WIN_LON = 12
FIELDS = 64
ROWS = 6
COLS = 12
PIX = PATCH * PATCH
GROUP = 4
QUADS = COLS // GROUP
LINE = 2 * COLS
OWN = ROWS * LINE
HALO = 128
KEYS = 384
EDGE = 120

EPSILON = 1e-05
MASKED = -1e30
EXP2_SCALE = math.log2(math.e) / math.sqrt(HEAD)
F32 = jnp.float32
BF16 = jnp.bfloat16
NT = (((1,), (1,)), ((), ()))
MESH = pl.DeviceIdType.MESH
PIECES = ((0, 16), (16, 32), (48, 32))
SEND_ORDER = (4, 3, 5, 2, 6, 1, 7)
QUERY_PARTS = (((0, OWN),), ((0, 96), (96, OWN)))


def dot(a, b):
    return jnp.dot(a, b, preferred_element_type=F32)


def iota(shape, dim):
    return lax.broadcasted_iota(jnp.int32, shape, dim)


def layer_norm(values):
    row_mean = jnp.sum(values, axis=-1, keepdims=True) * (1.0 / D)
    centred = values - row_mean
    variance = jnp.sum(centred * centred, axis=-1, keepdims=True) * (1.0 / D)
    return centred * lax.rsqrt(variance + EPSILON)


def softmax_rows(scores):
    row_top = jnp.max(scores, axis=-1, keepdims=True)
    lifted = jnp.exp2(scores - row_top)
    return lifted * (1.0 / jnp.sum(lifted, axis=-1, keepdims=True))


def column_of(token):
    return (token % LINE) // 8 * GROUP + token % GROUP


def remote(src, dst, send_sem, recv_sem, **device):
    return pltpu.make_async_remote_copy(
        src_ref=src, dst_ref=dst, send_sem=send_sem, recv_sem=recv_sem,
        device_id=device, device_id_type=MESH,
    )


def attention(queries, keys, values, bias):
    count = queries.shape[0]
    lane_head = iota((count, 256), 1) // HEAD
    halves = []
    for half in range(2):
        cut = slice(256 * half, 256 * half + 256)
        part = queries[:, cut]
        stacked = jnp.concatenate(
            [jnp.where(lane_head == h, part, 0.0).astype(BF16) for h in range(8)], axis=0
        )
        scores = lax.dot_general(stacked, keys[:, cut], NT, preferred_element_type=F32)
        scores = scores.reshape(8, count, KEYS) * EXP2_SCALE + bias[None]
        weights = softmax_rows(scores).astype(BF16).reshape(8 * count, KEYS)
        mixed = dot(weights, values[:, cut]).reshape(8, count, 256)
        total = jnp.zeros((count, 256), F32)
        for h in range(8):
            total = jnp.where(lane_head == h, mixed[h], total)
        halves.append(total.astype(BF16))
    return jnp.concatenate(halves, axis=-1)


def pick_pixels(fields, stage, send):
    flat = fields.astype(F32).reshape(8 * ROWS * PATCH, 384).astype(BF16)
    row = iota((512, 1), 0)
    column = row % 16
    source = jnp.where(column < COLS, (row % 128) // 16 * 48 + column * PATCH + row // 128, -1)
    pick = jnp.where(source == iota((512, 384), 1), 1.0, 0.0).astype(BF16)
    turned = lax.dot_general(pick, flat, NT, preferred_element_type=F32).astype(BF16)
    row = iota((192, 1), 0)
    target = (row // PATCH) % ROWS * 128 + row // (ROWS * PATCH) * PIX + row % PATCH * PATCH
    lane = iota((192, 768), 1)
    total = jnp.zeros((128, 768), F32)
    for j in range(PATCH):
        place = jnp.where(target + j == lane, 1.0, 0.0).astype(BF16)
        total = total + dot(turned[128 * j : 128 * j + 128], place)
    for sector in range(8):
        stage[sector, 72:80, :] = jnp.zeros((8, 128), F32)
        for line in range(ROWS):
            stage[sector, COLS * line : COLS * line + COLS, :] = total[
                16 * sector : 16 * sector + COLS, 128 * line : 128 * line + 128
            ]
    send[...] = stage[...].astype(BF16)


def prepare_weights(ids_ref, shift_ref, embed, query_ref, wk, slot_w, keys_scr, bias_scr, query_scr):
    def place(slot, carry):
        start = pl.multiple_of(slot * PIX, PIX)
        slot_w[pl.ds(start, PIX), :] = embed[ids_ref[slot]]
        return carry

    lax.fori_loop(0, FIELDS, place, 0)
    swap = shift_ref[1] > shift_ref[0]
    query = query_ref[...].astype(F32)
    swapped = jnp.concatenate([query[2:], query[:2]], axis=0)
    query = jnp.where(swap, swapped, query)
    level = (iota((256, D), 0) // GROUP) % LEVELS
    spread = jnp.zeros((256, D), F32)
    for lev in range(LEVELS):
        spread = jnp.where(level == lev, query[lev : lev + 1, :], spread)
    query_scr[...] = spread[:16]
    own_head = iota((256, D), 1) // HEAD == iota((256, D), 0) // 16
    masked = jnp.where(own_head, spread, 0.0).astype(BF16)
    keys_scr[...] = lax.dot_general(
        masked, wk[...], NT, preferred_element_type=F32
    ).astype(BF16)
    same = iota((256, 256), 1) // FIELDS == iota((256, 256), 0) % GROUP
    bias_scr[...] = jnp.where(same, 0.0, MASKED)


def merge_line(line, line_pixels, slot_w, keys_scr, bias_scr, normed_scr, pooled_scr):
    own_slot = iota((1, 16, 256), 2) // PIX == iota((1, 16, 256), 1)
    for part in range(4):
        pixels = line_pixels[line, :, 256 * part : 256 * part + 256][:COLS]
        spread = jnp.where(own_slot, pixels[:, None, :], 0.0).astype(BF16)
        tokens = dot(spread.reshape(COLS * 16, 256), slot_w[256 * part : 256 * part + 256, :])
        normed = layer_norm(tokens.astype(BF16).astype(F32)).astype(BF16)
        normed_scr[:, 16 * part : 16 * part + 16, :] = normed.reshape(COLS, 16, D)
    for quad in range(QUADS):
        normed = normed_scr[GROUP * quad : GROUP * quad + GROUP].reshape(GROUP * FIELDS, D)
        scores = lax.dot_general(keys_scr[...], normed, NT, preferred_element_type=F32)
        weights = softmax_rows(scores * EXP2_SCALE + bias_scr[...]).astype(BF16)
        pooled = dot(weights, normed).astype(BF16)
        start = pl.multiple_of(line * 48 + quad * 16, 16)
        pooled_scr[:, pl.ds(start, 16), :] = pooled.reshape(HEADS, 16, D)


def project(pooled_scr, wv, query_scr):
    halves = []
    for half in range(2):
        lane_head = iota((D, 256), 1) // HEAD
        value_w = wv[:, 256 * half : 256 * half + 256].astype(F32)
        total = jnp.zeros((2 * OWN, 256), F32)
        for head in range(8):
            masked = jnp.where(lane_head == head, value_w, 0.0).astype(BF16)
            total = total + dot(pooled_scr[8 * half + head], masked)
        halves.append(total)
    projected = jnp.concatenate(halves, axis=-1).reshape(ROWS * QUADS, 16, D)
    return projected + query_scr[...][None]


def last_quads(tokens):
    tokens = tokens.reshape(ROWS * QUADS, 8, D)
    return jnp.concatenate([tokens[QUADS * r + 2] for r in range(ROWS)], axis=0)


def with_last_column(tokens, quads):
    tokens = tokens.reshape(ROWS * QUADS, 8, D)
    is_last = iota((8, D), 0) % GROUP == GROUP - 1
    pieces = []
    for r in range(ROWS):
        own = tokens[QUADS * r + 2]
        pieces += [tokens[QUADS * r], tokens[QUADS * r + 1]]
        pieces += [jnp.where(is_last, quads[8 * r : 8 * r + 8], own)]
    return jnp.concatenate(pieces, axis=0)


def whole_kernel(
    ids_ref, shift_ref, window_ref, fields_ref, query_ref, embed_h, wk_h, wv_h, qkv_h, wo_h, out_ref,
    embed, wk, wv, qkv, wo, slot_w, keys_scr, bias_scr, normed_scr, pooled_scr, query_scr,
    stage, send, recv, line_pixels, latents, slab, edge_send, edge_recv, col_recv, up_recv, down_recv,
    encoded, back_edge_send, back_edge_recv, back_recv,
    load_sem, pix_send_sem, pix_recv_sem, col_send_sem, col_recv_sem, row_send_sem, row_recv_sem,
    back_send_sem, back_recv_sem,
):
    sector = lax.axis_index("var")
    sectors = lax.axis_size("var")
    band = lax.axis_index("lat")
    bands = lax.axis_size("lat")
    right = lax.rem(sector + 1, sectors)
    left = lax.rem(sector + sectors - 1, sectors)
    has_up = band > 0
    has_down = band < bands - 1

    barrier = pltpu.get_barrier_semaphore()
    for k in range(1, sectors):
        pl.semaphore_signal(
            barrier, inc=1, device_id={"var": lax.rem(sector + k, sectors)}, device_id_type=MESH
        )

    @pl.when(has_up)
    def _():
        pl.semaphore_signal(barrier, inc=1, device_id={"lat": band - 1}, device_id_type=MESH)

    @pl.when(has_down)
    def _():
        pl.semaphore_signal(barrier, inc=1, device_id={"lat": band + 1}, device_id_type=MESH)

    loads = [
        pltpu.make_async_copy(src, dst, load_sem.at[i])
        for i, (src, dst) in enumerate(
            [(embed_h, embed), (wk_h, wk), (wv_h, wv), (qkv_h, qkv), (wo_h, wo)]
        )
    ]
    for load in loads:
        load.start()

    pick_pixels(fields_ref[...], stage, send)

    @pl.when(jnp.logical_not(has_up))
    def _():
        up_recv[...] = jnp.zeros_like(up_recv)

    @pl.when(jnp.logical_not(has_down))
    def _():
        down_recv[...] = jnp.zeros_like(down_recv)

    neighbours = jnp.where(has_up, 1, 0) + jnp.where(has_down, 1, 0)
    pl.semaphore_wait(barrier, sectors - 1 + neighbours)

    def pixel_copy(piece, k, peer, slot):
        start, count = PIECES[piece]
        return remote(
            send.at[peer, pl.ds(start, count)], recv.at[slot, pl.ds(start, count)],
            pix_send_sem.at[piece, k], pix_recv_sem.at[piece, k], var=peer,
        )

    for piece in range(len(PIECES)):
        for k in SEND_ORDER:
            pixel_copy(piece, k, lax.rem(sector + k, sectors), sector).start()
    recv[sector] = send[sector]

    loads[0].wait()
    loads[1].wait()
    prepare_weights(
        ids_ref, shift_ref, embed, query_ref, wk, slot_w, keys_scr, bias_scr, query_scr
    )

    def take_piece(piece, lines):
        for k in range(1, sectors):
            source = lax.rem(sector + sectors - k, sectors)
            pixel_copy(piece, k, source, source).wait_recv()
        start, count = PIECES[piece]
        stage[:, start : start + count, :] = recv[:, start : start + count, :].astype(F32)
        for line in lines:
            for source in range(sectors):
                line_pixels[line, 0:COLS, 128 * source : 128 * source + 128] = stage[
                    source, COLS * line : COLS * line + COLS, :
                ]

    def one_line(line, carry):
        @pl.when(line == 0)
        def _():
            take_piece(0, (0,))

        @pl.when(line == 1)
        def _():
            take_piece(1, (1, 2, 3))

        @pl.when(line == 4)
        def _():
            take_piece(2, (4, 5))

        merge_line(line, line_pixels, slot_w, keys_scr, bias_scr, normed_scr, pooled_scr)
        return carry

    lax.fori_loop(0, ROWS, one_line, 0)

    loads[2].wait()
    fresh = project(pooled_scr, wv, query_scr)
    for pair in range(2):
        tokens = fresh[:, 8 * pair : 8 * pair + 8].reshape(OWN, D)
        latents[pair] = tokens.astype(BF16)
        if pair == 0:
            edge_send[...] = last_quads(tokens).astype(BF16)

    edge_out = remote(edge_send, edge_recv, col_send_sem.at[0], col_recv_sem.at[0], var=right)
    edge_out.start()
    col_out = remote(latents.at[1], col_recv, col_send_sem.at[1], col_recv_sem.at[1], var=left)
    col_out.start()

    def row_copies(pair):
        upward = remote(
            slab.at[pair, pl.ds(0, HALO)], down_recv.at[pair],
            row_send_sem.at[pair, 0], row_recv_sem.at[pair, 0], lat=band - 1,
        )
        downward = remote(
            slab.at[pair, pl.ds(OWN - HALO, HALO)], up_recv.at[pair],
            row_send_sem.at[pair, 1], row_recv_sem.at[pair, 1], lat=band + 1,
        )
        return upward, downward

    def send_rows(pair):
        upward, downward = row_copies(pair)

        @pl.when(has_up)
        def _():
            upward.start()

        @pl.when(has_down)
        def _():
            downward.start()

    def take_rows(pair):
        upward, downward = row_copies(pair)

        @pl.when(has_down)
        def _():
            upward.wait_recv()

        @pl.when(has_up)
        def _():
            downward.wait_recv()

    shift = jnp.minimum(shift_ref[0], shift_ref[1])
    column = column_of(iota((OWN, D), 0))
    edge_out.wait_recv()
    slab[0] = with_last_column(latents[0].astype(F32), edge_recv[...].astype(F32)).astype(BF16)
    send_rows(0)
    col_out.wait_recv()
    slab[1] = jnp.where(
        column < shift, col_recv[...].astype(F32), latents[1].astype(F32)
    ).astype(BF16)
    send_rows(1)

    first = band * ROWS - (WIN_LAT - 1)
    total_rows = window_ref.shape[0]
    key_token = iota((1, KEYS), 1)
    query_token = iota((OWN, 1), 0)
    key_row = jnp.full((1, KEYS), -1, jnp.int32)
    query_row = jnp.full((OWN, 1), -1, jnp.int32)
    for k in range(ROWS + 2 * (WIN_LAT - 1)):
        row = first + k
        inside = (row >= 0) & (row < total_rows)
        ident = jnp.where(inside, window_ref[jnp.clip(row, 0, total_rows - 1)], -1)
        key_row = jnp.where(key_token // LINE == k, ident, key_row)
        if 0 <= k - (WIN_LAT - 1) < ROWS:
            query_row = jnp.where(query_token // LINE == k - (WIN_LAT - 1), ident, query_row)

    loads[3].wait()
    loads[4].wait()
    for pair in range(2):
        def wrapped(token):
            if pair == 0:
                return jnp.where((column_of(token) == COLS - 1) & (sector == 0), 1, 0)
            return jnp.where((column_of(token) < shift) & (sector == sectors - 1), 1, 0)

        same = (query_row * 2 + wrapped(query_token)) == (key_row * 2 + wrapped(key_token))
        bias = jnp.where(same, 0.0, MASKED)
        own = slab[pair].astype(F32)
        take_rows(pair)
        up = up_recv[pair].astype(F32)[HALO - EDGE :]
        down = down_recv[pair].astype(F32)[:EDGE]
        normed = layer_norm(jnp.concatenate([up, own, down], axis=0))
        queries = dot(normed[EDGE : EDGE + OWN].astype(BF16), qkv[:, :D])
        normed = normed.astype(BF16)
        keys = dot(normed, qkv[:, D : 2 * D]).astype(BF16)
        values = dot(normed, qkv[:, 2 * D :]).astype(BF16)
        for part, (start, stop) in enumerate(QUERY_PARTS[pair]):
            mixed = attention(queries[start:stop], keys, values, bias[start:stop])
            done = own[start:stop] + dot(mixed, wo[...])
            encoded[pair, start:stop] = done.astype(BF16)
            if pair == 0:
                back_edge_send[...] = last_quads(done).astype(BF16)
                back_edge = remote(
                    back_edge_send, back_edge_recv, back_send_sem.at[0], back_recv_sem.at[0], var=left
                )
                back_edge.start()
                backs = [back_edge]
            else:
                back = remote(
                    encoded.at[1, pl.ds(start, stop - start)], back_recv.at[pl.ds(start, stop - start)],
                    back_send_sem.at[1 + part], back_recv_sem.at[1 + part], var=right,
                )
                back.start()
                backs.append(back)

    row = iota((192, OWN), 0)
    place = row // 16 % ROWS * LINE + row % 16 // GROUP * 8 + row // 96 * GROUP + row % GROUP
    place = jnp.where(row % 16 < COLS, place, -1)
    order = jnp.where(place == iota((192, OWN), 1), 1.0, 0.0).astype(BF16)

    def in_place(tokens):
        return dot(order, tokens.astype(BF16)).reshape(2, ROWS, 16, D)[:, :, :COLS]

    backs[0].wait_recv()
    first_pair = in_place(
        with_last_column(encoded[0].astype(F32), back_edge_recv[...].astype(F32))
    )
    backs[1].wait_recv()
    backs[2].wait_recv()
    second_pair = in_place(
        jnp.where(column < shift, back_recv[...].astype(F32), encoded[1].astype(F32))
    )
    swap = shift_ref[1] > shift_ref[0]
    out_ref[0:2] = jnp.where(swap, second_pair, first_pair).astype(BF16)
    out_ref[2:4] = jnp.where(swap, first_pair, second_pair).astype(BF16)

    for piece in range(len(PIECES)):
        for k in range(1, sectors):
            pixel_copy(piece, k, lax.rem(sector + k, sectors), sector).wait_send()
    edge_out.wait_send()
    col_out.wait_send()
    for pair in range(2):
        upward, downward = row_copies(pair)

        @pl.when(has_up)
        def _():
            upward.wait_send()

        @pl.when(has_down)
        def _():
            downward.wait_send()

    for back in backs:
        back.wait_send()


def shards(
    fields, field_ids, embed_w, lat_query, perc_wk, perc_wv, swin_qkv, swin_wo, row_window, lon_shift
):
    vmem = pl.BlockSpec(memory_space=pltpu.VMEM)
    smem = pl.BlockSpec(memory_space=pltpu.SMEM)
    hbm = pl.BlockSpec(memory_space=pl.ANY)
    return pl.pallas_call(
        whole_kernel,
        out_shape=jax.ShapeDtypeStruct((LEVELS, ROWS, COLS, D), BF16),
        in_specs=[smem] * 3 + [vmem] * 2 + [hbm] * 5,
        out_specs=vmem,
        scratch_shapes=[
            pltpu.VMEM((FIELDS, PIX, D), BF16),
            pltpu.VMEM((D, D), BF16),
            pltpu.VMEM((D, D), BF16),
            pltpu.VMEM((D, 3 * D), BF16),
            pltpu.VMEM((D, D), BF16),
            pltpu.VMEM((FIELDS * PIX, D), BF16),
            pltpu.VMEM((256, D), BF16),
            pltpu.VMEM((256, 256), F32),
            pltpu.VMEM((COLS, FIELDS, D), BF16),
            pltpu.VMEM((HEADS, 2 * OWN, D), BF16),
            pltpu.VMEM((16, D), F32),
            pltpu.VMEM((8, 80, 128), F32),
            pltpu.VMEM((8, 80, 128), BF16),
            pltpu.VMEM((8, 80, 128), BF16),
            pltpu.VMEM((ROWS, 16, FIELDS * PIX), F32),
            pltpu.VMEM((2, OWN, D), BF16),
            pltpu.VMEM((2, OWN, D), BF16),
            pltpu.VMEM((48, D), BF16),
            pltpu.VMEM((48, D), BF16),
            pltpu.VMEM((OWN, D), BF16),
            pltpu.VMEM((2, HALO, D), BF16),
            pltpu.VMEM((2, HALO, D), BF16),
            pltpu.VMEM((2, OWN, D), BF16),
            pltpu.VMEM((48, D), BF16),
            pltpu.VMEM((48, D), BF16),
            pltpu.VMEM((OWN, D), BF16),
            pltpu.SemaphoreType.DMA((5,)),
            pltpu.SemaphoreType.DMA((3, 8)),
            pltpu.SemaphoreType.DMA((3, 8)),
            pltpu.SemaphoreType.DMA((2,)),
            pltpu.SemaphoreType.DMA((2,)),
            pltpu.SemaphoreType.DMA((2, 2)),
            pltpu.SemaphoreType.DMA((2, 2)),
            pltpu.SemaphoreType.DMA((3,)),
            pltpu.SemaphoreType.DMA((3,)),
        ],
        compiler_params=pltpu.CompilerParams(
            vmem_limit_bytes=63 << 20, collective_id=0, has_side_effects=True
        ),
        name="whole",
    )(
        field_ids, lon_shift, row_window, fields, lat_query, embed_w, perc_wk, perc_wv, swin_qkv, swin_wo
    )


def solution(mesh):
    in_specs = (P("var", "lat", None), P(), P(), P(), P(), P(), P(), P(), P(), P())
    out_specs = P(None, "lat", "var", None)
    return jax.shard_map(shards, mesh=mesh, in_specs=in_specs, out_specs=out_specs, check_vma=False)
```

```python
import math

import jax
import jax.numpy as jnp
from jax import lax
from jax.experimental import pallas as pl
from jax.experimental.pallas import tpu as pltpu
from jax.sharding import PartitionSpec as P

D = 512
HEADS = 16
HEAD = 32
LEVELS = 4
PATCH = 4
WIN_LAT = 6
WIN_LON = 12
FIELDS = 64
ROWS = 6
COLS = 12
PIX = PATCH * PATCH
GROUP = 4
QUADS = COLS // GROUP
LINE = 2 * COLS
OWN = ROWS * LINE
HALO = 128
KEYS = 384
EDGE = 120

EPSILON = 1e-05
MASKED = -1e30
EXP2_SCALE = math.log2(math.e) / math.sqrt(HEAD)
F32 = jnp.float32
BF16 = jnp.bfloat16
NT = (((1,), (1,)), ((), ()))
MESH = pl.DeviceIdType.MESH
PIECES = ((0, 16), (16, 32), (48, 32))
SEND_ORDER = (4, 3, 5, 2, 6, 1, 7)
QUERY_PARTS = (((0, 96), (96, OWN)), ((0, 96), (96, OWN)))


def dot(a, b):
    return jnp.dot(a, b, preferred_element_type=F32)


def iota(shape, dim):
    return lax.broadcasted_iota(jnp.int32, shape, dim)


def layer_norm(values):
    row_mean = jnp.sum(values, axis=-1, keepdims=True) * (1.0 / D)
    centred = values - row_mean
    variance = jnp.sum(centred * centred, axis=-1, keepdims=True) * (1.0 / D)
    return centred * lax.rsqrt(variance + EPSILON)


def softmax_rows(scores):
    row_top = jnp.max(scores, axis=-1, keepdims=True)
    lifted = jnp.exp2(scores - row_top)
    return lifted * (1.0 / jnp.sum(lifted, axis=-1, keepdims=True))


def column_of(token):
    return (token % LINE) // 8 * GROUP + token % GROUP


def remote(src, dst, send_sem, recv_sem, **device):
    return pltpu.make_async_remote_copy(
        src_ref=src, dst_ref=dst, send_sem=send_sem, recv_sem=recv_sem,
        device_id=device, device_id_type=MESH,
    )


def attention(queries, keys, values, bias):
    count = queries.shape[0]
    lane_head = iota((count, 256), 1) // HEAD
    halves = []
    for half in range(2):
        cut = slice(256 * half, 256 * half + 256)
        part = queries[:, cut]
        stacked = jnp.concatenate(
            [jnp.where(lane_head == h, part, 0.0).astype(BF16) for h in range(8)], axis=0
        )
        scores = lax.dot_general(stacked, keys[:, cut], NT, preferred_element_type=F32)
        scores = scores.reshape(8, count, KEYS) * EXP2_SCALE + bias[None]
        weights = softmax_rows(scores).astype(BF16).reshape(8 * count, KEYS)
        mixed = dot(weights, values[:, cut]).reshape(8, count, 256)
        total = jnp.zeros((count, 256), F32)
        for h in range(8):
            total = jnp.where(lane_head == h, mixed[h], total)
        halves.append(total.astype(BF16))
    return jnp.concatenate(halves, axis=-1)


def pick_pixels(fields, stage, send):
    flat = fields.astype(F32).reshape(8 * ROWS * PATCH, 384).astype(BF16)
    row = iota((512, 1), 0)
    column = row % 16
    source = jnp.where(column < COLS, (row % 128) // 16 * 48 + column * PATCH + row // 128, -1)
    pick = jnp.where(source == iota((512, 384), 1), 1.0, 0.0).astype(BF16)
    turned = lax.dot_general(pick, flat, NT, preferred_element_type=F32).astype(BF16)
    row = iota((192, 1), 0)
    target = (row // PATCH) % ROWS * 128 + row // (ROWS * PATCH) * PIX + row % PATCH * PATCH
    lane = iota((192, 768), 1)
    total = jnp.zeros((128, 768), F32)
    for j in range(PATCH):
        place = jnp.where(target + j == lane, 1.0, 0.0).astype(BF16)
        total = total + dot(turned[128 * j : 128 * j + 128], place)
    for sector in range(8):
        stage[sector, 72:80, :] = jnp.zeros((8, 128), F32)
        for line in range(ROWS):
            stage[sector, COLS * line : COLS * line + COLS, :] = total[
                16 * sector : 16 * sector + COLS, 128 * line : 128 * line + 128
            ]
    send[...] = stage[...].astype(BF16)


def prepare_weights(ids_ref, shift_ref, embed, query_ref, wk, slot_w, keys_scr, bias_scr, query_scr):
    def place(slot, carry):
        start = pl.multiple_of(slot * PIX, PIX)
        slot_w[pl.ds(start, PIX), :] = embed[ids_ref[slot]]
        return carry

    lax.fori_loop(0, FIELDS, place, 0)
    swap = shift_ref[1] > shift_ref[0]
    query = query_ref[...].astype(F32)
    swapped = jnp.concatenate([query[2:], query[:2]], axis=0)
    query = jnp.where(swap, swapped, query)
    level = (iota((256, D), 0) // GROUP) % LEVELS
    spread = jnp.zeros((256, D), F32)
    for lev in range(LEVELS):
        spread = jnp.where(level == lev, query[lev : lev + 1, :], spread)
    query_scr[...] = spread[:16]
    own_head = iota((256, D), 1) // HEAD == iota((256, D), 0) // 16
    masked = jnp.where(own_head, spread, 0.0).astype(BF16)
    keys_scr[...] = lax.dot_general(
        masked, wk[...], NT, preferred_element_type=F32
    ).astype(BF16)
    same = iota((256, 256), 1) // FIELDS == iota((256, 256), 0) % GROUP
    bias_scr[...] = jnp.where(same, 0.0, MASKED)


def merge_line(line, line_pixels, slot_w, keys_scr, bias_scr, normed_scr, pooled_scr):
    own_slot = iota((1, 16, 256), 2) // PIX == iota((1, 16, 256), 1)
    for part in range(4):
        pixels = line_pixels[line, :, 256 * part : 256 * part + 256][:COLS]
        spread = jnp.where(own_slot, pixels[:, None, :], 0.0).astype(BF16)
        tokens = dot(spread.reshape(COLS * 16, 256), slot_w[256 * part : 256 * part + 256, :])
        normed = layer_norm(tokens.astype(BF16).astype(F32)).astype(BF16)
        normed_scr[:, 16 * part : 16 * part + 16, :] = normed.reshape(COLS, 16, D)
    for quad in range(QUADS):
        normed = normed_scr[GROUP * quad : GROUP * quad + GROUP].reshape(GROUP * FIELDS, D)
        scores = lax.dot_general(keys_scr[...], normed, NT, preferred_element_type=F32)
        weights = softmax_rows(scores * EXP2_SCALE + bias_scr[...]).astype(BF16)
        pooled = dot(weights, normed).astype(BF16)
        start = pl.multiple_of(line * 48 + quad * 16, 16)
        pooled_scr[:, pl.ds(start, 16), :] = pooled.reshape(HEADS, 16, D)


def project(pooled_scr, wv, query_scr):
    halves = []
    for half in range(2):
        lane_head = iota((D, 256), 1) // HEAD
        value_w = wv[:, 256 * half : 256 * half + 256].astype(F32)
        total = jnp.zeros((2 * OWN, 256), F32)
        for head in range(8):
            masked = jnp.where(lane_head == head, value_w, 0.0).astype(BF16)
            total = total + dot(pooled_scr[8 * half + head], masked)
        halves.append(total)
    projected = jnp.concatenate(halves, axis=-1).reshape(ROWS * QUADS, 16, D)
    return projected + query_scr[...][None]


def last_quads(tokens):
    tokens = tokens.reshape(ROWS * QUADS, 8, D)
    return jnp.concatenate([tokens[QUADS * r + 2] for r in range(ROWS)], axis=0)


def with_last_column(tokens, quads):
    tokens = tokens.reshape(ROWS * QUADS, 8, D)
    is_last = iota((8, D), 0) % GROUP == GROUP - 1
    pieces = []
    for r in range(ROWS):
        own = tokens[QUADS * r + 2]
        pieces += [tokens[QUADS * r], tokens[QUADS * r + 1]]
        pieces += [jnp.where(is_last, quads[8 * r : 8 * r + 8], own)]
    return jnp.concatenate(pieces, axis=0)


def whole_kernel(
    ids_ref, shift_ref, window_ref, fields_ref, query_ref, embed_h, wk_h, wv_h, qkv_h, wo_h, out_ref,
    embed, wk, wv, qkv, wo, slot_w, keys_scr, bias_scr, normed_scr, pooled_scr, query_scr,
    stage, send, recv, line_pixels, latents, slab, edge_send, edge_recv, col_recv, up_recv, down_recv,
    encoded, back_edge_send, back_edge_recv, back_recv,
    load_sem, pix_send_sem, pix_recv_sem, col_send_sem, col_recv_sem, row_send_sem, row_recv_sem,
    back_send_sem, back_recv_sem, relay, relay_send_sem, relay_recv_sem, hub_send_sem, unit_recv_sem,
):
    sector = lax.axis_index("var")
    sectors = lax.axis_size("var")
    band = lax.axis_index("lat")
    bands = lax.axis_size("lat")
    right = lax.rem(sector + 1, sectors)
    left = lax.rem(sector + sectors - 1, sectors)
    relayed = bands == 64
    half_bands = bands // 2
    hub_low, hub_high = half_bands - 1, half_bands
    partner = lax.rem(band + half_bands, bands)
    is_low = band < half_bands
    is_hub = (band == hub_low) | (band == hub_high)
    is_odd = lax.rem(band, 2) == 1
    sends_on = is_odd == is_low
    unit = lax.rem(band, half_bands) // 2
    has_up = band > 0
    has_down = band < bands - 1
    if relayed:
        has_up = has_up & (band != hub_high)
        has_down = has_down & (band != hub_low)

    barrier = pltpu.get_barrier_semaphore()
    for k in range(1, sectors):
        pl.semaphore_signal(
            barrier, inc=1, device_id={"var": lax.rem(sector + k, sectors)}, device_id_type=MESH
        )

    @pl.when(has_up)
    def _():
        pl.semaphore_signal(barrier, inc=1, device_id={"lat": band - 1}, device_id_type=MESH)

    @pl.when(has_down)
    def _():
        pl.semaphore_signal(barrier, inc=1, device_id={"lat": band + 1}, device_id_type=MESH)

    greetings = sectors - 1 + jnp.where(has_up, 1, 0) + jnp.where(has_down, 1, 0)
    if relayed:
        pl.semaphore_signal(barrier, inc=1, device_id={"lat": partner}, device_id_type=MESH)
        greetings = greetings + 1 + jnp.where(is_hub, half_bands - 1, 1)

        @pl.when(jnp.logical_not(is_hub))
        def _():
            hub = jnp.where(is_low, hub_low, hub_high)
            pl.semaphore_signal(barrier, inc=1, device_id={"lat": hub}, device_id_type=MESH)

        def greet(other, carry):
            other = other + jnp.where(band == hub_high, hub_high + 1, 0)
            pl.semaphore_signal(barrier, inc=1, device_id={"lat": other}, device_id_type=MESH)
            return carry

        @pl.when(is_hub)
        def _():
            lax.fori_loop(0, half_bands - 1, greet, 0)

    loads = [
        pltpu.make_async_copy(src, dst, load_sem.at[i])
        for i, (src, dst) in enumerate(
            [(embed_h, embed), (wk_h, wk), (wv_h, wv), (qkv_h, qkv), (wo_h, wo)]
        )
    ]
    for load in loads:
        load.start()

    pick_pixels(fields_ref[...], stage, send)

    @pl.when(band == 0)
    def _():
        up_recv[...] = jnp.zeros_like(up_recv)

    @pl.when(band == bands - 1)
    def _():
        down_recv[...] = jnp.zeros_like(down_recv)

    pl.semaphore_wait(barrier, greetings)

    def pixel_copy(piece, k, peer, slot):
        start, count = PIECES[piece]
        return remote(
            send.at[peer, pl.ds(start, count)], recv.at[slot, pl.ds(start, count)],
            pix_send_sem.at[piece, k], pix_recv_sem.at[piece, k], var=peer,
        )

    for piece in range(len(PIECES)):
        for k in SEND_ORDER:
            pixel_copy(piece, k, lax.rem(sector + k, sectors), sector).start()
    recv[sector] = send[sector]

    loads[0].wait()
    loads[1].wait()
    prepare_weights(
        ids_ref, shift_ref, embed, query_ref, wk, slot_w, keys_scr, bias_scr, query_scr
    )

    def take_piece(piece, lines):
        for k in range(1, sectors):
            source = lax.rem(sector + sectors - k, sectors)
            pixel_copy(piece, k, source, source).wait_recv()
        start, count = PIECES[piece]
        stage[:, start : start + count, :] = recv[:, start : start + count, :].astype(F32)
        for line in lines:
            for source in range(sectors):
                line_pixels[line, 0:COLS, 128 * source : 128 * source + 128] = stage[
                    source, COLS * line : COLS * line + COLS, :
                ]

    def one_line(line, carry):
        @pl.when(line == 0)
        def _():
            take_piece(0, (0,))

        @pl.when(line == 1)
        def _():
            take_piece(1, (1, 2, 3))

        @pl.when(line == 4)
        def _():
            take_piece(2, (4, 5))

        merge_line(line, line_pixels, slot_w, keys_scr, bias_scr, normed_scr, pooled_scr)
        return carry

    lax.fori_loop(0, ROWS, one_line, 0)

    loads[2].wait()
    fresh = project(pooled_scr, wv, query_scr)
    for pair in range(2):
        tokens = fresh[:, 8 * pair : 8 * pair + 8].reshape(OWN, D)
        latents[pair] = tokens.astype(BF16)
        if pair == 0:
            edge_send[...] = last_quads(tokens).astype(BF16)

    edge_out = remote(edge_send, edge_recv, col_send_sem.at[0], col_recv_sem.at[0], var=right)
    edge_out.start()
    col_out = remote(latents.at[1], col_recv, col_send_sem.at[1], col_recv_sem.at[1], var=left)
    col_out.start()

    def row_copies(pair):
        upward = remote(
            slab.at[pair, pl.ds(0, HALO)], down_recv.at[pair],
            row_send_sem.at[pair, 0], row_recv_sem.at[pair, 0], lat=band - 1,
        )
        downward = remote(
            slab.at[pair, pl.ds(OWN - HALO, HALO)], up_recv.at[pair],
            row_send_sem.at[pair, 1], row_recv_sem.at[pair, 1], lat=band + 1,
        )
        return upward, downward

    def hub_copies(pair, upward):
        copies = []
        for block in range(8):
            number = 8 * pair + block
            helper = half_bands + 2 * number if upward else 2 * number + 1
            helper = {hub_low: bands - 1, hub_high: 0}.get(helper, helper)
            start = 16 * block + (0 if upward else OWN - HALO)
            copies.append(
                remote(
                    slab.at[pair, pl.ds(start, 16)], relay, hub_send_sem.at[number], relay_recv_sem.at[0],
                    lat=helper,
                )
            )
        return copies

    relay_pair, relay_start = unit // 8, pl.multiple_of(lax.rem(unit, 8) * 16, 16)
    relay_on = remote(relay, relay, relay_send_sem.at[0], relay_recv_sem.at[0], lat=partner)

    def relay_in(landing, number, start, pair, hub):
        return remote(
            relay, landing.at[pair, pl.ds(start, 16)],
            relay_send_sem.at[0], unit_recv_sem.at[number], lat=hub,
        )

    def relay_first(pair):
        @pl.when(sends_on & jnp.logical_not(is_hub) & (relay_pair == pair))
        def _():
            relay_on.wait_recv()
            relay_on.start()

    def relay_second(pair):
        @pl.when(jnp.logical_not(sends_on) & (relay_pair == pair))
        def _():
            relay_on.wait_recv()

            @pl.when(is_low)
            def _():
                relay_in(down_recv, unit, relay_start, relay_pair, hub_low).start()

            @pl.when(jnp.logical_not(is_low))
            def _():
                relay_in(up_recv, unit, relay_start, relay_pair, hub_high).start()

    def send_rows(pair):
        upward, downward = row_copies(pair)

        @pl.when(has_up)
        def _():
            upward.start()

        @pl.when(has_down)
        def _():
            downward.start()

        if relayed:
            @pl.when(band == hub_low)
            def _():
                for copy in hub_copies(pair, False):
                    copy.start()

            @pl.when(band == hub_high)
            def _():
                for copy in hub_copies(pair, True):
                    copy.start()

    def take_rows(pair):
        upward, downward = row_copies(pair)

        @pl.when(has_down)
        def _():
            upward.wait_recv()

        @pl.when(has_up)
        def _():
            downward.wait_recv()

        if relayed:
            @pl.when(band == hub_low)
            def _():
                for block in range(8):
                    relay_in(down_recv, 8 * pair + block, 16 * block, pair, hub_low).wait_recv()

            @pl.when(band == hub_high)
            def _():
                for block in range(8):
                    relay_in(up_recv, 8 * pair + block, 16 * block, pair, hub_high).wait_recv()

    shift = jnp.minimum(shift_ref[0], shift_ref[1])
    column = column_of(iota((OWN, D), 0))
    edge_out.wait_recv()
    slab[0] = with_last_column(latents[0].astype(F32), edge_recv[...].astype(F32)).astype(BF16)
    send_rows(0)
    if relayed:
        relay_first(0)
    col_out.wait_recv()
    slab[1] = jnp.where(
        column < shift, col_recv[...].astype(F32), latents[1].astype(F32)
    ).astype(BF16)
    send_rows(1)
    if relayed:
        relay_second(0)
        relay_first(1)

    first = band * ROWS - (WIN_LAT - 1)
    total_rows = window_ref.shape[0]
    key_token = iota((1, KEYS), 1)
    query_token = iota((OWN, 1), 0)
    key_row = jnp.full((1, KEYS), -1, jnp.int32)
    query_row = jnp.full((OWN, 1), -1, jnp.int32)
    for k in range(ROWS + 2 * (WIN_LAT - 1)):
        row = first + k
        inside = (row >= 0) & (row < total_rows)
        ident = jnp.where(inside, window_ref[jnp.clip(row, 0, total_rows - 1)], -1)
        key_row = jnp.where(key_token // LINE == k, ident, key_row)
        if 0 <= k - (WIN_LAT - 1) < ROWS:
            query_row = jnp.where(query_token // LINE == k - (WIN_LAT - 1), ident, query_row)

    loads[3].wait()
    loads[4].wait()
    for pair in range(2):
        def wrapped(token):
            if pair == 0:
                return jnp.where((column_of(token) == COLS - 1) & (sector == 0), 1, 0)
            return jnp.where((column_of(token) < shift) & (sector == sectors - 1), 1, 0)

        same = (query_row * 2 + wrapped(query_token)) == (key_row * 2 + wrapped(key_token))
        bias = jnp.where(same, 0.0, MASKED)
        own = slab[pair].astype(F32)
        take_rows(pair)
        up = up_recv[pair].astype(F32)[HALO - EDGE :]
        down = down_recv[pair].astype(F32)[:EDGE]
        normed = layer_norm(jnp.concatenate([up, own, down], axis=0))
        queries = dot(normed[EDGE : EDGE + OWN].astype(BF16), qkv[:, :D])
        normed = normed.astype(BF16)
        keys = dot(normed, qkv[:, D : 2 * D]).astype(BF16)
        values = dot(normed, qkv[:, 2 * D :]).astype(BF16)
        for part, (start, stop) in enumerate(QUERY_PARTS[pair]):
            mixed = attention(queries[start:stop], keys, values, bias[start:stop])
            done = own[start:stop] + dot(mixed, wo[...])
            encoded[pair, start:stop] = done.astype(BF16)
            if relayed and pair == 0 and part == 0:
                relay_second(1)
            if pair == 0 and part == 0:
                continue
            if pair == 0:
                done = encoded[0].astype(F32)
                back_edge_send[...] = last_quads(done).astype(BF16)
                back_edge = remote(
                    back_edge_send, back_edge_recv, back_send_sem.at[0], back_recv_sem.at[0], var=left
                )
                back_edge.start()
                backs = [back_edge]
            else:
                back = remote(
                    encoded.at[1, pl.ds(start, stop - start)], back_recv.at[pl.ds(start, stop - start)],
                    back_send_sem.at[1 + part], back_recv_sem.at[1 + part], var=right,
                )
                back.start()
                backs.append(back)

    swap = jnp.where(shift_ref[1] > shift_ref[0], 1, 0)
    row = iota((2 * OWN, OWN), 0)
    level = row % LEVELS
    place = row // 48 * LINE + row % 48 // 16 * 8 + level % 2 * GROUP + row % 16 // LEVELS
    hit = place == iota((2 * OWN, OWN), 1)
    orders = [
        jnp.where(hit & (level // 2 == (swap if pair == 0 else 1 - swap)), 1.0, 0.0).astype(BF16)
        for pair in range(2)
    ]
    backs[0].wait_recv()
    first_pair = with_last_column(encoded[0].astype(F32), back_edge_recv[...].astype(F32))
    result = dot(orders[0], first_pair.astype(BF16))
    backs[1].wait_recv()
    backs[2].wait_recv()
    second_pair = jnp.where(column < shift, back_recv[...].astype(F32), encoded[1].astype(F32))
    result = result + dot(orders[1], second_pair.astype(BF16))
    out_ref[...] = result.reshape(ROWS, COLS, LEVELS, D).astype(BF16)

    for piece in range(len(PIECES)):
        for k in range(1, sectors):
            pixel_copy(piece, k, lax.rem(sector + k, sectors), sector).wait_send()
    edge_out.wait_send()
    col_out.wait_send()
    for pair in range(2):
        upward, downward = row_copies(pair)

        @pl.when(has_up)
        def _():
            upward.wait_send()

        @pl.when(has_down)
        def _():
            downward.wait_send()

    if relayed:
        @pl.when(band == hub_low)
        def _():
            for copy in hub_copies(0, False) + hub_copies(1, False):
                copy.wait_send()

        @pl.when(band == hub_high)
        def _():
            for copy in hub_copies(0, True) + hub_copies(1, True):
                copy.wait_send()

        @pl.when(jnp.logical_not(sends_on & is_hub))
        def _():
            relay_on.wait_send()

    for back in backs:
        back.wait_send()


def shards(
    fields, field_ids, embed_w, lat_query, perc_wk, perc_wv, swin_qkv, swin_wo, row_window, lon_shift
):
    vmem = pl.BlockSpec(memory_space=pltpu.VMEM)
    smem = pl.BlockSpec(memory_space=pltpu.SMEM)
    hbm = pl.BlockSpec(memory_space=pl.ANY)
    encoded = pl.pallas_call(
        whole_kernel,
        out_shape=jax.ShapeDtypeStruct((ROWS, COLS, LEVELS, D), BF16),
        in_specs=[smem] * 3 + [vmem] * 2 + [hbm] * 5,
        out_specs=vmem,
        scratch_shapes=[
            pltpu.VMEM((FIELDS, PIX, D), BF16),
            pltpu.VMEM((D, D), BF16),
            pltpu.VMEM((D, D), BF16),
            pltpu.VMEM((D, 3 * D), BF16),
            pltpu.VMEM((D, D), BF16),
            pltpu.VMEM((FIELDS * PIX, D), BF16),
            pltpu.VMEM((256, D), BF16),
            pltpu.VMEM((256, 256), F32),
            pltpu.VMEM((COLS, FIELDS, D), BF16),
            pltpu.VMEM((HEADS, 2 * OWN, D), BF16),
            pltpu.VMEM((16, D), F32),
            pltpu.VMEM((8, 80, 128), F32),
            pltpu.VMEM((8, 80, 128), BF16),
            pltpu.VMEM((8, 80, 128), BF16),
            pltpu.VMEM((ROWS, 16, FIELDS * PIX), F32),
            pltpu.VMEM((2, OWN, D), BF16),
            pltpu.VMEM((2, OWN, D), BF16),
            pltpu.VMEM((48, D), BF16),
            pltpu.VMEM((48, D), BF16),
            pltpu.VMEM((OWN, D), BF16),
            pltpu.VMEM((2, HALO, D), BF16),
            pltpu.VMEM((2, HALO, D), BF16),
            pltpu.VMEM((2, OWN, D), BF16),
            pltpu.VMEM((48, D), BF16),
            pltpu.VMEM((48, D), BF16),
            pltpu.VMEM((OWN, D), BF16),
            pltpu.SemaphoreType.DMA((5,)),
            pltpu.SemaphoreType.DMA((3, 8)),
            pltpu.SemaphoreType.DMA((3, 8)),
            pltpu.SemaphoreType.DMA((2,)),
            pltpu.SemaphoreType.DMA((2,)),
            pltpu.SemaphoreType.DMA((2, 2)),
            pltpu.SemaphoreType.DMA((2, 2)),
            pltpu.SemaphoreType.DMA((3,)),
            pltpu.SemaphoreType.DMA((3,)),
            pltpu.VMEM((16, D), BF16),
            pltpu.SemaphoreType.DMA((1,)),
            pltpu.SemaphoreType.DMA((1,)),
            pltpu.SemaphoreType.DMA((16,)),
            pltpu.SemaphoreType.DMA((16,)),
        ],
        compiler_params=pltpu.CompilerParams(
            vmem_limit_bytes=63 << 20, collective_id=0, has_side_effects=True
        ),
        name="whole",
    )(
        field_ids, lon_shift, row_window, fields, lat_query, embed_w, perc_wk, perc_wv, swin_qkv, swin_wo
    )
    return jnp.transpose(encoded, (2, 0, 1, 3))


def solution(mesh):
    in_specs = (P("var", "lat", None), P(), P(), P(), P(), P(), P(), P(), P(), P())
    out_specs = P(None, "lat", "var", None)
    return jax.shard_map(shards, mesh=mesh, in_specs=in_specs, out_specs=out_specs, check_vma=False)
```

```python
import functools
import math

import jax
import jax.numpy as jnp
from jax import lax
from jax.experimental import pallas as pl
from jax.experimental.pallas import tpu as pltpu
from jax.sharding import PartitionSpec as P

D = 512
HEADS = 16
HEAD = 32
LEVELS = 4
PATCH = 4
WIN_LAT = 6
WIN_LON = 12
FIELDS = 64
ROWS = 6
COLS = 12
PIX = PATCH * PATCH
GROUP = 4
QUADS = COLS // GROUP
LINE = 2 * COLS
OWN = ROWS * LINE
HALO = 128
KEYS = 384
EDGE = 120

EPSILON = 1e-05
MASKED = -1e30
EXP2_SCALE = math.log2(math.e) / math.sqrt(HEAD)
F32 = jnp.float32
BF16 = jnp.bfloat16
NT = (((1,), (1,)), ((), ()))
MESH = pl.DeviceIdType.MESH
SEND_ORDER = (4, 3, 5, 2, 6, 1, 7)
CHUNKS = 3
EMBED_STEP = 2
MERGE_STEP = 3
CHUNK = 2 * LINE
UP_PARTS = ((0, 48), (48, 48), (96, 32))
DOWN_PARTS = ((16, 32), (48, 48), (96, 48))


def dot(a, b):
    return jnp.dot(a, b, preferred_element_type=F32)


def iota(shape, dim):
    return lax.broadcasted_iota(jnp.int32, shape, dim)


def layer_norm(values):
    row_mean = jnp.sum(values, axis=-1, keepdims=True) * (1.0 / D)
    centred = values - row_mean
    variance = jnp.sum(centred * centred, axis=-1, keepdims=True) * (1.0 / D)
    return centred * lax.rsqrt(variance + EPSILON)


def softmax_rows(scores):
    row_top = jnp.max(scores, axis=-1, keepdims=True)
    lifted = jnp.exp2(scores - row_top)
    return lifted * (1.0 / jnp.sum(lifted, axis=-1, keepdims=True))


def column_of(token):
    return (token % LINE) // 8 * GROUP + token % GROUP


def remote(src, dst, send_sem, recv_sem, **device):
    return pltpu.make_async_remote_copy(
        src_ref=src, dst_ref=dst, send_sem=send_sem, recv_sem=recv_sem,
        device_id=device, device_id_type=MESH,
    )


def start_copy(copy):
    copy.start()


def wait_received(copy):
    copy.wait_recv()


def wait_sent(copy):
    copy.wait_send()


def attention(queries, keys, values, bias):
    count, key_count = queries.shape[0], keys.shape[0]
    lane_head = iota((count, 256), 1) // HEAD
    halves = []
    for half in range(2):
        cut = slice(256 * half, 256 * half + 256)
        part = queries[:, cut]
        stacked = jnp.concatenate(
            [jnp.where(lane_head == h, part, 0.0).astype(BF16) for h in range(8)], axis=0
        )
        scores = lax.dot_general(stacked, keys[:, cut], NT, preferred_element_type=F32)
        scores = scores.reshape(8, count, key_count) * EXP2_SCALE + bias[None]
        weights = softmax_rows(scores).astype(BF16).reshape(8 * count, key_count)
        mixed = dot(weights, values[:, cut]).reshape(8, count, 256)
        total = jnp.zeros((count, 256), F32)
        for h in range(8):
            total = jnp.where(lane_head == h, mixed[h], total)
        halves.append(total.astype(BF16))
    return jnp.concatenate(halves, axis=-1)


def pick_pixels(fields, stage, send):
    flat = fields.astype(F32).reshape(8 * ROWS * PATCH, 384).astype(BF16)
    row = iota((512, 1), 0)
    column = row % 16
    source = jnp.where(column < COLS, (row % 128) // 16 * 48 + column * PATCH + row // 128, -1)
    pick = jnp.where(source == iota((512, 384), 1), 1.0, 0.0).astype(BF16)
    turned = lax.dot_general(pick, flat, NT, preferred_element_type=F32).astype(BF16)
    row = iota((192, 1), 0)
    target = (row // PATCH) % ROWS * 128 + row // (ROWS * PATCH) * PIX + row % PATCH * PATCH
    lane = iota((192, 768), 1)
    total = jnp.zeros((128, 768), F32)
    for j in range(PATCH):
        place = jnp.where(target + j == lane, 1.0, 0.0).astype(BF16)
        total = total + dot(turned[128 * j : 128 * j + 128], place)
    for sector in range(8):
        stage[sector, 72:80, :] = jnp.zeros((8, 128), F32)
        for line in range(ROWS):
            stage[sector, COLS * line : COLS * line + COLS, :] = total[
                16 * sector : 16 * sector + COLS, 128 * line : 128 * line + 128
            ]
    send[...] = stage[...].astype(BF16)


def prepare_weights(ids_ref, shift_ref, embed, query_ref, wk, slot_w, keys_scr, bias_scr, query_scr):
    def place(slot, carry):
        start = pl.multiple_of(slot * PIX, PIX)
        slot_w[pl.ds(start, PIX), :] = embed[ids_ref[slot]]
        return carry

    lax.fori_loop(0, FIELDS, place, 0)
    swap = shift_ref[1] > shift_ref[0]
    query = query_ref[...].astype(F32)
    swapped = jnp.concatenate([query[2:], query[:2]], axis=0)
    query = jnp.where(swap, swapped, query)
    level = (iota((256, D), 0) // GROUP) % LEVELS
    spread = jnp.zeros((256, D), F32)
    for lev in range(LEVELS):
        spread = jnp.where(level == lev, query[lev : lev + 1, :], spread)
    query_scr[...] = spread[:16]
    own_head = iota((256, D), 1) // HEAD == iota((256, D), 0) // 16
    masked = jnp.where(own_head, spread, 0.0).astype(BF16)
    keys_scr[...] = lax.dot_general(
        masked, wk[...], NT, preferred_element_type=F32
    ).astype(BF16)
    same = iota((256, 256), 1) // FIELDS == iota((256, 256), 0) % GROUP
    bias_scr[...] = jnp.where(same, 0.0, MASKED)


def embed_line(line, part, line_pixels, slot_w, normed_scr):
    own_slot = iota((1, 16, 256), 2) // PIX == iota((1, 16, 256), 1)
    pixels = line_pixels[line][:COLS]
    spread = jnp.where(own_slot, pixels[:, None, :], 0.0).astype(BF16)
    weight = slot_w[pl.ds(pl.multiple_of(256 * part, 256), 256), :]
    tokens = dot(spread.reshape(COLS * 16, 256), weight)
    normed = layer_norm(tokens.astype(BF16).astype(F32)).astype(BF16)
    slots = pl.ds(pl.multiple_of(16 * part, 16), 16)
    normed_scr[pl.ds(line * COLS, COLS), slots, :] = normed.reshape(COLS, 16, D)


def merge_quad(quad, keys_scr, bias_scr, normed_scr, pooled_scr):
    normed = normed_scr[pl.ds(quad * GROUP, GROUP)].reshape(GROUP * FIELDS, D)
    scores = lax.dot_general(keys_scr[...], normed, NT, preferred_element_type=F32)
    weights = softmax_rows(scores * EXP2_SCALE + bias_scr[...]).astype(BF16)
    pooled = dot(weights, normed).astype(BF16)
    start = pl.multiple_of(quad * 16, 16)
    pooled_scr[:, pl.ds(start, 16), :] = pooled.reshape(HEADS, 16, D)


def project(chunk, pooled_scr, wv, query_scr):
    start = pl.multiple_of(chunk * 2 * CHUNK, 2 * CHUNK)
    halves = []
    for half in range(2):
        lane_head = iota((D, 256), 1) // HEAD
        value_w = wv[:, 256 * half : 256 * half + 256].astype(F32)
        total = jnp.zeros((2 * CHUNK, 256), F32)
        for head in range(8):
            masked = jnp.where(lane_head == head, value_w, 0.0).astype(BF16)
            total = total + dot(pooled_scr[8 * half + head, pl.ds(start, 2 * CHUNK), :], masked)
        halves.append(total)
    projected = jnp.concatenate(halves, axis=-1).reshape(2 * QUADS, 16, D)
    return projected + query_scr[...][None]


def quads_of(tokens, last):
    width = tokens.shape[-1]
    tokens = tokens.reshape(tokens.shape[0] // 8, 8, width)
    picked = [q for q in range(tokens.shape[0]) if (q % QUADS == QUADS - 1) == last]
    return jnp.concatenate([tokens[q] for q in picked], axis=0)


def with_last_column(rest, own, received):
    is_last = iota(own.shape, 0) % GROUP == GROUP - 1
    last = jnp.where(is_last, received, own)
    pieces = []
    for r in range(own.shape[0] // 8):
        pieces += [rest[16 * r : 16 * r + 16], last[8 * r : 8 * r + 8]]
    return jnp.concatenate(pieces, axis=0)


def whole_kernel(
    ids_ref, shift_ref, window_ref, fields_ref, query_ref, embed_h, wk_h, wv_h, qkv_h, wo_h, out_ref,
    embed, wk, wv, qkv, wo, slot_w, keys_scr, bias_scr, normed_scr, pooled_scr, query_scr,
    stage, send, recv, line_pixels, latents, slab, edge_send, edge_recv, col_recv, up_recv, down_recv,
    encoded, back_edge_recv, back_recv,
    load_sem, pix_send_sem, pix_recv_sem, col_send_sem, col_recv_sem, row_send_sem, row_recv_sem,
    back_send_sem, back_recv_sem, extra_up, extra_down, extra_send_sem, extra_recv_sem,
):
    sector = lax.axis_index("var")
    sectors = lax.axis_size("var")
    band = lax.axis_index("lat")
    bands = lax.axis_size("lat")
    right = lax.rem(sector + 1, sectors)
    left = lax.rem(sector + sectors - 1, sectors)
    is_first = sector == 0
    is_last = sector == sectors - 1
    is_end = is_first | is_last
    has_left = jnp.logical_not(is_first)
    has_right = jnp.logical_not(is_last)
    has_up = band > 0
    has_down = band < bands - 1

    barrier = pltpu.get_barrier_semaphore()
    for k in range(1, sectors):
        pl.semaphore_signal(
            barrier, inc=1, device_id={"var": lax.rem(sector + k, sectors)}, device_id_type=MESH
        )

    @pl.when(has_up)
    def _():
        pl.semaphore_signal(barrier, inc=1, device_id={"lat": band - 1}, device_id_type=MESH)

    @pl.when(has_down)
    def _():
        pl.semaphore_signal(barrier, inc=1, device_id={"lat": band + 1}, device_id_type=MESH)

    loads = [
        pltpu.make_async_copy(src, dst, load_sem.at[i])
        for i, (src, dst) in enumerate(
            [(embed_h, embed), (wk_h, wk), (wv_h, wv), (qkv_h, qkv), (wo_h, wo)]
        )
    ]
    for load in loads:
        load.start()

    pick_pixels(fields_ref[...], stage, send)

    @pl.when(jnp.logical_not(has_up))
    def _():
        up_recv[...] = jnp.zeros_like(up_recv)

    @pl.when(jnp.logical_not(has_down))
    def _():
        down_recv[...] = jnp.zeros_like(down_recv)

    @pl.when((band == 0) & is_end)
    def _():
        extra_up[...] = jnp.zeros_like(extra_up)

    @pl.when((band == bands - 1) & is_end)
    def _():
        extra_down[...] = jnp.zeros_like(extra_down)

    @pl.when(is_first)
    def _():
        edge_recv[...] = jnp.zeros_like(edge_recv)

    @pl.when(is_last)
    def _():
        col_recv[...] = jnp.zeros_like(col_recv)

    neighbours = jnp.where(has_up, 1, 0) + jnp.where(has_down, 1, 0)
    pl.semaphore_wait(barrier, sectors - 1 + neighbours)

    def pixel_copy(k, peer, slot):
        return remote(
            send.at[peer], recv.at[slot], pix_send_sem.at[k], pix_recv_sem.at[k], var=peer
        )

    for k in SEND_ORDER:
        pixel_copy(k, lax.rem(sector + k, sectors), sector).start()
    recv[sector] = send[sector]

    loads[0].wait()
    loads[1].wait()
    prepare_weights(
        ids_ref, shift_ref, embed, query_ref, wk, slot_w, keys_scr, bias_scr, query_scr
    )

    def one_part(turn, carry):
        own = sector // 2
        part = lax.rem(own // 2 + turn // 2, 2) * 2 + lax.rem(own % 2 + turn % 2, 2)
        for side in range(2):
            source = part * 2 + side

            @pl.when(source != sector)
            def _():
                pixel_copy(lax.rem(sector + sectors - source, sectors), source, source).wait_recv()

            stage[side] = recv[source].astype(F32)
            for line in range(ROWS):
                line_pixels[line, 0:COLS, 128 * side : 128 * side + 128] = stage[
                    side, COLS * line : COLS * line + COLS, :
                ]

        def lines(step, carry):
            for k in range(EMBED_STEP):
                embed_line(step * EMBED_STEP + k, part, line_pixels, slot_w, normed_scr)
            return carry

        lax.fori_loop(0, ROWS // EMBED_STEP, lines, 0)
        return carry

    lax.fori_loop(0, 4, one_part, 0)

    shift = jnp.minimum(shift_ref[0], shift_ref[1])

    def column_copies(chunk):
        quads = pl.ds(pl.multiple_of(chunk * 16, 16), 16)
        tokens = pl.ds(pl.multiple_of(chunk * CHUNK, 16), CHUNK)
        return (
            remote(
                edge_send.at[quads], edge_recv.at[quads],
                col_send_sem.at[0, chunk], col_recv_sem.at[0, chunk], var=right,
            ),
            remote(
                latents.at[1, tokens], col_recv.at[tokens],
                col_send_sem.at[1, chunk], col_recv_sem.at[1, chunk], var=left,
            ),
        )

    def extra_copies(chunk):
        quads = pl.ds(pl.multiple_of(chunk * 16, 16), 16)
        tokens = pl.ds(pl.multiple_of(chunk * CHUNK, 16), CHUNK)
        copies = []
        for end, src, part in ((is_first, latents.at[1, tokens], tokens), (is_last, edge_send.at[quads], quads)):
            copies.append((end & has_up, remote(
                src, extra_down.at[part], extra_send_sem.at[0, chunk], extra_recv_sem.at[0, chunk], lat=band - 1
            )))
            copies.append((end & has_down, remote(
                src, extra_up.at[part], extra_send_sem.at[1, chunk], extra_recv_sem.at[1, chunk], lat=band + 1
            )))
        return copies

    def take_extra():
        for chunk in range(CHUNKS):
            for i, (_, copy) in enumerate(extra_copies(chunk)):
                end = is_first if i < 2 else is_last
                pl.when(end & (has_down if i % 2 == 0 else has_up))(functools.partial(wait_received, copy))

    def row_copies(pair, chunk):
        (up_start, up_count), (down_start, down_count) = UP_PARTS[chunk], DOWN_PARTS[chunk]
        up_part, down_part = pl.ds(up_start, up_count), pl.ds(down_start, down_count)
        upward = remote(
            slab.at[pair, up_part], down_recv.at[pair, up_part],
            row_send_sem.at[pair, 0, chunk], row_recv_sem.at[pair, 0, chunk], lat=band - 1,
        )
        downward = remote(
            slab.at[pair, down_part], up_recv.at[pair, down_part],
            row_send_sem.at[pair, 1, chunk], row_recv_sem.at[pair, 1, chunk], lat=band + 1,
        )
        return upward, downward

    def send_rows(pair, chunk):
        upward, downward = row_copies(pair, chunk)

        @pl.when(has_up)
        def _():
            upward.start()

        @pl.when(has_down)
        def _():
            downward.start()

    def take_rows(pair):
        for chunk in range(CHUNKS):
            upward, downward = row_copies(pair, chunk)

            @pl.when(has_down)
            def _():
                upward.wait_recv()

            @pl.when(has_up)
            def _():
                downward.wait_recv()

    def share_rows(chunk):
        edge_copy, col_copy = column_copies(chunk)
        tokens = slice(CHUNK * chunk, CHUNK * chunk + CHUNK)
        quads = slice(16 * chunk, 16 * chunk + 16)
        pl.when(has_right)(lambda: wait_received(col_copy))
        column = column_of(iota((CHUNK, D), 0))
        slab[1, tokens] = jnp.where(
            column < shift, col_recv[tokens].astype(F32), latents[1, tokens].astype(F32)
        ).astype(BF16)
        send_rows(1, chunk)
        pl.when(has_left)(lambda: wait_received(edge_copy))
        own = latents[0, tokens].astype(F32)
        slab[0, tokens] = with_last_column(
            quads_of(own, False), quads_of(own, True), edge_recv[quads].astype(F32)
        ).astype(BF16)
        send_rows(0, chunk)

    loads[2].wait()

    def one_chunk(chunk, carry):
        def quads(step, carry):
            for k in range(MERGE_STEP):
                quad = chunk * 2 * QUADS + step * MERGE_STEP + k
                merge_quad(quad, keys_scr, bias_scr, normed_scr, pooled_scr)
            return carry

        lax.fori_loop(0, 2 * QUADS // MERGE_STEP, quads, 0)
        fresh = project(chunk, pooled_scr, wv, query_scr)
        start = pl.multiple_of(chunk * CHUNK, 16)
        for pair in range(2):
            tokens = fresh[:, 8 * pair : 8 * pair + 8].reshape(CHUNK, D)
            latents[pair, pl.ds(start, CHUNK), :] = tokens.astype(BF16)
            if pair == 0:
                quads = pl.ds(pl.multiple_of(chunk * 16, 16), 16)
                edge_send[quads, :] = quads_of(tokens, True).astype(BF16)
        edge_copy, col_copy = column_copies(chunk)
        pl.when(has_right)(lambda: start_copy(edge_copy))
        pl.when(has_left)(lambda: start_copy(col_copy))
        for where, copy in extra_copies(chunk):
            pl.when(where)(functools.partial(start_copy, copy))
        for ready in range(CHUNKS - 1):
            @pl.when(chunk == ready + 1)
            def _():
                share_rows(ready)

        return carry

    lax.fori_loop(0, CHUNKS, one_chunk, 0)
    share_rows(CHUNKS - 1)

    first = band * ROWS - (WIN_LAT - 1)
    total_rows = window_ref.shape[0]

    def row_ident(k):
        row = first + k
        inside = (row >= 0) & (row < total_rows)
        return jnp.where(inside, window_ref[jnp.clip(row, 0, total_rows - 1)], -1)

    key_token = iota((1, KEYS), 1)
    query_token = iota((OWN, 1), 0)
    key_row = jnp.full((1, KEYS), -1, jnp.int32)
    query_row = jnp.full((OWN, 1), -1, jnp.int32)
    for k in range(ROWS + 2 * (WIN_LAT - 1)):
        ident = row_ident(k)
        key_row = jnp.where(key_token // LINE == k, ident, key_row)
        if 0 <= k - (WIN_LAT - 1) < ROWS:
            query_row = jnp.where(query_token // LINE == k - (WIN_LAT - 1), ident, query_row)

    loads[3].wait()
    loads[4].wait()
    def around(own_part, halo_part):
        edge = halo_part.shape[0] // 2
        return jnp.concatenate([halo_part[:edge], own_part, halo_part[edge:]], axis=0).astype(BF16)

    def attend_extra(own, up, down, same):
        own_qkv = dot(layer_norm(own).astype(BF16), qkv[...])
        halo = jnp.concatenate([up.astype(F32), down.astype(F32)], axis=0)
        halo = dot(layer_norm(halo).astype(BF16), qkv[:, D:])
        keys = around(own_qkv[:, D : 2 * D], halo[:, :D])
        values = around(own_qkv[:, 2 * D :], halo[:, D:])
        mixed = attention(own_qkv[:, :D], keys, values, jnp.where(same, 0.0, MASKED))
        return (own + dot(mixed, wo[...])).astype(BF16)

    take_extra()

    @pl.when(is_first)
    def _():
        below = [jnp.where(column_of(token) < shift, 1, 0) for token in (query_token, key_token)]
        same = (query_row * 2 + below[0]) == (key_row * 2 + below[1])
        back_recv[...] = attend_extra(
            latents[1].astype(F32), extra_up[OWN - EDGE :], extra_down[:EDGE], same
        )

    @pl.when(is_last)
    def _():
        ident = [jnp.full((48, 1), -1, jnp.int32), jnp.full((1, 128), -1, jnp.int32)]
        token = [iota((48, 1), 0), iota((1, 128), 1)]
        for k in range(ROWS + 2 * (WIN_LAT - 1)):
            ident[1] = jnp.where(token[1] // 8 == k, row_ident(k), ident[1])
            ident[0] = jnp.where(token[0] // 8 == k - (WIN_LAT - 1), row_ident(k), ident[0])
        side = [jnp.where(t % GROUP == GROUP - 1, 1, 0) for t in token]
        same = (ident[0] * 2 + side[0]) == (ident[1] * 2 + side[1])
        back_edge_recv[...] = attend_extra(
            edge_send[...].astype(F32), extra_up[0:48].astype(F32)[8:], extra_down[0:48].astype(F32)[:40], same
        )

    own_parts = []
    for pair in range(2):
        own = slab[pair].astype(F32)
        own_parts.append((own, dot(layer_norm(own).astype(BF16), qkv[...])))

    def windows(pair):
        def wrapped(token):
            if pair == 0:
                return jnp.where((column_of(token) == COLS - 1) & (sector == 0), 1, 0)
            return jnp.where((column_of(token) < shift) & (sector == sectors - 1), 1, 0)

        same = (query_row * 2 + wrapped(query_token)) == (key_row * 2 + wrapped(key_token))
        bias = jnp.where(same, 0.0, MASKED)
        own, own_qkv = own_parts[pair]
        take_rows(pair)
        halo = jnp.concatenate(
            [up_recv[pair].astype(F32)[OWN - EDGE :], down_recv[pair].astype(F32)[:EDGE]], axis=0
        )
        halo = dot(layer_norm(halo).astype(BF16), qkv[:, D:])

        keys = around(own_qkv[:, D : 2 * D], halo[:, :D])
        values = around(own_qkv[:, 2 * D :], halo[:, D:])
        return own, own_qkv[:, :D], keys, values, bias

    backs = []
    own, queries, keys, values, bias = windows(1)
    for part, (start, stop) in enumerate(((0, 96), (96, OWN))):
        mixed = attention(queries[start:stop], keys, values, bias[start:stop])
        encoded[1, start:stop] = (own[start:stop] + dot(mixed, wo[...])).astype(BF16)
        back = remote(
            encoded.at[1, pl.ds(start, stop - start)], back_recv.at[pl.ds(start, stop - start)],
            back_send_sem.at[part], back_recv_sem.at[part], var=right,
        )
        pl.when(has_right)(functools.partial(start_copy, back))
        backs.append(back)

    own, queries, keys, values, bias = windows(0)
    for part, last in enumerate((True, False)):
        mixed = attention(quads_of(queries, last), keys, values, quads_of(bias, last))
        done = quads_of(own, last) + dot(mixed, wo[...])
        if last:
            encoded[0, 0:48] = done.astype(BF16)
            back = remote(
                encoded.at[0, pl.ds(0, 48)], back_edge_recv,
                back_send_sem.at[2], back_recv_sem.at[2], var=left,
            )
            pl.when(has_left)(functools.partial(start_copy, back))
            backs.append(back)
        else:
            first_rest = done

    swap = jnp.where(shift_ref[1] > shift_ref[0], 1, 0)
    row = iota((2 * OWN, OWN), 0)
    level = row % LEVELS
    place = row // 48 * LINE + row % 48 // 16 * 8 + level % 2 * GROUP + row % 16 // LEVELS
    hit = place == iota((2 * OWN, OWN), 1)
    orders = [
        jnp.where(hit & (level // 2 == (swap if pair == 0 else 1 - swap)), 1.0, 0.0).astype(BF16)
        for pair in range(2)
    ]
    pl.when(has_right)(lambda: wait_received(backs[2]))
    first_pair = with_last_column(
        first_rest, encoded[0, 0:48].astype(F32), back_edge_recv[...].astype(F32)
    )
    result = dot(orders[0], first_pair.astype(BF16))
    pl.when(has_left)(lambda: wait_received(backs[0]))
    pl.when(has_left)(lambda: wait_received(backs[1]))
    column = column_of(iota((OWN, D), 0))
    second_pair = jnp.where(column < shift, back_recv[...].astype(F32), encoded[1].astype(F32))
    result = result + dot(orders[1], second_pair.astype(BF16))
    out_ref[...] = result.reshape(ROWS, COLS, LEVELS, D).astype(BF16)

    for k in range(1, sectors):
        pixel_copy(k, lax.rem(sector + k, sectors), sector).wait_send()
    for chunk in range(CHUNKS):
        edge_copy, col_copy = column_copies(chunk)
        pl.when(has_right)(functools.partial(wait_sent, edge_copy))
        pl.when(has_left)(functools.partial(wait_sent, col_copy))
        for where, copy in extra_copies(chunk):
            pl.when(where)(functools.partial(wait_sent, copy))
        for pair in range(2):
            upward, downward = row_copies(pair, chunk)

            @pl.when(has_up)
            def _():
                upward.wait_send()

            @pl.when(has_down)
            def _():
                downward.wait_send()

    for back, where in zip(backs, (has_right, has_right, has_left)):
        pl.when(where)(functools.partial(wait_sent, back))


def shards(
    fields, field_ids, embed_w, lat_query, perc_wk, perc_wv, swin_qkv, swin_wo, row_window, lon_shift
):
    vmem = pl.BlockSpec(memory_space=pltpu.VMEM)
    smem = pl.BlockSpec(memory_space=pltpu.SMEM)
    hbm = pl.BlockSpec(memory_space=pl.ANY)
    encoded = pl.pallas_call(
        whole_kernel,
        out_shape=jax.ShapeDtypeStruct((ROWS, COLS, LEVELS, D), BF16),
        in_specs=[smem] * 3 + [vmem] * 2 + [hbm] * 5,
        out_specs=vmem,
        scratch_shapes=[
            pltpu.VMEM((FIELDS, PIX, D), BF16),
            pltpu.VMEM((D, D), BF16),
            pltpu.VMEM((D, D), BF16),
            pltpu.VMEM((D, 3 * D), BF16),
            pltpu.VMEM((D, D), BF16),
            pltpu.VMEM((FIELDS * PIX, D), BF16),
            pltpu.VMEM((256, D), BF16),
            pltpu.VMEM((256, 256), F32),
            pltpu.VMEM((ROWS * COLS, FIELDS, D), BF16),
            pltpu.VMEM((HEADS, 2 * OWN, D), BF16),
            pltpu.VMEM((16, D), F32),
            pltpu.VMEM((8, 80, 128), F32),
            pltpu.VMEM((8, 80, 128), BF16),
            pltpu.VMEM((8, 80, 128), BF16),
            pltpu.VMEM((ROWS, 16, 256), F32),
            pltpu.VMEM((2, OWN, D), BF16),
            pltpu.VMEM((2, OWN, D), BF16),
            pltpu.VMEM((48, D), BF16),
            pltpu.VMEM((48, D), BF16),
            pltpu.VMEM((OWN, D), BF16),
            pltpu.VMEM((2, OWN, D), BF16),
            pltpu.VMEM((2, OWN, D), BF16),
            pltpu.VMEM((2, OWN, D), BF16),
            pltpu.VMEM((48, D), BF16),
            pltpu.VMEM((OWN, D), BF16),
            pltpu.SemaphoreType.DMA((5,)),
            pltpu.SemaphoreType.DMA((8,)),
            pltpu.SemaphoreType.DMA((8,)),
            pltpu.SemaphoreType.DMA((2, CHUNKS)),
            pltpu.SemaphoreType.DMA((2, CHUNKS)),
            pltpu.SemaphoreType.DMA((2, 2, CHUNKS)),
            pltpu.SemaphoreType.DMA((2, 2, CHUNKS)),
            pltpu.SemaphoreType.DMA((3,)),
            pltpu.SemaphoreType.DMA((3,)),
            pltpu.VMEM((OWN, D), BF16),
            pltpu.VMEM((OWN, D), BF16),
            pltpu.SemaphoreType.DMA((2, CHUNKS)),
            pltpu.SemaphoreType.DMA((2, CHUNKS)),
        ],
        compiler_params=pltpu.CompilerParams(
            vmem_limit_bytes=63 << 20, collective_id=0, has_side_effects=True
        ),
        name="whole",
    )(
        field_ids, lon_shift, row_window, fields, lat_query, embed_w, perc_wk, perc_wv, swin_qkv, swin_wo
    )
    return jnp.transpose(encoded, (2, 0, 1, 3))


def solution(mesh):
    in_specs = (P("var", "lat", None), P(), P(), P(), P(), P(), P(), P(), P(), P())
    out_specs = P(None, "lat", "var", None)
    return jax.shard_map(shards, mesh=mesh, in_specs=in_specs, out_specs=out_specs, check_vma=False)
```

```python
import functools
import math

import jax
import jax.numpy as jnp
from jax import lax
from jax.experimental import pallas as pl
from jax.experimental.pallas import tpu as pltpu
from jax.sharding import PartitionSpec as P

D = 512
HEADS = 16
HEAD = 32
LEVELS = 4
PATCH = 4
WIN_LAT = 6
WIN_LON = 12
FIELDS = 64
ROWS = 6
COLS = 12
PIX = PATCH * PATCH
GROUP = 4
QUADS = COLS // GROUP
LINE = 2 * COLS
OWN = ROWS * LINE
HALO = 128
KEYS = 384
EDGE = 120

EPSILON = 1e-05
MASKED = -1e30
EXP2_SCALE = math.log2(math.e) / math.sqrt(HEAD)
F32 = jnp.float32
BF16 = jnp.bfloat16
NT = (((1,), (1,)), ((), ()))
MESH = pl.DeviceIdType.MESH
SEND_ORDER = (4, 3, 5, 2, 6, 1, 7)
CHUNKS = 3
EMBED_STEP = 6
MERGE_STEP = 6
NEAR = 128
CHUNK = 2 * LINE
UP_PARTS = ((0, 48), (48, 48), (96, 32))
DOWN_PARTS = ((16, 32), (48, 48), (96, 48))


def dot(a, b):
    return jnp.dot(a, b, preferred_element_type=F32)


def iota(shape, dim):
    return lax.broadcasted_iota(jnp.int32, shape, dim)


def layer_norm(values):
    row_mean = jnp.sum(values, axis=-1, keepdims=True) * (1.0 / D)
    centred = values - row_mean
    variance = jnp.sum(centred * centred, axis=-1, keepdims=True) * (1.0 / D)
    return centred * lax.rsqrt(variance + EPSILON)


def softmax_rows(scores):
    row_top = jnp.max(scores, axis=-1, keepdims=True)
    lifted = jnp.exp2(scores - row_top)
    return lifted * (1.0 / jnp.sum(lifted, axis=-1, keepdims=True))


def column_of(token):
    return (token % LINE) // 8 * GROUP + token % GROUP


def remote(src, dst, send_sem, recv_sem, **device):
    return pltpu.make_async_remote_copy(
        src_ref=src, dst_ref=dst, send_sem=send_sem, recv_sem=recv_sem,
        device_id=device, device_id_type=MESH,
    )


def start_copy(copy):
    copy.start()


def wait_received(copy):
    copy.wait_recv()


def wait_sent(copy):
    copy.wait_send()


def attention(queries, keys, values, bias):
    count, key_count = queries.shape[0], keys.shape[0]
    lane_head = iota((count, 256), 1) // HEAD
    halves = []
    for half in range(2):
        cut = slice(256 * half, 256 * half + 256)
        part = queries[:, cut]
        stacked = jnp.concatenate(
            [jnp.where(lane_head == h, part, 0.0).astype(BF16) for h in range(8)], axis=0
        )
        scores = lax.dot_general(stacked, keys[:, cut], NT, preferred_element_type=F32)
        scores = scores.reshape(8, count, key_count) * EXP2_SCALE + bias[None]
        weights = softmax_rows(scores).astype(BF16).reshape(8 * count, key_count)
        mixed = dot(weights, values[:, cut]).reshape(8, count, 256)
        total = jnp.zeros((count, 256), F32)
        for h in range(8):
            total = jnp.where(lane_head == h, mixed[h], total)
        halves.append(total.astype(BF16))
    return jnp.concatenate(halves, axis=-1)


def heads_apart(queries):
    lane_head = iota(queries.shape, 1) // HEAD
    return jnp.concatenate(
        [jnp.where(lane_head == h, queries, 0.0).astype(BF16) for h in range(8)], axis=0
    )


def heads_together(stacked):
    lane_head = iota((stacked.shape[1], 256), 1) // HEAD
    total = jnp.broadcast_to(stacked[0], lane_head.shape)
    for h in range(1, 8):
        total = jnp.where(lane_head == h, stacked[h], total)
    return total


def attend_near(queries, keys, values, bias):
    count, key_count = bias.shape
    state = []
    for half in range(2):
        cut = slice(256 * half, 256 * half + 256)
        scores = lax.dot_general(
            heads_apart(queries[:, cut]), keys[:, cut], NT, preferred_element_type=F32
        )
        scores = scores.reshape(8, count, key_count) * EXP2_SCALE + bias[None]
        top = jnp.max(scores, axis=-1, keepdims=True)
        lifted = jnp.exp2(scores - top)
        total = jnp.sum(lifted, axis=-1, keepdims=True)
        mixed = dot(lifted.astype(BF16).reshape(8 * count, key_count), values[:, cut])
        state.append((top, total, heads_together(mixed.reshape(8, count, 256))))
    return state


def attend_far(queries, keys, values, bias, state):
    count, key_count = bias.shape
    halves = []
    for half, (near_top, near_total, near_mixed) in enumerate(state):
        cut = slice(256 * half, 256 * half + 256)
        scores = lax.dot_general(
            heads_apart(queries[:, cut]), keys[:, cut], NT, preferred_element_type=F32
        )
        scores = scores.reshape(8, count, key_count) * EXP2_SCALE + bias[None]
        top = jnp.maximum(near_top, jnp.max(scores, axis=-1, keepdims=True))
        lifted = jnp.exp2(scores - top)
        near_scale = jnp.exp2(near_top - top)
        total = near_scale * near_total + jnp.sum(lifted, axis=-1, keepdims=True)
        inverse = 1.0 / total
        mixed = dot(
            (lifted * inverse).astype(BF16).reshape(8 * count, key_count), values[:, cut]
        )
        mixed = heads_together(mixed.reshape(8, count, 256))
        mixed = mixed + near_mixed * heads_together(near_scale * inverse)
        halves.append(mixed.astype(BF16))
    return jnp.concatenate(halves, axis=-1)


def pick_pixels(fields, stage, send):
    flat = fields.astype(F32).reshape(8 * ROWS * PATCH, 384).astype(BF16)
    row = iota((512, 1), 0)
    column = row % 16
    source = jnp.where(column < COLS, (row % 128) // 16 * 48 + column * PATCH + row // 128, -1)
    pick = jnp.where(source == iota((512, 384), 1), 1.0, 0.0).astype(BF16)
    turned = lax.dot_general(pick, flat, NT, preferred_element_type=F32).astype(BF16)
    row = iota((192, 1), 0)
    target = (row // PATCH) % ROWS * 128 + row // (ROWS * PATCH) * PIX + row % PATCH * PATCH
    lane = iota((192, 768), 1)
    total = jnp.zeros((128, 768), F32)
    for j in range(PATCH):
        place = jnp.where(target + j == lane, 1.0, 0.0).astype(BF16)
        total = total + dot(turned[128 * j : 128 * j + 128], place)
    for sector in range(8):
        stage[sector, 72:80, :] = jnp.zeros((8, 128), F32)
        for line in range(ROWS):
            stage[sector, COLS * line : COLS * line + COLS, :] = total[
                16 * sector : 16 * sector + COLS, 128 * line : 128 * line + 128
            ]
    send[...] = stage[...].astype(BF16)


def prepare_weights(ids_ref, shift_ref, embed, query_ref, wk, slot_w, keys_scr, bias_scr, query_scr):
    def place(slot, carry):
        start = pl.multiple_of(slot * PIX, PIX)
        slot_w[pl.ds(start, PIX), :] = embed[ids_ref[slot]]
        return carry

    lax.fori_loop(0, FIELDS, place, 0)
    swap = shift_ref[1] > shift_ref[0]
    query = query_ref[...].astype(F32)
    swapped = jnp.concatenate([query[2:], query[:2]], axis=0)
    query = jnp.where(swap, swapped, query)
    level = (iota((256, D), 0) // GROUP) % LEVELS
    spread = jnp.zeros((256, D), F32)
    for lev in range(LEVELS):
        spread = jnp.where(level == lev, query[lev : lev + 1, :], spread)
    query_scr[...] = spread[:16]
    own_head = iota((256, D), 1) // HEAD == iota((256, D), 0) // 16
    masked = jnp.where(own_head, spread, 0.0).astype(BF16)
    keys_scr[...] = lax.dot_general(
        masked, wk[...], NT, preferred_element_type=F32
    ).astype(BF16)
    same = iota((256, 256), 1) // FIELDS == iota((256, 256), 0) % GROUP
    bias_scr[...] = jnp.where(same, 0.0, MASKED)


def embed_line(line, part, line_pixels, slot_w, normed_scr):
    own_slot = iota((1, 16, 256), 2) // PIX == iota((1, 16, 256), 1)
    pixels = line_pixels[line][:COLS]
    spread = jnp.where(own_slot, pixels[:, None, :], 0.0).astype(BF16)
    weight = slot_w[pl.ds(pl.multiple_of(256 * part, 256), 256), :]
    tokens = dot(spread.reshape(COLS * 16, 256), weight)
    normed = layer_norm(tokens.astype(BF16).astype(F32)).astype(BF16)
    slots = pl.ds(pl.multiple_of(16 * part, 16), 16)
    normed_scr[pl.ds(line * COLS, COLS), slots, :] = normed.reshape(COLS, 16, D)


def merge_quad(quad, keys_scr, bias_scr, normed_scr, pooled_scr):
    normed = normed_scr[pl.ds(quad * GROUP, GROUP)].reshape(GROUP * FIELDS, D)
    scores = lax.dot_general(keys_scr[...], normed, NT, preferred_element_type=F32)
    weights = softmax_rows(scores * EXP2_SCALE + bias_scr[...]).astype(BF16)
    pooled = dot(weights, normed).astype(BF16)
    start = pl.multiple_of(quad * 16, 16)
    pooled_scr[:, pl.ds(start, 16), :] = pooled.reshape(HEADS, 16, D)


def project(chunk, pooled_scr, wv, query_scr):
    start = pl.multiple_of(chunk * 2 * CHUNK, 2 * CHUNK)
    halves = []
    for half in range(2):
        lane_head = iota((D, 256), 1) // HEAD
        value_w = wv[:, 256 * half : 256 * half + 256].astype(F32)
        total = jnp.zeros((2 * CHUNK, 256), F32)
        for head in range(8):
            masked = jnp.where(lane_head == head, value_w, 0.0).astype(BF16)
            total = total + dot(pooled_scr[8 * half + head, pl.ds(start, 2 * CHUNK), :], masked)
        halves.append(total)
    projected = jnp.concatenate(halves, axis=-1).reshape(2 * QUADS, 16, D)
    return projected + query_scr[...][None]


def quads_of(tokens, last):
    width = tokens.shape[-1]
    tokens = tokens.reshape(tokens.shape[0] // 8, 8, width)
    picked = [q for q in range(tokens.shape[0]) if (q % QUADS == QUADS - 1) == last]
    return jnp.concatenate([tokens[q] for q in picked], axis=0)


def with_last_column(rest, own, received):
    is_last = iota(own.shape, 0) % GROUP == GROUP - 1
    last = jnp.where(is_last, received, own)
    pieces = []
    for r in range(own.shape[0] // 8):
        pieces += [rest[16 * r : 16 * r + 16], last[8 * r : 8 * r + 8]]
    return jnp.concatenate(pieces, axis=0)


def whole_kernel(
    ids_ref, shift_ref, window_ref, fields_ref, query_ref, embed_h, wk_h, wv_h, qkv_h, wo_h, out_ref,
    embed, wk, wv, qkv, wo, slot_w, keys_scr, bias_scr, normed_scr, pooled_scr, query_scr,
    stage, send, recv, line_pixels, latents, slab, edge_send, edge_recv, col_recv, up_recv, down_recv,
    encoded, back_edge_recv, back_recv,
    load_sem, pix_send_sem, pix_recv_sem, col_send_sem, col_recv_sem, row_send_sem, row_recv_sem,
    back_send_sem, back_recv_sem, extra_up, extra_down, extra_send_sem, extra_recv_sem,
):
    sector = lax.axis_index("var")
    sectors = lax.axis_size("var")
    band = lax.axis_index("lat")
    bands = lax.axis_size("lat")
    right = lax.rem(sector + 1, sectors)
    left = lax.rem(sector + sectors - 1, sectors)
    is_first = sector == 0
    is_last = sector == sectors - 1
    is_end = is_first | is_last
    has_left = jnp.logical_not(is_first)
    has_right = jnp.logical_not(is_last)
    has_up = band > 0
    has_down = band < bands - 1

    barrier = pltpu.get_barrier_semaphore()
    for k in range(1, sectors):
        pl.semaphore_signal(
            barrier, inc=1, device_id={"var": lax.rem(sector + k, sectors)}, device_id_type=MESH
        )

    @pl.when(has_up)
    def _():
        pl.semaphore_signal(barrier, inc=1, device_id={"lat": band - 1}, device_id_type=MESH)

    @pl.when(has_down)
    def _():
        pl.semaphore_signal(barrier, inc=1, device_id={"lat": band + 1}, device_id_type=MESH)

    loads = [
        pltpu.make_async_copy(src, dst, load_sem.at[i])
        for i, (src, dst) in enumerate(
            [(embed_h, embed), (wk_h, wk), (wv_h, wv), (qkv_h, qkv), (wo_h, wo)]
        )
    ]
    for load in loads:
        load.start()

    pick_pixels(fields_ref[...], stage, send)

    @pl.when(jnp.logical_not(has_up))
    def _():
        up_recv[...] = jnp.zeros_like(up_recv)

    @pl.when(jnp.logical_not(has_down))
    def _():
        down_recv[...] = jnp.zeros_like(down_recv)

    @pl.when((band == 0) & is_end)
    def _():
        extra_up[...] = jnp.zeros_like(extra_up)

    @pl.when((band == bands - 1) & is_end)
    def _():
        extra_down[...] = jnp.zeros_like(extra_down)

    @pl.when(is_first)
    def _():
        edge_recv[...] = jnp.zeros_like(edge_recv)

    @pl.when(is_last)
    def _():
        col_recv[...] = jnp.zeros_like(col_recv)

    neighbours = jnp.where(has_up, 1, 0) + jnp.where(has_down, 1, 0)
    pl.semaphore_wait(barrier, sectors - 1 + neighbours)

    def pixel_copy(k, peer, slot):
        return remote(
            send.at[peer], recv.at[slot], pix_send_sem.at[k], pix_recv_sem.at[k], var=peer
        )

    for k in SEND_ORDER:
        pixel_copy(k, lax.rem(sector + k, sectors), sector).start()
    recv[sector] = send[sector]

    loads[0].wait()
    loads[1].wait()
    prepare_weights(
        ids_ref, shift_ref, embed, query_ref, wk, slot_w, keys_scr, bias_scr, query_scr
    )

    def one_part(turn, carry):
        own = sector // 2
        part = lax.rem(own // 2 + turn // 2, 2) * 2 + lax.rem(own % 2 + turn % 2, 2)
        for side in range(2):
            source = part * 2 + side

            @pl.when(source != sector)
            def _():
                pixel_copy(lax.rem(sector + sectors - source, sectors), source, source).wait_recv()

            stage[side] = recv[source].astype(F32)
            for line in range(ROWS):
                line_pixels[line, 0:COLS, 128 * side : 128 * side + 128] = stage[
                    side, COLS * line : COLS * line + COLS, :
                ]

        def lines(step, carry):
            for k in range(EMBED_STEP):
                embed_line(step * EMBED_STEP + k, part, line_pixels, slot_w, normed_scr)
            return carry

        lax.fori_loop(0, ROWS // EMBED_STEP, lines, 0)
        return carry

    lax.fori_loop(0, 4, one_part, 0)

    shift = jnp.minimum(shift_ref[0], shift_ref[1])

    def column_copies(chunk):
        quads = pl.ds(pl.multiple_of(chunk * 16, 16), 16)
        tokens = pl.ds(pl.multiple_of(chunk * CHUNK, 16), CHUNK)
        return (
            remote(
                edge_send.at[quads], edge_recv.at[quads],
                col_send_sem.at[0, chunk], col_recv_sem.at[0, chunk], var=right,
            ),
            remote(
                latents.at[1, tokens], col_recv.at[tokens],
                col_send_sem.at[1, chunk], col_recv_sem.at[1, chunk], var=left,
            ),
        )

    def extra_copies(chunk):
        quads = pl.ds(pl.multiple_of(chunk * 16, 16), 16)
        tokens = pl.ds(pl.multiple_of(chunk * CHUNK, 16), CHUNK)
        copies = []
        for end, src, part in ((is_first, latents.at[1, tokens], tokens), (is_last, edge_send.at[quads], quads)):
            copies.append((end & has_up, remote(
                src, extra_down.at[part], extra_send_sem.at[0, chunk], extra_recv_sem.at[0, chunk], lat=band - 1
            )))
            copies.append((end & has_down, remote(
                src, extra_up.at[part], extra_send_sem.at[1, chunk], extra_recv_sem.at[1, chunk], lat=band + 1
            )))
        return copies

    def take_extra():
        for chunk in range(CHUNKS):
            for i, (_, copy) in enumerate(extra_copies(chunk)):
                end = is_first if i < 2 else is_last
                pl.when(end & (has_down if i % 2 == 0 else has_up))(functools.partial(wait_received, copy))

    def row_copies(pair, chunk):
        (up_start, up_count), (down_start, down_count) = UP_PARTS[chunk], DOWN_PARTS[chunk]
        up_part, down_part = pl.ds(up_start, up_count), pl.ds(down_start, down_count)
        upward = remote(
            slab.at[pair, up_part], down_recv.at[pair, up_part],
            row_send_sem.at[pair, 0, chunk], row_recv_sem.at[pair, 0, chunk], lat=band - 1,
        )
        downward = remote(
            slab.at[pair, down_part], up_recv.at[pair, down_part],
            row_send_sem.at[pair, 1, chunk], row_recv_sem.at[pair, 1, chunk], lat=band + 1,
        )
        return upward, downward

    def send_rows(pair, chunk):
        upward, downward = row_copies(pair, chunk)

        @pl.when(has_up)
        def _():
            upward.start()

        @pl.when(has_down)
        def _():
            downward.start()

    def take_rows(pair):
        for chunk in range(CHUNKS):
            upward, downward = row_copies(pair, chunk)

            @pl.when(has_down)
            def _():
                upward.wait_recv()

            @pl.when(has_up)
            def _():
                downward.wait_recv()

    def share_rows(chunk):
        edge_copy, col_copy = column_copies(chunk)
        tokens = slice(CHUNK * chunk, CHUNK * chunk + CHUNK)
        quads = slice(16 * chunk, 16 * chunk + 16)
        pl.when(has_right)(lambda: wait_received(col_copy))
        column = column_of(iota((CHUNK, D), 0))
        slab[1, tokens] = jnp.where(
            column < shift, col_recv[tokens].astype(F32), latents[1, tokens].astype(F32)
        ).astype(BF16)
        send_rows(1, chunk)
        pl.when(has_left)(lambda: wait_received(edge_copy))
        own = latents[0, tokens].astype(F32)
        slab[0, tokens] = with_last_column(
            quads_of(own, False), quads_of(own, True), edge_recv[quads].astype(F32)
        ).astype(BF16)
        send_rows(0, chunk)

    loads[2].wait()

    def one_chunk(chunk, carry):
        def quads(step, carry):
            for k in range(MERGE_STEP):
                quad = chunk * 2 * QUADS + step * MERGE_STEP + k
                merge_quad(quad, keys_scr, bias_scr, normed_scr, pooled_scr)
            return carry

        lax.fori_loop(0, 2 * QUADS // MERGE_STEP, quads, 0)
        fresh = project(chunk, pooled_scr, wv, query_scr)
        start = pl.multiple_of(chunk * CHUNK, 16)
        for pair in range(2):
            tokens = fresh[:, 8 * pair : 8 * pair + 8].reshape(CHUNK, D)
            latents[pair, pl.ds(start, CHUNK), :] = tokens.astype(BF16)
            if pair == 0:
                quads = pl.ds(pl.multiple_of(chunk * 16, 16), 16)
                edge_send[quads, :] = quads_of(tokens, True).astype(BF16)
        edge_copy, col_copy = column_copies(chunk)
        pl.when(has_right)(lambda: start_copy(edge_copy))
        pl.when(has_left)(lambda: start_copy(col_copy))
        for where, copy in extra_copies(chunk):
            pl.when(where)(functools.partial(start_copy, copy))
        for ready in range(CHUNKS - 1):
            @pl.when(chunk == ready + 1)
            def _():
                share_rows(ready)

        return carry

    lax.fori_loop(0, CHUNKS, one_chunk, 0)
    share_rows(CHUNKS - 1)

    first = band * ROWS - (WIN_LAT - 1)
    total_rows = window_ref.shape[0]

    def row_ident(k):
        row = first + k
        inside = (row >= 0) & (row < total_rows)
        return jnp.where(inside, window_ref[jnp.clip(row, 0, total_rows - 1)], -1)

    key_token = iota((1, KEYS), 1)
    query_token = iota((OWN, 1), 0)
    key_row = jnp.full((1, KEYS), -1, jnp.int32)
    query_row = jnp.full((OWN, 1), -1, jnp.int32)
    for k in range(ROWS + 2 * (WIN_LAT - 1)):
        ident = row_ident(k)
        key_row = jnp.where(key_token // LINE == k, ident, key_row)
        if 0 <= k - (WIN_LAT - 1) < ROWS:
            query_row = jnp.where(query_token // LINE == k - (WIN_LAT - 1), ident, query_row)

    loads[3].wait()
    loads[4].wait()
    def around(own_part, halo_part):
        edge = halo_part.shape[0] // 2
        return jnp.concatenate([halo_part[:edge], own_part, halo_part[edge:]], axis=0).astype(BF16)

    def attend_extra(own, up, down, same):
        own_qkv = dot(layer_norm(own).astype(BF16), qkv[...])
        halo = jnp.concatenate([up.astype(F32), down.astype(F32)], axis=0)
        halo = dot(layer_norm(halo).astype(BF16), qkv[:, D:])
        keys = around(own_qkv[:, D : 2 * D], halo[:, :D])
        values = around(own_qkv[:, 2 * D :], halo[:, D:])
        mixed = attention(own_qkv[:, :D], keys, values, jnp.where(same, 0.0, MASKED))
        return (own + dot(mixed, wo[...])).astype(BF16)

    def window_bias(pair):
        def wrapped(token):
            if pair == 0:
                return jnp.where((column_of(token) == COLS - 1) & (sector == 0), 1, 0)
            return jnp.where((column_of(token) < shift) & (sector == sectors - 1), 1, 0)

        same = (query_row * 2 + wrapped(query_token)) == (key_row * 2 + wrapped(key_token))
        return jnp.where(same, 0.0, MASKED)

    near = {}
    for pair in (1, 0):
        own = slab[pair].astype(F32)
        own_qkv = dot(layer_norm(own).astype(BF16), qkv[...])
        queries, keys, values = own_qkv[:, :D], own_qkv[:, D : 2 * D], own_qkv[:, 2 * D :]
        bias = window_bias(pair)
        state = attend_near(
            queries, keys[:NEAR].astype(BF16), values[:NEAR].astype(BF16), bias[:, EDGE : EDGE + NEAR]
        )
        near[pair] = own, queries, keys[NEAR:], values[NEAR:], state

    take_extra()

    @pl.when(is_first)
    def _():
        below = [jnp.where(column_of(token) < shift, 1, 0) for token in (query_token, key_token)]
        same = (query_row * 2 + below[0]) == (key_row * 2 + below[1])
        back_recv[...] = attend_extra(
            latents[1].astype(F32), extra_up[OWN - EDGE :], extra_down[:EDGE], same
        )

    @pl.when(is_last)
    def _():
        ident = [jnp.full((48, 1), -1, jnp.int32), jnp.full((1, 128), -1, jnp.int32)]
        token = [iota((48, 1), 0), iota((1, 128), 1)]
        for k in range(ROWS + 2 * (WIN_LAT - 1)):
            ident[1] = jnp.where(token[1] // 8 == k, row_ident(k), ident[1])
            ident[0] = jnp.where(token[0] // 8 == k - (WIN_LAT - 1), row_ident(k), ident[0])
        side = [jnp.where(t % GROUP == GROUP - 1, 1, 0) for t in token]
        same = (ident[0] * 2 + side[0]) == (ident[1] * 2 + side[1])
        back_edge_recv[...] = attend_extra(
            edge_send[...].astype(F32), extra_up[0:48].astype(F32)[8:], extra_down[0:48].astype(F32)[:40], same
        )

    def attend_window(pair):
        own, queries, keys, values, state = near[pair]
        take_rows(pair)
        halo = jnp.concatenate(
            [up_recv[pair].astype(F32)[OWN - EDGE :], down_recv[pair].astype(F32)[:EDGE]], axis=0
        )
        halo = dot(layer_norm(halo).astype(BF16), qkv[:, D:])
        keys, values = around(keys, halo[:, :D]), around(values, halo[:, D:])
        far_token = iota((1, 2 * EDGE + OWN - NEAR), 1)
        far_token = jnp.where(far_token < EDGE, far_token, far_token + NEAR)
        far_row = jnp.full(far_token.shape, -1, jnp.int32)
        for k in range(ROWS + 2 * (WIN_LAT - 1)):
            far_row = jnp.where(far_token // LINE == k, row_ident(k), far_row)

        def wrapped(token):
            if pair == 0:
                return jnp.where((column_of(token) == COLS - 1) & (sector == 0), 1, 0)
            return jnp.where((column_of(token) < shift) & (sector == sectors - 1), 1, 0)

        same = (query_row * 2 + wrapped(query_token)) == (far_row * 2 + wrapped(far_token))
        mixed = attend_far(queries, keys, values, jnp.where(same, 0.0, MASKED), state)
        return own + dot(mixed, wo[...])

    backs = []
    encoded[1] = attend_window(1).astype(BF16)
    back = remote(encoded.at[1], back_recv, back_send_sem.at[0], back_recv_sem.at[0], var=right)
    pl.when(has_right)(functools.partial(start_copy, back))
    backs.append(back)
    done = attend_window(0)
    encoded[0, 0:48] = quads_of(done, True).astype(BF16)
    back = remote(
        encoded.at[0, pl.ds(0, 48)], back_edge_recv, back_send_sem.at[1], back_recv_sem.at[1], var=left
    )
    pl.when(has_left)(functools.partial(start_copy, back))
    backs.append(back)
    first_rest = quads_of(done, False)

    swap = jnp.where(shift_ref[1] > shift_ref[0], 1, 0)
    row = iota((2 * OWN, OWN), 0)
    level = row % LEVELS
    place = row // 48 * LINE + row % 48 // 16 * 8 + level % 2 * GROUP + row % 16 // LEVELS
    hit = place == iota((2 * OWN, OWN), 1)
    orders = [
        jnp.where(hit & (level // 2 == (swap if pair == 0 else 1 - swap)), 1.0, 0.0).astype(BF16)
        for pair in range(2)
    ]
    pl.when(has_right)(lambda: wait_received(backs[1]))
    first_pair = with_last_column(
        first_rest, encoded[0, 0:48].astype(F32), back_edge_recv[...].astype(F32)
    )
    result = dot(orders[0], first_pair.astype(BF16))
    pl.when(has_left)(lambda: wait_received(backs[0]))
    column = column_of(iota((OWN, D), 0))
    second_pair = jnp.where(column < shift, back_recv[...].astype(F32), encoded[1].astype(F32))
    result = result + dot(orders[1], second_pair.astype(BF16))
    out_ref[...] = result.reshape(ROWS, COLS, LEVELS, D).astype(BF16)

    for k in range(1, sectors):
        pixel_copy(k, lax.rem(sector + k, sectors), sector).wait_send()
    for chunk in range(CHUNKS):
        edge_copy, col_copy = column_copies(chunk)
        pl.when(has_right)(functools.partial(wait_sent, edge_copy))
        pl.when(has_left)(functools.partial(wait_sent, col_copy))
        for where, copy in extra_copies(chunk):
            pl.when(where)(functools.partial(wait_sent, copy))
        for pair in range(2):
            upward, downward = row_copies(pair, chunk)

            @pl.when(has_up)
            def _():
                upward.wait_send()

            @pl.when(has_down)
            def _():
                downward.wait_send()

    for back, where in zip(backs, (has_right, has_left)):
        pl.when(where)(functools.partial(wait_sent, back))


def shards(
    fields, field_ids, embed_w, lat_query, perc_wk, perc_wv, swin_qkv, swin_wo, row_window, lon_shift
):
    vmem = pl.BlockSpec(memory_space=pltpu.VMEM)
    smem = pl.BlockSpec(memory_space=pltpu.SMEM)
    hbm = pl.BlockSpec(memory_space=pl.ANY)
    encoded = pl.pallas_call(
        whole_kernel,
        out_shape=jax.ShapeDtypeStruct((ROWS, COLS, LEVELS, D), BF16),
        in_specs=[smem] * 3 + [vmem] * 2 + [hbm] * 5,
        out_specs=vmem,
        scratch_shapes=[
            pltpu.VMEM((FIELDS, PIX, D), BF16),
            pltpu.VMEM((D, D), BF16),
            pltpu.VMEM((D, D), BF16),
            pltpu.VMEM((D, 3 * D), BF16),
            pltpu.VMEM((D, D), BF16),
            pltpu.VMEM((FIELDS * PIX, D), BF16),
            pltpu.VMEM((256, D), BF16),
            pltpu.VMEM((256, 256), F32),
            pltpu.VMEM((ROWS * COLS, FIELDS, D), BF16),
            pltpu.VMEM((HEADS, 2 * OWN, D), BF16),
            pltpu.VMEM((16, D), F32),
            pltpu.VMEM((8, 80, 128), F32),
            pltpu.VMEM((8, 80, 128), BF16),
            pltpu.VMEM((8, 80, 128), BF16),
            pltpu.VMEM((ROWS, 16, 256), F32),
            pltpu.VMEM((2, OWN, D), BF16),
            pltpu.VMEM((2, OWN, D), BF16),
            pltpu.VMEM((48, D), BF16),
            pltpu.VMEM((48, D), BF16),
            pltpu.VMEM((OWN, D), BF16),
            pltpu.VMEM((2, OWN, D), BF16),
            pltpu.VMEM((2, OWN, D), BF16),
            pltpu.VMEM((2, OWN, D), BF16),
            pltpu.VMEM((48, D), BF16),
            pltpu.VMEM((OWN, D), BF16),
            pltpu.SemaphoreType.DMA((5,)),
            pltpu.SemaphoreType.DMA((8,)),
            pltpu.SemaphoreType.DMA((8,)),
            pltpu.SemaphoreType.DMA((2, CHUNKS)),
            pltpu.SemaphoreType.DMA((2, CHUNKS)),
            pltpu.SemaphoreType.DMA((2, 2, CHUNKS)),
            pltpu.SemaphoreType.DMA((2, 2, CHUNKS)),
            pltpu.SemaphoreType.DMA((2,)),
            pltpu.SemaphoreType.DMA((2,)),
            pltpu.VMEM((OWN, D), BF16),
            pltpu.VMEM((OWN, D), BF16),
            pltpu.SemaphoreType.DMA((2, CHUNKS)),
            pltpu.SemaphoreType.DMA((2, CHUNKS)),
        ],
        compiler_params=pltpu.CompilerParams(
            vmem_limit_bytes=63 << 20, collective_id=0, has_side_effects=True
        ),
        name="whole",
    )(
        field_ids, lon_shift, row_window, fields, lat_query, embed_w, perc_wk, perc_wv, swin_qkv, swin_wo
    )
    return jnp.transpose(encoded, (2, 0, 1, 3))


def solution(mesh):
    in_specs = (P("var", "lat", None), P(), P(), P(), P(), P(), P(), P(), P(), P())
    out_specs = P(None, "lat", "var", None)
    return jax.shard_map(shards, mesh=mesh, in_specs=in_specs, out_specs=out_specs, check_vma=False)
```

```python
import functools
import math

import jax
import jax.numpy as jnp
from jax import lax
from jax.experimental import pallas as pl
from jax.experimental.pallas import tpu as pltpu
from jax.sharding import PartitionSpec as P

D = 512
HEADS = 16
HEAD = 32
LEVELS = 4
PATCH = 4
WIN_LAT = 6
WIN_LON = 12
FIELDS = 64
ROWS = 6
COLS = 12
PIX = PATCH * PATCH
GROUP = 4
QUADS = COLS // GROUP
LINE = 2 * COLS
OWN = ROWS * LINE
HALO = 128
KEYS = 384
EDGE = 120

EPSILON = 1e-05
MASKED = -1e30
EXP2_SCALE = math.log2(math.e) / math.sqrt(HEAD)
F32 = jnp.float32
BF16 = jnp.bfloat16
NT = (((1,), (1,)), ((), ()))
MESH = pl.DeviceIdType.MESH
SEND_ORDER = (4, 3, 5, 2, 6, 1, 7)
CHUNKS = 3
EMBED_STEP = 6
MERGE_STEP = 6
NEAR = 128
CHUNK = 2 * LINE
UP_PARTS = ((0, 48), (48, 48), (96, 32))
DOWN_PARTS = ((16, 32), (48, 48), (96, 48))


def dot(a, b):
    return jnp.dot(a, b, preferred_element_type=F32)


def iota(shape, dim):
    return lax.broadcasted_iota(jnp.int32, shape, dim)


def layer_norm(values):
    row_mean = jnp.sum(values, axis=-1, keepdims=True) * (1.0 / D)
    centred = values - row_mean
    variance = jnp.sum(centred * centred, axis=-1, keepdims=True) * (1.0 / D)
    return centred * lax.rsqrt(variance + EPSILON)


def softmax_rows(scores):
    row_top = jnp.max(scores, axis=-1, keepdims=True)
    lifted = jnp.exp2(scores - row_top)
    return lifted * (1.0 / jnp.sum(lifted, axis=-1, keepdims=True))


def column_of(token):
    return (token % LINE) // 8 * GROUP + token % GROUP


def remote(src, dst, send_sem, recv_sem, **device):
    return pltpu.make_async_remote_copy(
        src_ref=src, dst_ref=dst, send_sem=send_sem, recv_sem=recv_sem,
        device_id=device, device_id_type=MESH,
    )


def start_copy(copy):
    copy.start()


def wait_received(copy):
    copy.wait_recv()


def wait_sent(copy):
    copy.wait_send()


def attention(queries, keys, values, bias):
    count, key_count = queries.shape[0], keys.shape[0]
    lane_head = iota((count, 256), 1) // HEAD
    halves = []
    for half in range(2):
        cut = slice(256 * half, 256 * half + 256)
        part = queries[:, cut]
        stacked = jnp.concatenate(
            [jnp.where(lane_head == h, part, 0.0).astype(BF16) for h in range(8)], axis=0
        )
        scores = lax.dot_general(stacked, keys[:, cut], NT, preferred_element_type=F32)
        scores = scores.reshape(8, count, key_count) * EXP2_SCALE + bias[None]
        weights = softmax_rows(scores).astype(BF16).reshape(8 * count, key_count)
        mixed = dot(weights, values[:, cut]).reshape(8, count, 256)
        total = jnp.zeros((count, 256), F32)
        for h in range(8):
            total = jnp.where(lane_head == h, mixed[h], total)
        halves.append(total.astype(BF16))
    return jnp.concatenate(halves, axis=-1)


def split_values(wv, value_scr):
    lane_head = iota((D, 256), 1) // HEAD
    for half in range(2):
        value_w = wv[:, 256 * half : 256 * half + 256].astype(F32)
        for head in range(8):
            value_scr[8 * half + head] = jnp.where(lane_head == head, value_w, 0.0).astype(BF16)


def heads_apart(queries):
    lane_head = iota(queries.shape, 1) // HEAD
    return jnp.concatenate(
        [jnp.where(lane_head == h, queries, 0.0).astype(BF16) for h in range(8)], axis=0
    )


def heads_together(stacked):
    lane_head = iota((stacked.shape[1], 256), 1) // HEAD
    total = jnp.broadcast_to(stacked[0], lane_head.shape)
    for h in range(1, 8):
        total = jnp.where(lane_head == h, stacked[h], total)
    return total


def attend_near(queries, keys, values, bias):
    count, key_count = bias.shape
    state = []
    for half in range(2):
        cut = slice(256 * half, 256 * half + 256)
        scores = lax.dot_general(
            heads_apart(queries[:, cut]), keys[:, cut], NT, preferred_element_type=F32
        )
        scores = scores.reshape(8, count, key_count) * EXP2_SCALE + bias[None]
        top = jnp.max(scores, axis=-1, keepdims=True)
        lifted = jnp.exp2(scores - top)
        total = jnp.sum(lifted, axis=-1, keepdims=True)
        mixed = dot(lifted.astype(BF16).reshape(8 * count, key_count), values[:, cut])
        state.append((top, total, heads_together(mixed.reshape(8, count, 256))))
    return state


def attend_far(queries, keys, values, bias, state):
    count, key_count = bias.shape
    halves = []
    for half, (near_top, near_total, near_mixed) in enumerate(state):
        cut = slice(256 * half, 256 * half + 256)
        scores = lax.dot_general(
            heads_apart(queries[:, cut]), keys[:, cut], NT, preferred_element_type=F32
        )
        scores = scores.reshape(8, count, key_count) * EXP2_SCALE + bias[None]
        top = jnp.maximum(near_top, jnp.max(scores, axis=-1, keepdims=True))
        lifted = jnp.exp2(scores - top)
        near_scale = jnp.exp2(near_top - top)
        total = near_scale * near_total + jnp.sum(lifted, axis=-1, keepdims=True)
        inverse = 1.0 / total
        mixed = dot(
            (lifted * inverse).astype(BF16).reshape(8 * count, key_count), values[:, cut]
        )
        mixed = heads_together(mixed.reshape(8, count, 256))
        mixed = mixed + near_mixed * heads_together(near_scale * inverse)
        halves.append(mixed.astype(BF16))
    return jnp.concatenate(halves, axis=-1)


def pick_pixels(fields, stage, send):
    flat = fields.astype(F32).reshape(8 * ROWS * PATCH, 384).astype(BF16)
    row = iota((512, 1), 0)
    column = row % 16
    source = jnp.where(column < COLS, (row % 128) // 16 * 48 + column * PATCH + row // 128, -1)
    pick = jnp.where(source == iota((512, 384), 1), 1.0, 0.0).astype(BF16)
    turned = lax.dot_general(pick, flat, NT, preferred_element_type=F32).astype(BF16)
    row = iota((192, 1), 0)
    target = (row // PATCH) % ROWS * 128 + row // (ROWS * PATCH) * PIX + row % PATCH * PATCH
    lane = iota((192, 768), 1)
    total = jnp.zeros((128, 768), F32)
    for j in range(PATCH):
        place = jnp.where(target + j == lane, 1.0, 0.0).astype(BF16)
        total = total + dot(turned[128 * j : 128 * j + 128], place)
    for sector in range(8):
        stage[sector, 72:80, :] = jnp.zeros((8, 128), F32)
        for line in range(ROWS):
            stage[sector, COLS * line : COLS * line + COLS, :] = total[
                16 * sector : 16 * sector + COLS, 128 * line : 128 * line + 128
            ]
    send[...] = stage[...].astype(BF16)


def prepare_weights(ids_ref, shift_ref, embed, query_ref, wk, slot_w, keys_scr, bias_scr, query_scr):
    def place(slot, carry):
        start = pl.multiple_of(slot * PIX, PIX)
        slot_w[pl.ds(start, PIX), :] = embed[ids_ref[slot]]
        return carry

    lax.fori_loop(0, FIELDS, place, 0)
    swap = shift_ref[1] > shift_ref[0]
    query = query_ref[...].astype(F32)
    swapped = jnp.concatenate([query[2:], query[:2]], axis=0)
    query = jnp.where(swap, swapped, query)
    level = (iota((256, D), 0) // GROUP) % LEVELS
    spread = jnp.zeros((256, D), F32)
    for lev in range(LEVELS):
        spread = jnp.where(level == lev, query[lev : lev + 1, :], spread)
    query_scr[...] = spread[:16]
    own_head = iota((256, D), 1) // HEAD == iota((256, D), 0) // 16
    masked = jnp.where(own_head, spread, 0.0).astype(BF16)
    keys_scr[...] = lax.dot_general(
        masked, wk[...], NT, preferred_element_type=F32
    ).astype(BF16)
    same = iota((256, 256), 1) // FIELDS == iota((256, 256), 0) % GROUP
    bias_scr[...] = jnp.where(same, 0.0, MASKED)


def embed_line(line, part, line_pixels, slot_w, normed_scr):
    own_slot = iota((1, 16, 256), 2) // PIX == iota((1, 16, 256), 1)
    pixels = line_pixels[line][:COLS]
    spread = jnp.where(own_slot, pixels[:, None, :], 0.0).astype(BF16)
    weight = slot_w[pl.ds(pl.multiple_of(256 * part, 256), 256), :]
    tokens = dot(spread.reshape(COLS * 16, 256), weight)
    normed = layer_norm(tokens).astype(BF16)
    slots = pl.ds(pl.multiple_of(16 * part, 16), 16)
    normed_scr[pl.ds(line * COLS, COLS), slots, :] = normed.reshape(COLS, 16, D)


def merge_quad(quad, keys_scr, bias_scr, normed_scr, pooled_scr):
    normed = normed_scr[pl.ds(quad * GROUP, GROUP)].reshape(GROUP * FIELDS, D)
    scores = lax.dot_general(keys_scr[...], normed, NT, preferred_element_type=F32)
    weights = softmax_rows(scores * EXP2_SCALE + bias_scr[...]).astype(BF16)
    pooled = dot(weights, normed).astype(BF16)
    start = pl.multiple_of(quad * 16, 16)
    pooled_scr[:, pl.ds(start, 16), :] = pooled.reshape(HEADS, 16, D)


def project(chunk, pooled_scr, value_scr, query_scr):
    start = pl.multiple_of(chunk * 2 * CHUNK, 2 * CHUNK)
    halves = []
    for half in range(2):
        total = jnp.zeros((2 * CHUNK, 256), F32)
        for head in range(8 * half, 8 * half + 8):
            total = total + dot(pooled_scr[head, pl.ds(start, 2 * CHUNK), :], value_scr[head])
        halves.append(total)
    projected = jnp.concatenate(halves, axis=-1).reshape(2 * QUADS, 16, D)
    return projected + query_scr[...][None]


def quads_of(tokens, last):
    width = tokens.shape[-1]
    tokens = tokens.reshape(tokens.shape[0] // 8, 8, width)
    picked = [q for q in range(tokens.shape[0]) if (q % QUADS == QUADS - 1) == last]
    return jnp.concatenate([tokens[q] for q in picked], axis=0)


def with_last_column(rest, own, received):
    is_last = iota(own.shape, 0) % GROUP == GROUP - 1
    last = jnp.where(is_last, received, own)
    pieces = []
    for r in range(own.shape[0] // 8):
        pieces += [rest[16 * r : 16 * r + 16], last[8 * r : 8 * r + 8]]
    return jnp.concatenate(pieces, axis=0)


def whole_kernel(
    ids_ref, shift_ref, window_ref, fields_ref, query_ref, embed_h, wk_h, wv_h, qkv_h, wo_h, out_ref,
    embed, wk, wv, qkv, wo, slot_w, keys_scr, bias_scr, normed_scr, pooled_scr, query_scr,
    stage, send, recv, line_pixels, latents, slab, edge_send, edge_recv, col_recv, up_recv, down_recv,
    encoded, back_edge_recv, back_recv,
    load_sem, pix_send_sem, pix_recv_sem, col_send_sem, col_recv_sem, row_send_sem, row_recv_sem,
    back_send_sem, back_recv_sem, extra_up, extra_down, extra_send_sem, extra_recv_sem,
    value_scr,
):
    sector = lax.axis_index("var")
    sectors = lax.axis_size("var")
    band = lax.axis_index("lat")
    bands = lax.axis_size("lat")
    right = lax.rem(sector + 1, sectors)
    left = lax.rem(sector + sectors - 1, sectors)
    is_first = sector == 0
    is_last = sector == sectors - 1
    is_end = is_first | is_last
    has_left = jnp.logical_not(is_first)
    has_right = jnp.logical_not(is_last)
    has_up = band > 0
    has_down = band < bands - 1

    barrier = pltpu.get_barrier_semaphore()
    for k in range(1, sectors):
        pl.semaphore_signal(
            barrier, inc=1, device_id={"var": lax.rem(sector + k, sectors)}, device_id_type=MESH
        )

    @pl.when(has_up)
    def _():
        pl.semaphore_signal(barrier, inc=1, device_id={"lat": band - 1}, device_id_type=MESH)

    @pl.when(has_down)
    def _():
        pl.semaphore_signal(barrier, inc=1, device_id={"lat": band + 1}, device_id_type=MESH)

    loads = [
        pltpu.make_async_copy(src, dst, load_sem.at[i])
        for i, (src, dst) in enumerate(
            [(embed_h, embed), (wk_h, wk), (wv_h, wv), (qkv_h, qkv), (wo_h, wo)]
        )
    ]
    for load in loads:
        load.start()

    pick_pixels(fields_ref[...], stage, send)

    @pl.when(jnp.logical_not(has_up))
    def _():
        up_recv[...] = jnp.zeros_like(up_recv)

    @pl.when(jnp.logical_not(has_down))
    def _():
        down_recv[...] = jnp.zeros_like(down_recv)

    @pl.when((band == 0) & is_end)
    def _():
        extra_up[...] = jnp.zeros_like(extra_up)

    @pl.when((band == bands - 1) & is_end)
    def _():
        extra_down[...] = jnp.zeros_like(extra_down)

    @pl.when(is_first)
    def _():
        edge_recv[...] = jnp.zeros_like(edge_recv)

    @pl.when(is_last)
    def _():
        col_recv[...] = jnp.zeros_like(col_recv)

    neighbours = jnp.where(has_up, 1, 0) + jnp.where(has_down, 1, 0)
    pl.semaphore_wait(barrier, sectors - 1 + neighbours)

    def pixel_copy(k, peer, slot):
        return remote(
            send.at[peer], recv.at[slot], pix_send_sem.at[k], pix_recv_sem.at[k], var=peer
        )

    for k in SEND_ORDER:
        pixel_copy(k, lax.rem(sector + k, sectors), sector).start()
    recv[sector] = send[sector]

    loads[0].wait()
    loads[1].wait()
    prepare_weights(
        ids_ref, shift_ref, embed, query_ref, wk, slot_w, keys_scr, bias_scr, query_scr
    )
    loads[2].wait()
    split_values(wv, value_scr)

    def one_part(turn, carry):
        own = sector // 2
        part = lax.rem(own // 2 + turn // 2, 2) * 2 + lax.rem(own % 2 + turn % 2, 2)
        for side in range(2):
            source = part * 2 + side

            @pl.when(source != sector)
            def _():
                pixel_copy(lax.rem(sector + sectors - source, sectors), source, source).wait_recv()

            stage[side] = recv[source].astype(F32)
            for line in range(ROWS):
                line_pixels[line, 0:COLS, 128 * side : 128 * side + 128] = stage[
                    side, COLS * line : COLS * line + COLS, :
                ]

        def lines(step, carry):
            for k in range(EMBED_STEP):
                embed_line(step * EMBED_STEP + k, part, line_pixels, slot_w, normed_scr)
            return carry

        lax.fori_loop(0, ROWS // EMBED_STEP, lines, 0)
        return carry

    lax.fori_loop(0, 4, one_part, 0)

    shift = jnp.minimum(shift_ref[0], shift_ref[1])

    def column_copies(chunk):
        quads = pl.ds(pl.multiple_of(chunk * 16, 16), 16)
        tokens = pl.ds(pl.multiple_of(chunk * CHUNK, 16), CHUNK)
        return (
            remote(
                edge_send.at[quads], edge_recv.at[quads],
                col_send_sem.at[0, chunk], col_recv_sem.at[0, chunk], var=right,
            ),
            remote(
                latents.at[1, tokens], col_recv.at[tokens],
                col_send_sem.at[1, chunk], col_recv_sem.at[1, chunk], var=left,
            ),
        )

    def extra_copies(chunk):
        quads = pl.ds(pl.multiple_of(chunk * 16, 16), 16)
        tokens = pl.ds(pl.multiple_of(chunk * CHUNK, 16), CHUNK)
        copies = []
        for end, src, part in ((is_first, latents.at[1, tokens], tokens), (is_last, edge_send.at[quads], quads)):
            copies.append((end & has_up, remote(
                src, extra_down.at[part], extra_send_sem.at[0, chunk], extra_recv_sem.at[0, chunk], lat=band - 1
            )))
            copies.append((end & has_down, remote(
                src, extra_up.at[part], extra_send_sem.at[1, chunk], extra_recv_sem.at[1, chunk], lat=band + 1
            )))
        return copies

    def take_extra():
        for chunk in range(CHUNKS):
            for i, (_, copy) in enumerate(extra_copies(chunk)):
                end = is_first if i < 2 else is_last
                pl.when(end & (has_down if i % 2 == 0 else has_up))(functools.partial(wait_received, copy))

    def row_copies(pair, chunk):
        (up_start, up_count), (down_start, down_count) = UP_PARTS[chunk], DOWN_PARTS[chunk]
        up_part, down_part = pl.ds(up_start, up_count), pl.ds(down_start, down_count)
        upward = remote(
            slab.at[pair, up_part], down_recv.at[pair, up_part],
            row_send_sem.at[pair, 0, chunk], row_recv_sem.at[pair, 0, chunk], lat=band - 1,
        )
        downward = remote(
            slab.at[pair, down_part], up_recv.at[pair, down_part],
            row_send_sem.at[pair, 1, chunk], row_recv_sem.at[pair, 1, chunk], lat=band + 1,
        )
        return upward, downward

    def send_rows(pair, chunk):
        upward, downward = row_copies(pair, chunk)

        @pl.when(has_up)
        def _():
            upward.start()

        @pl.when(has_down)
        def _():
            downward.start()

    def take_rows(pair):
        for chunk in range(CHUNKS):
            upward, downward = row_copies(pair, chunk)

            @pl.when(has_down)
            def _():
                upward.wait_recv()

            @pl.when(has_up)
            def _():
                downward.wait_recv()

    def share_rows(chunk):
        edge_copy, col_copy = column_copies(chunk)
        tokens = slice(CHUNK * chunk, CHUNK * chunk + CHUNK)
        quads = slice(16 * chunk, 16 * chunk + 16)
        pl.when(has_right)(lambda: wait_received(col_copy))
        column = column_of(iota((CHUNK, D), 0))
        slab[1, tokens] = jnp.where(
            column < shift, col_recv[tokens].astype(F32), latents[1, tokens].astype(F32)
        ).astype(BF16)
        send_rows(1, chunk)
        pl.when(has_left)(lambda: wait_received(edge_copy))
        own = latents[0, tokens].astype(F32)
        slab[0, tokens] = with_last_column(
            quads_of(own, False), quads_of(own, True), edge_recv[quads].astype(F32)
        ).astype(BF16)
        send_rows(0, chunk)


    def one_chunk(chunk, carry):
        def quads(step, carry):
            for k in range(MERGE_STEP):
                quad = chunk * 2 * QUADS + step * MERGE_STEP + k
                merge_quad(quad, keys_scr, bias_scr, normed_scr, pooled_scr)
            return carry

        lax.fori_loop(0, 2 * QUADS // MERGE_STEP, quads, 0)
        fresh = project(chunk, pooled_scr, value_scr, query_scr)
        start = pl.multiple_of(chunk * CHUNK, 16)
        for pair in range(2):
            tokens = fresh[:, 8 * pair : 8 * pair + 8].reshape(CHUNK, D)
            latents[pair, pl.ds(start, CHUNK), :] = tokens.astype(BF16)
            if pair == 0:
                quads = pl.ds(pl.multiple_of(chunk * 16, 16), 16)
                edge_send[quads, :] = quads_of(tokens, True).astype(BF16)
        edge_copy, col_copy = column_copies(chunk)
        pl.when(has_right)(lambda: start_copy(edge_copy))
        pl.when(has_left)(lambda: start_copy(col_copy))
        for where, copy in extra_copies(chunk):
            pl.when(where)(functools.partial(start_copy, copy))
        for ready in range(CHUNKS - 1):
            @pl.when(chunk == ready + 1)
            def _():
                share_rows(ready)

        return carry

    lax.fori_loop(0, CHUNKS, one_chunk, 0)
    share_rows(CHUNKS - 1)

    first = band * ROWS - (WIN_LAT - 1)
    total_rows = window_ref.shape[0]

    def row_ident(k):
        row = first + k
        inside = (row >= 0) & (row < total_rows)
        return jnp.where(inside, window_ref[jnp.clip(row, 0, total_rows - 1)], -1)

    key_token = iota((1, KEYS), 1)
    query_token = iota((OWN, 1), 0)
    key_row = jnp.full((1, KEYS), -1, jnp.int32)
    query_row = jnp.full((OWN, 1), -1, jnp.int32)
    for k in range(ROWS + 2 * (WIN_LAT - 1)):
        ident = row_ident(k)
        key_row = jnp.where(key_token // LINE == k, ident, key_row)
        if 0 <= k - (WIN_LAT - 1) < ROWS:
            query_row = jnp.where(query_token // LINE == k - (WIN_LAT - 1), ident, query_row)

    loads[3].wait()
    loads[4].wait()
    def around(own_part, halo_part):
        edge = halo_part.shape[0] // 2
        return jnp.concatenate([halo_part[:edge], own_part, halo_part[edge:]], axis=0).astype(BF16)

    def attend_extra(own, up, down, same):
        own_qkv = dot(layer_norm(own).astype(BF16), qkv[...])
        halo = jnp.concatenate([up.astype(F32), down.astype(F32)], axis=0)
        halo = dot(layer_norm(halo).astype(BF16), qkv[:, D:])
        keys = around(own_qkv[:, D : 2 * D], halo[:, :D])
        values = around(own_qkv[:, 2 * D :], halo[:, D:])
        mixed = attention(own_qkv[:, :D], keys, values, jnp.where(same, 0.0, MASKED))
        return (own + dot(mixed, wo[...])).astype(BF16)

    def window_bias(pair):
        def wrapped(token):
            if pair == 0:
                return jnp.where((column_of(token) == COLS - 1) & (sector == 0), 1, 0)
            return jnp.where((column_of(token) < shift) & (sector == sectors - 1), 1, 0)

        same = (query_row * 2 + wrapped(query_token)) == (key_row * 2 + wrapped(key_token))
        return jnp.where(same, 0.0, MASKED)

    near = {}
    for pair in (1, 0):
        own = slab[pair].astype(F32)
        own_qkv = dot(layer_norm(own).astype(BF16), qkv[...])
        queries, keys, values = own_qkv[:, :D], own_qkv[:, D : 2 * D], own_qkv[:, 2 * D :]
        bias = window_bias(pair)
        state = attend_near(
            queries, keys[:NEAR].astype(BF16), values[:NEAR].astype(BF16), bias[:, EDGE : EDGE + NEAR]
        )
        near[pair] = own, queries, keys[NEAR:], values[NEAR:], state

    take_extra()

    @pl.when(is_first)
    def _():
        below = [jnp.where(column_of(token) < shift, 1, 0) for token in (query_token, key_token)]
        same = (query_row * 2 + below[0]) == (key_row * 2 + below[1])
        back_recv[...] = attend_extra(
            latents[1].astype(F32), extra_up[OWN - EDGE :], extra_down[:EDGE], same
        )

    @pl.when(is_last)
    def _():
        ident = [jnp.full((48, 1), -1, jnp.int32), jnp.full((1, 128), -1, jnp.int32)]
        token = [iota((48, 1), 0), iota((1, 128), 1)]
        for k in range(ROWS + 2 * (WIN_LAT - 1)):
            ident[1] = jnp.where(token[1] // 8 == k, row_ident(k), ident[1])
            ident[0] = jnp.where(token[0] // 8 == k - (WIN_LAT - 1), row_ident(k), ident[0])
        side = [jnp.where(t % GROUP == GROUP - 1, 1, 0) for t in token]
        same = (ident[0] * 2 + side[0]) == (ident[1] * 2 + side[1])
        back_edge_recv[...] = attend_extra(
            edge_send[...].astype(F32), extra_up[0:48].astype(F32)[8:], extra_down[0:48].astype(F32)[:40], same
        )

    def attend_window(pair):
        own, queries, keys, values, state = near[pair]
        take_rows(pair)
        halo = jnp.concatenate(
            [up_recv[pair].astype(F32)[OWN - EDGE :], down_recv[pair].astype(F32)[:EDGE]], axis=0
        )
        halo = dot(layer_norm(halo).astype(BF16), qkv[:, D:])
        keys, values = around(keys, halo[:, :D]), around(values, halo[:, D:])
        far_token = iota((1, 2 * EDGE + OWN - NEAR), 1)
        far_token = jnp.where(far_token < EDGE, far_token, far_token + NEAR)
        far_row = jnp.full(far_token.shape, -1, jnp.int32)
        for k in range(ROWS + 2 * (WIN_LAT - 1)):
            far_row = jnp.where(far_token // LINE == k, row_ident(k), far_row)

        def wrapped(token):
            if pair == 0:
                return jnp.where((column_of(token) == COLS - 1) & (sector == 0), 1, 0)
            return jnp.where((column_of(token) < shift) & (sector == sectors - 1), 1, 0)

        same = (query_row * 2 + wrapped(query_token)) == (far_row * 2 + wrapped(far_token))
        mixed = attend_far(queries, keys, values, jnp.where(same, 0.0, MASKED), state)
        return own + dot(mixed, wo[...])

    backs = []
    encoded[1] = attend_window(1).astype(BF16)
    back = remote(encoded.at[1], back_recv, back_send_sem.at[0], back_recv_sem.at[0], var=right)
    pl.when(has_right)(functools.partial(start_copy, back))
    backs.append(back)
    done = attend_window(0)
    encoded[0, 0:48] = quads_of(done, True).astype(BF16)
    back = remote(
        encoded.at[0, pl.ds(0, 48)], back_edge_recv, back_send_sem.at[1], back_recv_sem.at[1], var=left
    )
    pl.when(has_left)(functools.partial(start_copy, back))
    backs.append(back)
    first_rest = quads_of(done, False)

    swap = jnp.where(shift_ref[1] > shift_ref[0], 1, 0)
    row = iota((2 * OWN, OWN), 0)
    level = row % LEVELS
    place = row // 48 * LINE + row % 48 // 16 * 8 + level % 2 * GROUP + row % 16 // LEVELS
    hit = place == iota((2 * OWN, OWN), 1)
    orders = [
        jnp.where(hit & (level // 2 == (swap if pair == 0 else 1 - swap)), 1.0, 0.0).astype(BF16)
        for pair in range(2)
    ]
    pl.when(has_right)(lambda: wait_received(backs[1]))
    first_pair = with_last_column(
        first_rest, encoded[0, 0:48].astype(F32), back_edge_recv[...].astype(F32)
    )
    result = dot(orders[0], first_pair.astype(BF16))
    pl.when(has_left)(lambda: wait_received(backs[0]))
    column = column_of(iota((OWN, D), 0))
    second_pair = jnp.where(column < shift, back_recv[...].astype(F32), encoded[1].astype(F32))
    result = result + dot(orders[1], second_pair.astype(BF16))
    out_ref[...] = result.reshape(ROWS, COLS, LEVELS, D).astype(BF16)

    for k in range(1, sectors):
        pixel_copy(k, lax.rem(sector + k, sectors), sector).wait_send()
    for chunk in range(CHUNKS):
        edge_copy, col_copy = column_copies(chunk)
        pl.when(has_right)(functools.partial(wait_sent, edge_copy))
        pl.when(has_left)(functools.partial(wait_sent, col_copy))
        for where, copy in extra_copies(chunk):
            pl.when(where)(functools.partial(wait_sent, copy))
        for pair in range(2):
            upward, downward = row_copies(pair, chunk)

            @pl.when(has_up)
            def _():
                upward.wait_send()

            @pl.when(has_down)
            def _():
                downward.wait_send()

    for back, where in zip(backs, (has_right, has_left)):
        pl.when(where)(functools.partial(wait_sent, back))


def shards(
    fields, field_ids, embed_w, lat_query, perc_wk, perc_wv, swin_qkv, swin_wo, row_window, lon_shift
):
    vmem = pl.BlockSpec(memory_space=pltpu.VMEM)
    smem = pl.BlockSpec(memory_space=pltpu.SMEM)
    hbm = pl.BlockSpec(memory_space=pltpu.HBM)
    encoded = pl.pallas_call(
        whole_kernel,
        out_shape=jax.ShapeDtypeStruct((ROWS, COLS, LEVELS, D), BF16),
        in_specs=[smem] * 3 + [vmem] * 2 + [hbm] * 5,
        out_specs=vmem,
        scratch_shapes=[
            pltpu.VMEM((FIELDS, PIX, D), BF16),
            pltpu.VMEM((D, D), BF16),
            pltpu.VMEM((D, D), BF16),
            pltpu.VMEM((D, 3 * D), BF16),
            pltpu.VMEM((D, D), BF16),
            pltpu.VMEM((FIELDS * PIX, D), BF16),
            pltpu.VMEM((256, D), BF16),
            pltpu.VMEM((256, 256), F32),
            pltpu.VMEM((ROWS * COLS, FIELDS, D), BF16),
            pltpu.VMEM((HEADS, 2 * OWN, D), BF16),
            pltpu.VMEM((16, D), F32),
            pltpu.VMEM((8, 80, 128), F32),
            pltpu.VMEM((8, 80, 128), BF16),
            pltpu.VMEM((8, 80, 128), BF16),
            pltpu.VMEM((ROWS, 16, 256), F32),
            pltpu.VMEM((2, OWN, D), BF16),
            pltpu.VMEM((2, OWN, D), BF16),
            pltpu.VMEM((48, D), BF16),
            pltpu.VMEM((48, D), BF16),
            pltpu.VMEM((OWN, D), BF16),
            pltpu.VMEM((2, OWN, D), BF16),
            pltpu.VMEM((2, OWN, D), BF16),
            pltpu.VMEM((2, OWN, D), BF16),
            pltpu.VMEM((48, D), BF16),
            pltpu.VMEM((OWN, D), BF16),
            pltpu.SemaphoreType.DMA((5,)),
            pltpu.SemaphoreType.DMA((8,)),
            pltpu.SemaphoreType.DMA((8,)),
            pltpu.SemaphoreType.DMA((2, CHUNKS)),
            pltpu.SemaphoreType.DMA((2, CHUNKS)),
            pltpu.SemaphoreType.DMA((2, 2, CHUNKS)),
            pltpu.SemaphoreType.DMA((2, 2, CHUNKS)),
            pltpu.SemaphoreType.DMA((2,)),
            pltpu.SemaphoreType.DMA((2,)),
            pltpu.VMEM((OWN, D), BF16),
            pltpu.VMEM((OWN, D), BF16),
            pltpu.SemaphoreType.DMA((2, CHUNKS)),
            pltpu.SemaphoreType.DMA((2, CHUNKS)),
            pltpu.VMEM((HEADS, D, 256), BF16),
        ],
        compiler_params=pltpu.CompilerParams(
            vmem_limit_bytes=63 << 20, collective_id=0, has_side_effects=True
        ),
        name="whole",
    )(
        field_ids, lon_shift, row_window, fields, lat_query, embed_w, perc_wk, perc_wv, swin_qkv, swin_wo
    )
    return jnp.transpose(encoded, (2, 0, 1, 3))


def solution(mesh):
    in_specs = (P("var", "lat", None), P(), P(), P(), P(), P(), P(), P(), P(), P())
    out_specs = P(None, "lat", "var", None)
    return jax.shard_map(shards, mesh=mesh, in_specs=in_specs, out_specs=out_specs, check_vma=False)
```

```python
import functools
import math

import jax
import jax.numpy as jnp
from jax import lax
from jax.experimental import pallas as pl
from jax.experimental.pallas import tpu as pltpu
from jax.sharding import PartitionSpec as P

D = 512
HEADS = 16
HEAD = 32
LEVELS = 4
PATCH = 4
WIN_LAT = 6
WIN_LON = 12
FIELDS = 64
ROWS = 6
COLS = 12
PIX = PATCH * PATCH
GROUP = 4
QUADS = COLS // GROUP
LINE = 2 * COLS
OWN = ROWS * LINE
HALO = 128
KEYS = 384
EDGE = 120

EPSILON = 1e-05
MASKED = -1e30
EXP2_SCALE = math.log2(math.e) / math.sqrt(HEAD)
F32 = jnp.float32
BF16 = jnp.bfloat16
NT = (((1,), (1,)), ((), ()))
TN = (((0,), (0,)), ((), ()))
MESH = pl.DeviceIdType.MESH
SEND_ORDER = (4, 3, 5, 2, 6, 1, 7)
CHUNKS = 3
EMBED_STEP = 6
MERGE_STEP = 6
NEAR = 128
CHUNK = 2 * LINE
UP_PARTS = ((0, 48), (48, 48), (96, 32))
DOWN_PARTS = ((16, 32), (48, 48), (96, 48))


def dot(a, b):
    return jnp.dot(a, b, preferred_element_type=F32)


def iota(shape, dim):
    return lax.broadcasted_iota(jnp.int32, shape, dim)


def layer_norm(values):
    row_mean = jnp.sum(values, axis=-1, keepdims=True) * (1.0 / D)
    centred = values - row_mean
    variance = jnp.sum(centred * centred, axis=-1, keepdims=True) * (1.0 / D)
    return centred * lax.rsqrt(variance + EPSILON)


def softmax_rows(scores):
    row_top = jnp.max(scores, axis=-1, keepdims=True)
    lifted = jnp.exp2(scores - row_top)
    return lifted * (1.0 / jnp.sum(lifted, axis=-1, keepdims=True))


def column_of(token):
    return (token % LINE) // 8 * GROUP + token % GROUP


def remote(src, dst, send_sem, recv_sem, **device):
    return pltpu.make_async_remote_copy(
        src_ref=src, dst_ref=dst, send_sem=send_sem, recv_sem=recv_sem,
        device_id=device, device_id_type=MESH,
    )


def start_copy(copy):
    copy.start()


def wait_received(copy):
    copy.wait_recv()


def wait_sent(copy):
    copy.wait_send()


def attention(queries, keys, values, bias):
    count, key_count = queries.shape[0], keys.shape[0]
    lane_head = iota((count, 256), 1) // HEAD
    halves = []
    for half in range(2):
        cut = slice(256 * half, 256 * half + 256)
        part = queries[:, cut]
        stacked = jnp.concatenate(
            [jnp.where(lane_head == h, part, 0.0).astype(BF16) for h in range(8)], axis=0
        )
        scores = lax.dot_general(stacked, keys[:, cut], NT, preferred_element_type=F32)
        scores = scores.reshape(8, count, key_count) * EXP2_SCALE + bias[None]
        weights = softmax_rows(scores).astype(BF16).reshape(8 * count, key_count)
        mixed = dot(weights, values[:, cut]).reshape(8, count, 256)
        total = jnp.zeros((count, 256), F32)
        for h in range(8):
            total = jnp.where(lane_head == h, mixed[h], total)
        halves.append(total.astype(BF16))
    return jnp.concatenate(halves, axis=-1)


def split_values(wv, value_scr):
    lane_head = iota((D, 256), 1) // HEAD
    for half in range(2):
        value_w = wv[:, 256 * half : 256 * half + 256].astype(F32)
        for head in range(8):
            value_scr[8 * half + head] = jnp.where(lane_head == head, value_w, 0.0).astype(BF16)


def heads_apart(queries):
    lane_head = iota(queries.shape, 1) // HEAD
    return jnp.concatenate(
        [jnp.where(lane_head == h, queries, 0.0).astype(BF16) for h in range(8)], axis=0
    )


def heads_together(stacked):
    lane_head = iota((stacked.shape[1], 256), 1) // HEAD
    total = jnp.broadcast_to(stacked[0], lane_head.shape)
    for h in range(1, 8):
        total = jnp.where(lane_head == h, stacked[h], total)
    return total


def attend_near(queries, keys, values, bias):
    count, key_count = bias.shape
    state = []
    for half in range(2):
        cut = slice(256 * half, 256 * half + 256)
        scores = lax.dot_general(
            heads_apart(queries[:, cut]), keys[:, cut], NT, preferred_element_type=F32
        )
        scores = scores.reshape(8, count, key_count) * EXP2_SCALE + bias[None]
        top = jnp.max(scores, axis=-1, keepdims=True)
        lifted = jnp.exp2(scores - top)
        total = jnp.sum(lifted, axis=-1, keepdims=True)
        mixed = dot(lifted.astype(BF16).reshape(8 * count, key_count), values[:, cut])
        state.append((top, total, heads_together(mixed.reshape(8, count, 256))))
    return state


def attend_far(queries, keys, values, bias, state):
    count, key_count = bias.shape
    halves = []
    for half, (near_top, near_total, near_mixed) in enumerate(state):
        cut = slice(256 * half, 256 * half + 256)
        scores = lax.dot_general(
            heads_apart(queries[:, cut]), keys[:, cut], NT, preferred_element_type=F32
        )
        scores = scores.reshape(8, count, key_count) * EXP2_SCALE + bias[None]
        top = jnp.maximum(near_top, jnp.max(scores, axis=-1, keepdims=True))
        lifted = jnp.exp2(scores - top)
        near_scale = jnp.exp2(near_top - top)
        total = near_scale * near_total + jnp.sum(lifted, axis=-1, keepdims=True)
        inverse = 1.0 / total
        mixed = dot(
            (lifted * inverse).astype(BF16).reshape(8 * count, key_count), values[:, cut]
        )
        mixed = heads_together(mixed.reshape(8, count, 256))
        mixed = mixed + near_mixed * heads_together(near_scale * inverse)
        halves.append(mixed.astype(BF16))
    return jnp.concatenate(halves, axis=-1)


def pick_pixels(fields, stage, send):
    flat = fields.astype(F32).reshape(8 * ROWS * PATCH, 384).astype(BF16)
    row = iota((512, 1), 0)
    column = row % 16
    source = jnp.where(column < COLS, (row % 128) // 16 * 48 + column * PATCH + row // 128, -1)
    pick = jnp.where(source == iota((512, 384), 1), 1.0, 0.0).astype(BF16)
    turned = lax.dot_general(pick, flat, NT, preferred_element_type=F32).astype(BF16)
    row = iota((192, 1), 0)
    target = (row // PATCH) % ROWS * 128 + row // (ROWS * PATCH) * PIX + row % PATCH * PATCH
    lane = iota((192, 768), 1)
    total = jnp.zeros((128, 768), F32)
    for j in range(PATCH):
        place = jnp.where(target + j == lane, 1.0, 0.0).astype(BF16)
        total = total + dot(turned[128 * j : 128 * j + 128], place)
    for sector in range(8):
        stage[sector, 72:80, :] = jnp.zeros((8, 128), F32)
        for line in range(ROWS):
            stage[sector, COLS * line : COLS * line + COLS, :] = total[
                16 * sector : 16 * sector + COLS, 128 * line : 128 * line + 128
            ]
    send[...] = stage[...].astype(BF16)


def prepare_weights(ids_ref, shift_ref, embed, query_ref, wk, slot_w, keys_scr, bias_scr, query_scr):
    def place(slot, carry):
        start = pl.multiple_of(slot * PIX, PIX)
        slot_w[pl.ds(start, PIX), :] = embed[ids_ref[slot]]
        return carry

    lax.fori_loop(0, FIELDS, place, 0)
    swap = shift_ref[1] > shift_ref[0]
    query = query_ref[...].astype(F32)
    swapped = jnp.concatenate([query[2:], query[:2]], axis=0)
    query = jnp.where(swap, swapped, query)
    level = (iota((256, D), 0) // GROUP) % LEVELS
    spread = jnp.zeros((256, D), F32)
    for lev in range(LEVELS):
        spread = jnp.where(level == lev, query[lev : lev + 1, :], spread)
    query_scr[...] = spread[:16]
    own_head = iota((256, D), 1) // HEAD == iota((256, D), 0) // 16
    masked = jnp.where(own_head, spread, 0.0).astype(BF16)
    keys_scr[...] = lax.dot_general(
        wk[...], masked, NT, preferred_element_type=F32
    ).astype(BF16)
    same = iota((256, 256), 0) // FIELDS == iota((256, 256), 1) % GROUP
    bias_scr[...] = jnp.where(same, 0.0, MASKED)


def embed_line(line, part, line_pixels, slot_w, normed_scr):
    own_slot = iota((1, 16, 256), 2) // PIX == iota((1, 16, 256), 1)
    pixels = line_pixels[line][:COLS]
    spread = jnp.where(own_slot, pixels[:, None, :], 0.0).astype(BF16)
    weight = slot_w[pl.ds(pl.multiple_of(256 * part, 256), 256), :]
    tokens = dot(spread.reshape(COLS * 16, 256), weight)
    normed = layer_norm(tokens).astype(BF16)
    slots = pl.ds(pl.multiple_of(16 * part, 16), 16)
    normed_scr[pl.ds(line * COLS, COLS), slots, :] = normed.reshape(COLS, 16, D)


def merge_quad(quad, keys_scr, bias_scr, normed_scr, pooled_scr):
    normed = normed_scr[pl.ds(quad * GROUP, GROUP)].reshape(GROUP * FIELDS, D)
    scores = dot(normed, keys_scr[...]) * EXP2_SCALE + bias_scr[...]
    lifted = jnp.exp2(scores - jnp.max(scores, axis=0, keepdims=True))
    weights = (lifted * (1.0 / jnp.sum(lifted, axis=0, keepdims=True))).astype(BF16)
    pooled = lax.dot_general(weights, normed, TN, preferred_element_type=F32).astype(BF16)
    start = pl.multiple_of(quad * 16, 16)
    pooled_scr[:, pl.ds(start, 16), :] = pooled.reshape(HEADS, 16, D)


def project(chunk, pooled_scr, value_scr, query_scr):
    start = pl.multiple_of(chunk * 2 * CHUNK, 2 * CHUNK)
    halves = []
    for half in range(2):
        total = jnp.zeros((2 * CHUNK, 256), F32)
        for head in range(8 * half, 8 * half + 8):
            total = total + dot(pooled_scr[head, pl.ds(start, 2 * CHUNK), :], value_scr[head])
        halves.append(total)
    projected = jnp.concatenate(halves, axis=-1).reshape(2 * QUADS, 16, D)
    return projected + query_scr[...][None]


def quads_of(tokens, last):
    width = tokens.shape[-1]
    tokens = tokens.reshape(tokens.shape[0] // 8, 8, width)
    picked = [q for q in range(tokens.shape[0]) if (q % QUADS == QUADS - 1) == last]
    return jnp.concatenate([tokens[q] for q in picked], axis=0)


def with_last_column(rest, own, received):
    is_last = iota(own.shape, 0) % GROUP == GROUP - 1
    last = jnp.where(is_last, received, own)
    pieces = []
    for r in range(own.shape[0] // 8):
        pieces += [rest[16 * r : 16 * r + 16], last[8 * r : 8 * r + 8]]
    return jnp.concatenate(pieces, axis=0)


def whole_kernel(
    ids_ref, shift_ref, window_ref, fields_ref, query_ref, embed_h, wk_h, wv_h, qkv_h, wo_h, out_ref,
    embed, wk, wv, qkv, wo, slot_w, keys_scr, bias_scr, normed_scr, pooled_scr, query_scr,
    stage, send, recv, line_pixels, latents, slab, edge_send, edge_recv, col_recv, up_recv, down_recv,
    encoded, back_edge_recv, back_recv,
    load_sem, pix_send_sem, pix_recv_sem, col_send_sem, col_recv_sem, row_send_sem, row_recv_sem,
    back_send_sem, back_recv_sem, extra_up, extra_down, extra_send_sem, extra_recv_sem,
    value_scr,
):
    sector = lax.axis_index("var")
    sectors = lax.axis_size("var")
    band = lax.axis_index("lat")
    bands = lax.axis_size("lat")
    right = lax.rem(sector + 1, sectors)
    left = lax.rem(sector + sectors - 1, sectors)
    is_first = sector == 0
    is_last = sector == sectors - 1
    is_end = is_first | is_last
    has_left = jnp.logical_not(is_first)
    has_right = jnp.logical_not(is_last)
    has_up = band > 0
    has_down = band < bands - 1

    barrier = pltpu.get_barrier_semaphore()
    for k in range(1, sectors):
        pl.semaphore_signal(
            barrier, inc=1, device_id={"var": lax.rem(sector + k, sectors)}, device_id_type=MESH
        )

    @pl.when(has_up)
    def _():
        pl.semaphore_signal(barrier, inc=1, device_id={"lat": band - 1}, device_id_type=MESH)

    @pl.when(has_down)
    def _():
        pl.semaphore_signal(barrier, inc=1, device_id={"lat": band + 1}, device_id_type=MESH)

    loads = [
        pltpu.make_async_copy(src, dst, load_sem.at[i])
        for i, (src, dst) in enumerate(
            [(embed_h, embed), (wk_h, wk), (wv_h, wv), (qkv_h, qkv), (wo_h, wo)]
        )
    ]
    for load in loads:
        load.start()

    pick_pixels(fields_ref[...], stage, send)

    @pl.when(jnp.logical_not(has_up))
    def _():
        up_recv[...] = jnp.zeros_like(up_recv)

    @pl.when(jnp.logical_not(has_down))
    def _():
        down_recv[...] = jnp.zeros_like(down_recv)

    @pl.when((band == 0) & is_end)
    def _():
        extra_up[...] = jnp.zeros_like(extra_up)

    @pl.when((band == bands - 1) & is_end)
    def _():
        extra_down[...] = jnp.zeros_like(extra_down)

    @pl.when(is_first)
    def _():
        edge_recv[...] = jnp.zeros_like(edge_recv)

    @pl.when(is_last)
    def _():
        col_recv[...] = jnp.zeros_like(col_recv)

    neighbours = jnp.where(has_up, 1, 0) + jnp.where(has_down, 1, 0)
    pl.semaphore_wait(barrier, sectors - 1 + neighbours)

    def pixel_copy(k, peer, slot):
        return remote(
            send.at[peer], recv.at[slot], pix_send_sem.at[k], pix_recv_sem.at[k], var=peer
        )

    for k in SEND_ORDER:
        pixel_copy(k, lax.rem(sector + k, sectors), sector).start()
    recv[sector] = send[sector]

    loads[0].wait()
    loads[1].wait()
    prepare_weights(
        ids_ref, shift_ref, embed, query_ref, wk, slot_w, keys_scr, bias_scr, query_scr
    )
    loads[2].wait()
    split_values(wv, value_scr)

    def one_part(turn, carry):
        own = sector // 2
        part = lax.rem(own // 2 + turn // 2, 2) * 2 + lax.rem(own % 2 + turn % 2, 2)
        for side in range(2):
            source = part * 2 + side

            @pl.when(source != sector)
            def _():
                pixel_copy(lax.rem(sector + sectors - source, sectors), source, source).wait_recv()

            stage[side] = recv[source].astype(F32)
            for line in range(ROWS):
                line_pixels[line, 0:COLS, 128 * side : 128 * side + 128] = stage[
                    side, COLS * line : COLS * line + COLS, :
                ]

        def lines(step, carry):
            for k in range(EMBED_STEP):
                embed_line(step * EMBED_STEP + k, part, line_pixels, slot_w, normed_scr)
            return carry

        lax.fori_loop(0, ROWS // EMBED_STEP, lines, 0)
        return carry

    lax.fori_loop(0, 4, one_part, 0)

    shift = jnp.minimum(shift_ref[0], shift_ref[1])

    def column_copies(chunk):
        quads = pl.ds(pl.multiple_of(chunk * 16, 16), 16)
        tokens = pl.ds(pl.multiple_of(chunk * CHUNK, 16), CHUNK)
        return (
            remote(
                edge_send.at[quads], edge_recv.at[quads],
                col_send_sem.at[0, chunk], col_recv_sem.at[0, chunk], var=right,
            ),
            remote(
                latents.at[1, tokens], col_recv.at[tokens],
                col_send_sem.at[1, chunk], col_recv_sem.at[1, chunk], var=left,
            ),
        )

    def extra_copies(chunk):
        quads = pl.ds(pl.multiple_of(chunk * 16, 16), 16)
        tokens = pl.ds(pl.multiple_of(chunk * CHUNK, 16), CHUNK)
        copies = []
        for end, src, part in ((is_first, latents.at[1, tokens], tokens), (is_last, edge_send.at[quads], quads)):
            copies.append((end & has_up, remote(
                src, extra_down.at[part], extra_send_sem.at[0, chunk], extra_recv_sem.at[0, chunk], lat=band - 1
            )))
            copies.append((end & has_down, remote(
                src, extra_up.at[part], extra_send_sem.at[1, chunk], extra_recv_sem.at[1, chunk], lat=band + 1
            )))
        return copies

    def take_extra():
        for chunk in range(CHUNKS):
            for i, (_, copy) in enumerate(extra_copies(chunk)):
                end = is_first if i < 2 else is_last
                pl.when(end & (has_down if i % 2 == 0 else has_up))(functools.partial(wait_received, copy))

    def row_copies(pair, chunk):
        (up_start, up_count), (down_start, down_count) = UP_PARTS[chunk], DOWN_PARTS[chunk]
        up_part, down_part = pl.ds(up_start, up_count), pl.ds(down_start, down_count)
        upward = remote(
            slab.at[pair, up_part], down_recv.at[pair, up_part],
            row_send_sem.at[pair, 0, chunk], row_recv_sem.at[pair, 0, chunk], lat=band - 1,
        )
        downward = remote(
            slab.at[pair, down_part], up_recv.at[pair, down_part],
            row_send_sem.at[pair, 1, chunk], row_recv_sem.at[pair, 1, chunk], lat=band + 1,
        )
        return upward, downward

    def send_rows(pair, chunk):
        upward, downward = row_copies(pair, chunk)

        @pl.when(has_up)
        def _():
            upward.start()

        @pl.when(has_down)
        def _():
            downward.start()

    def take_rows(pair):
        for chunk in range(CHUNKS):
            upward, downward = row_copies(pair, chunk)

            @pl.when(has_down)
            def _():
                upward.wait_recv()

            @pl.when(has_up)
            def _():
                downward.wait_recv()

    def share_rows(chunk):
        edge_copy, col_copy = column_copies(chunk)
        tokens = slice(CHUNK * chunk, CHUNK * chunk + CHUNK)
        quads = slice(16 * chunk, 16 * chunk + 16)
        pl.when(has_right)(lambda: wait_received(col_copy))
        column = column_of(iota((CHUNK, D), 0))
        slab[1, tokens] = jnp.where(
            column < shift, col_recv[tokens].astype(F32), latents[1, tokens].astype(F32)
        ).astype(BF16)
        send_rows(1, chunk)
        pl.when(has_left)(lambda: wait_received(edge_copy))
        own = latents[0, tokens].astype(F32)
        slab[0, tokens] = with_last_column(
            quads_of(own, False), quads_of(own, True), edge_recv[quads].astype(F32)
        ).astype(BF16)
        send_rows(0, chunk)


    def one_chunk(chunk, carry):
        def quads(step, carry):
            for k in range(MERGE_STEP):
                quad = chunk * 2 * QUADS + step * MERGE_STEP + k
                merge_quad(quad, keys_scr, bias_scr, normed_scr, pooled_scr)
            return carry

        lax.fori_loop(0, 2 * QUADS // MERGE_STEP, quads, 0)
        fresh = project(chunk, pooled_scr, value_scr, query_scr)
        start = pl.multiple_of(chunk * CHUNK, 16)
        for pair in range(2):
            tokens = fresh[:, 8 * pair : 8 * pair + 8].reshape(CHUNK, D)
            latents[pair, pl.ds(start, CHUNK), :] = tokens.astype(BF16)
            if pair == 0:
                quads = pl.ds(pl.multiple_of(chunk * 16, 16), 16)
                edge_send[quads, :] = quads_of(tokens, True).astype(BF16)
        edge_copy, col_copy = column_copies(chunk)
        pl.when(has_right)(lambda: start_copy(edge_copy))
        pl.when(has_left)(lambda: start_copy(col_copy))
        for where, copy in extra_copies(chunk):
            pl.when(where)(functools.partial(start_copy, copy))
        for ready in range(CHUNKS - 1):
            @pl.when(chunk == ready + 1)
            def _():
                share_rows(ready)

        return carry

    lax.fori_loop(0, CHUNKS, one_chunk, 0)
    share_rows(CHUNKS - 1)

    first = band * ROWS - (WIN_LAT - 1)
    total_rows = window_ref.shape[0]

    def row_ident(k):
        row = first + k
        inside = (row >= 0) & (row < total_rows)
        return jnp.where(inside, window_ref[jnp.clip(row, 0, total_rows - 1)], -1)

    key_token = iota((1, KEYS), 1)
    query_token = iota((OWN, 1), 0)
    key_row = jnp.full((1, KEYS), -1, jnp.int32)
    query_row = jnp.full((OWN, 1), -1, jnp.int32)
    for k in range(ROWS + 2 * (WIN_LAT - 1)):
        ident = row_ident(k)
        key_row = jnp.where(key_token // LINE == k, ident, key_row)
        if 0 <= k - (WIN_LAT - 1) < ROWS:
            query_row = jnp.where(query_token // LINE == k - (WIN_LAT - 1), ident, query_row)

    loads[3].wait()
    loads[4].wait()
    def around(own_part, halo_part):
        edge = halo_part.shape[0] // 2
        return jnp.concatenate([halo_part[:edge], own_part, halo_part[edge:]], axis=0).astype(BF16)

    def attend_extra(own, up, down, same):
        own_qkv = dot(layer_norm(own).astype(BF16), qkv[...])
        halo = jnp.concatenate([up.astype(F32), down.astype(F32)], axis=0)
        halo = dot(layer_norm(halo).astype(BF16), qkv[:, D:])
        keys = around(own_qkv[:, D : 2 * D], halo[:, :D])
        values = around(own_qkv[:, 2 * D :], halo[:, D:])
        mixed = attention(own_qkv[:, :D], keys, values, jnp.where(same, 0.0, MASKED))
        return (own + dot(mixed, wo[...])).astype(BF16)

    def window_bias(pair):
        def wrapped(token):
            if pair == 0:
                return jnp.where((column_of(token) == COLS - 1) & (sector == 0), 1, 0)
            return jnp.where((column_of(token) < shift) & (sector == sectors - 1), 1, 0)

        same = (query_row * 2 + wrapped(query_token)) == (key_row * 2 + wrapped(key_token))
        return jnp.where(same, 0.0, MASKED)

    near = {}
    for pair in (1, 0):
        own = slab[pair].astype(F32)
        own_qkv = dot(layer_norm(own).astype(BF16), qkv[...])
        queries, keys, values = own_qkv[:, :D], own_qkv[:, D : 2 * D], own_qkv[:, 2 * D :]
        bias = window_bias(pair)
        state = attend_near(
            queries, keys[:NEAR].astype(BF16), values[:NEAR].astype(BF16), bias[:, EDGE : EDGE + NEAR]
        )
        near[pair] = own, queries, keys[NEAR:], values[NEAR:], state

    take_extra()

    @pl.when(is_first)
    def _():
        below = [jnp.where(column_of(token) < shift, 1, 0) for token in (query_token, key_token)]
        same = (query_row * 2 + below[0]) == (key_row * 2 + below[1])
        back_recv[...] = attend_extra(
            latents[1].astype(F32), extra_up[OWN - EDGE :], extra_down[:EDGE], same
        )

    @pl.when(is_last)
    def _():
        ident = [jnp.full((48, 1), -1, jnp.int32), jnp.full((1, 128), -1, jnp.int32)]
        token = [iota((48, 1), 0), iota((1, 128), 1)]
        for k in range(ROWS + 2 * (WIN_LAT - 1)):
            ident[1] = jnp.where(token[1] // 8 == k, row_ident(k), ident[1])
            ident[0] = jnp.where(token[0] // 8 == k - (WIN_LAT - 1), row_ident(k), ident[0])
        side = [jnp.where(t % GROUP == GROUP - 1, 1, 0) for t in token]
        same = (ident[0] * 2 + side[0]) == (ident[1] * 2 + side[1])
        back_edge_recv[...] = attend_extra(
            edge_send[...].astype(F32), extra_up[0:48].astype(F32)[8:], extra_down[0:48].astype(F32)[:40], same
        )

    def attend_window(pair):
        own, queries, keys, values, state = near[pair]
        take_rows(pair)
        halo = jnp.concatenate(
            [up_recv[pair].astype(F32)[OWN - EDGE :], down_recv[pair].astype(F32)[:EDGE]], axis=0
        )
        halo = dot(layer_norm(halo).astype(BF16), qkv[:, D:])
        keys, values = around(keys, halo[:, :D]), around(values, halo[:, D:])
        far_token = iota((1, 2 * EDGE + OWN - NEAR), 1)
        far_token = jnp.where(far_token < EDGE, far_token, far_token + NEAR)
        far_row = jnp.full(far_token.shape, -1, jnp.int32)
        for k in range(ROWS + 2 * (WIN_LAT - 1)):
            far_row = jnp.where(far_token // LINE == k, row_ident(k), far_row)

        def wrapped(token):
            if pair == 0:
                return jnp.where((column_of(token) == COLS - 1) & (sector == 0), 1, 0)
            return jnp.where((column_of(token) < shift) & (sector == sectors - 1), 1, 0)

        same = (query_row * 2 + wrapped(query_token)) == (far_row * 2 + wrapped(far_token))
        mixed = attend_far(queries, keys, values, jnp.where(same, 0.0, MASKED), state)
        return own + dot(mixed, wo[...])

    backs = []
    encoded[1] = attend_window(1).astype(BF16)
    back = remote(encoded.at[1], back_recv, back_send_sem.at[0], back_recv_sem.at[0], var=right)
    pl.when(has_right)(functools.partial(start_copy, back))
    backs.append(back)
    done = attend_window(0)
    encoded[0, 0:48] = quads_of(done, True).astype(BF16)
    back = remote(
        encoded.at[0, pl.ds(0, 48)], back_edge_recv, back_send_sem.at[1], back_recv_sem.at[1], var=left
    )
    pl.when(has_left)(functools.partial(start_copy, back))
    backs.append(back)
    first_rest = quads_of(done, False)

    swap = jnp.where(shift_ref[1] > shift_ref[0], 1, 0)
    row = iota((2 * OWN, OWN), 0)
    level = row % LEVELS
    place = row // 48 * LINE + row % 48 // 16 * 8 + level % 2 * GROUP + row % 16 // LEVELS
    hit = place == iota((2 * OWN, OWN), 1)
    orders = [
        jnp.where(hit & (level // 2 == (swap if pair == 0 else 1 - swap)), 1.0, 0.0).astype(BF16)
        for pair in range(2)
    ]
    pl.when(has_right)(lambda: wait_received(backs[1]))
    first_pair = with_last_column(
        first_rest, encoded[0, 0:48].astype(F32), back_edge_recv[...].astype(F32)
    )
    result = dot(orders[0], first_pair.astype(BF16))
    pl.when(has_left)(lambda: wait_received(backs[0]))
    column = column_of(iota((OWN, D), 0))
    second_pair = jnp.where(column < shift, back_recv[...].astype(F32), encoded[1].astype(F32))
    result = result + dot(orders[1], second_pair.astype(BF16))
    out_ref[...] = result.reshape(ROWS, COLS, LEVELS, D).astype(BF16)

    for k in range(1, sectors):
        pixel_copy(k, lax.rem(sector + k, sectors), sector).wait_send()
    for chunk in range(CHUNKS):
        edge_copy, col_copy = column_copies(chunk)
        pl.when(has_right)(functools.partial(wait_sent, edge_copy))
        pl.when(has_left)(functools.partial(wait_sent, col_copy))
        for where, copy in extra_copies(chunk):
            pl.when(where)(functools.partial(wait_sent, copy))
        for pair in range(2):
            upward, downward = row_copies(pair, chunk)

            @pl.when(has_up)
            def _():
                upward.wait_send()

            @pl.when(has_down)
            def _():
                downward.wait_send()

    for back, where in zip(backs, (has_right, has_left)):
        pl.when(where)(functools.partial(wait_sent, back))


def shards(
    fields, field_ids, embed_w, lat_query, perc_wk, perc_wv, swin_qkv, swin_wo, row_window, lon_shift
):
    vmem = pl.BlockSpec(memory_space=pltpu.VMEM)
    smem = pl.BlockSpec(memory_space=pltpu.SMEM)
    hbm = pl.BlockSpec(memory_space=pltpu.HBM)
    encoded = pl.pallas_call(
        whole_kernel,
        out_shape=jax.ShapeDtypeStruct((ROWS, COLS, LEVELS, D), BF16),
        in_specs=[smem] * 3 + [vmem] * 2 + [hbm] * 5,
        out_specs=vmem,
        scratch_shapes=[
            pltpu.VMEM((FIELDS, PIX, D), BF16),
            pltpu.VMEM((D, D), BF16),
            pltpu.VMEM((D, D), BF16),
            pltpu.VMEM((D, 3 * D), BF16),
            pltpu.VMEM((D, D), BF16),
            pltpu.VMEM((FIELDS * PIX, D), BF16),
            pltpu.VMEM((D, 256), BF16),
            pltpu.VMEM((256, 256), F32),
            pltpu.VMEM((ROWS * COLS, FIELDS, D), BF16),
            pltpu.VMEM((HEADS, 2 * OWN, D), BF16),
            pltpu.VMEM((16, D), F32),
            pltpu.VMEM((8, 80, 128), F32),
            pltpu.VMEM((8, 80, 128), BF16),
            pltpu.VMEM((8, 80, 128), BF16),
            pltpu.VMEM((ROWS, 16, 256), F32),
            pltpu.VMEM((2, OWN, D), BF16),
            pltpu.VMEM((2, OWN, D), BF16),
            pltpu.VMEM((48, D), BF16),
            pltpu.VMEM((48, D), BF16),
            pltpu.VMEM((OWN, D), BF16),
            pltpu.VMEM((2, OWN, D), BF16),
            pltpu.VMEM((2, OWN, D), BF16),
            pltpu.VMEM((2, OWN, D), BF16),
            pltpu.VMEM((48, D), BF16),
            pltpu.VMEM((OWN, D), BF16),
            pltpu.SemaphoreType.DMA((5,)),
            pltpu.SemaphoreType.DMA((8,)),
            pltpu.SemaphoreType.DMA((8,)),
            pltpu.SemaphoreType.DMA((2, CHUNKS)),
            pltpu.SemaphoreType.DMA((2, CHUNKS)),
            pltpu.SemaphoreType.DMA((2, 2, CHUNKS)),
            pltpu.SemaphoreType.DMA((2, 2, CHUNKS)),
            pltpu.SemaphoreType.DMA((2,)),
            pltpu.SemaphoreType.DMA((2,)),
            pltpu.VMEM((OWN, D), BF16),
            pltpu.VMEM((OWN, D), BF16),
            pltpu.SemaphoreType.DMA((2, CHUNKS)),
            pltpu.SemaphoreType.DMA((2, CHUNKS)),
            pltpu.VMEM((HEADS, D, 256), BF16),
        ],
        compiler_params=pltpu.CompilerParams(
            vmem_limit_bytes=63 << 20, collective_id=0, has_side_effects=True
        ),
        name="whole",
    )(
        field_ids, lon_shift, row_window, fields, lat_query, embed_w, perc_wk, perc_wv, swin_qkv, swin_wo
    )
    return jnp.transpose(encoded, (2, 0, 1, 3))


def solution(mesh):
    in_specs = (P("var", "lat", None), P(), P(), P(), P(), P(), P(), P(), P(), P())
    out_specs = P(None, "lat", "var", None)
    return jax.shard_map(shards, mesh=mesh, in_specs=in_specs, out_specs=out_specs, check_vma=False)
```

```python
import functools
import math

import jax
import jax.numpy as jnp
from jax import lax
from jax.experimental import pallas as pl
from jax.experimental.pallas import tpu as pltpu
from jax.sharding import PartitionSpec as P

D = 512
HEADS = 16
HEAD = 32
LEVELS = 4
PATCH = 4
WIN_LAT = 6
WIN_LON = 12
FIELDS = 64
ROWS = 6
COLS = 12
PIX = PATCH * PATCH
GROUP = 4
QUADS = COLS // GROUP
LINE = 2 * COLS
OWN = ROWS * LINE
HALO = 128
KEYS = 384
EDGE = 120

EPSILON = 1e-05
MASKED = -1e30
EXP2_SCALE = math.log2(math.e) / math.sqrt(HEAD)
F32 = jnp.float32
BF16 = jnp.bfloat16
NT = (((1,), (1,)), ((), ()))
TN = (((0,), (0,)), ((), ()))
MESH = pl.DeviceIdType.MESH
SEND_ORDER = (7, 1, 6, 2, 5, 3, 4)
CHUNKS = 3
EMBED_STEP = 6
MERGE_STEP = 6
NEAR = 128
CHUNK = 2 * LINE
UP_PARTS = ((0, 48), (48, 48), (96, 32))
DOWN_PARTS = ((16, 32), (48, 48), (96, 48))


def dot(a, b):
    return jnp.dot(a, b, preferred_element_type=F32)


def iota(shape, dim):
    return lax.broadcasted_iota(jnp.int32, shape, dim)


def layer_norm(values):
    row_mean = jnp.sum(values, axis=-1, keepdims=True) * (1.0 / D)
    centred = values - row_mean
    variance = jnp.sum(centred * centred, axis=-1, keepdims=True) * (1.0 / D)
    return centred * lax.rsqrt(variance + EPSILON)


def softmax_rows(scores):
    row_top = jnp.max(scores, axis=-1, keepdims=True)
    lifted = jnp.exp2(scores - row_top)
    return lifted * (1.0 / jnp.sum(lifted, axis=-1, keepdims=True))


def column_of(token):
    return (token % LINE) // 8 * GROUP + token % GROUP


def remote(src, dst, send_sem, recv_sem, **device):
    return pltpu.make_async_remote_copy(
        src_ref=src, dst_ref=dst, send_sem=send_sem, recv_sem=recv_sem,
        device_id=device, device_id_type=MESH,
    )


def start_copy(copy):
    copy.start()


def wait_received(copy):
    copy.wait_recv()


def wait_sent(copy):
    copy.wait_send()


def attention(queries, keys, values, bias):
    count, key_count = queries.shape[0], keys.shape[0]
    lane_head = iota((count, 256), 1) // HEAD
    halves = []
    for half in range(2):
        cut = slice(256 * half, 256 * half + 256)
        part = queries[:, cut]
        stacked = jnp.concatenate(
            [jnp.where(lane_head == h, part, 0.0).astype(BF16) for h in range(8)], axis=0
        )
        scores = lax.dot_general(stacked, keys[:, cut], NT, preferred_element_type=F32)
        scores = scores.reshape(8, count, key_count) * EXP2_SCALE + bias[None]
        weights = softmax_rows(scores).astype(BF16).reshape(8 * count, key_count)
        mixed = dot(weights, values[:, cut]).reshape(8, count, 256)
        total = jnp.zeros((count, 256), F32)
        for h in range(8):
            total = jnp.where(lane_head == h, mixed[h], total)
        halves.append(total.astype(BF16))
    return jnp.concatenate(halves, axis=-1)


def split_values(wv, value_scr):
    lane_head = iota((D, 256), 1) // HEAD
    for half in range(2):
        value_w = wv[:, 256 * half : 256 * half + 256].astype(F32)
        for head in range(8):
            value_scr[8 * half + head] = jnp.where(lane_head == head, value_w, 0.0).astype(BF16)


def heads_apart(queries):
    lane_head = iota(queries.shape, 1) // HEAD
    return jnp.concatenate(
        [jnp.where(lane_head == h, queries, 0.0).astype(BF16) for h in range(8)], axis=0
    )


def heads_together(stacked):
    lane_head = iota((stacked.shape[1], 256), 1) // HEAD
    total = jnp.broadcast_to(stacked[0], lane_head.shape)
    for h in range(1, 8):
        total = jnp.where(lane_head == h, stacked[h], total)
    return total


def attend_near(queries, keys, values, bias):
    count, key_count = bias.shape
    state = []
    for half in range(2):
        cut = slice(256 * half, 256 * half + 256)
        scores = lax.dot_general(
            heads_apart(queries[:, cut]), keys[:, cut], NT, preferred_element_type=F32
        )
        scores = scores.reshape(8, count, key_count) * EXP2_SCALE + bias[None]
        top = jnp.max(scores, axis=-1, keepdims=True)
        lifted = jnp.exp2(scores - top)
        total = jnp.sum(lifted, axis=-1, keepdims=True)
        mixed = dot(lifted.astype(BF16).reshape(8 * count, key_count), values[:, cut])
        state.append((top, total, heads_together(mixed.reshape(8, count, 256))))
    return state


def attend_far(queries, keys, values, bias, state):
    count, key_count = bias.shape
    halves = []
    for half, (near_top, near_total, near_mixed) in enumerate(state):
        cut = slice(256 * half, 256 * half + 256)
        scores = lax.dot_general(
            heads_apart(queries[:, cut]), keys[:, cut], NT, preferred_element_type=F32
        )
        scores = scores.reshape(8, count, key_count) * EXP2_SCALE + bias[None]
        top = jnp.maximum(near_top, jnp.max(scores, axis=-1, keepdims=True))
        lifted = jnp.exp2(scores - top)
        near_scale = jnp.exp2(near_top - top)
        total = near_scale * near_total + jnp.sum(lifted, axis=-1, keepdims=True)
        inverse = 1.0 / total
        mixed = dot(
            (lifted * inverse).astype(BF16).reshape(8 * count, key_count), values[:, cut]
        )
        mixed = heads_together(mixed.reshape(8, count, 256))
        mixed = mixed + near_mixed * heads_together(near_scale * inverse)
        halves.append(mixed.astype(BF16))
    return jnp.concatenate(halves, axis=-1)


def pick_pixels(fields, stage, send):
    flat = fields.astype(F32).reshape(8 * ROWS * PATCH, 384).astype(BF16)
    row = iota((512, 1), 0)
    column = row % 16
    source = jnp.where(column < COLS, (row % 128) // 16 * 48 + column * PATCH + row // 128, -1)
    pick = jnp.where(source == iota((512, 384), 1), 1.0, 0.0).astype(BF16)
    turned = lax.dot_general(pick, flat, NT, preferred_element_type=F32).astype(BF16)
    row = iota((192, 1), 0)
    target = (row // PATCH) % ROWS * 128 + row // (ROWS * PATCH) * PIX + row % PATCH * PATCH
    lane = iota((192, 768), 1)
    total = jnp.zeros((128, 768), F32)
    for j in range(PATCH):
        place = jnp.where(target + j == lane, 1.0, 0.0).astype(BF16)
        total = total + dot(turned[128 * j : 128 * j + 128], place)
    for sector in range(8):
        stage[sector, 72:80, :] = jnp.zeros((8, 128), F32)
        for line in range(ROWS):
            stage[sector, COLS * line : COLS * line + COLS, :] = total[
                16 * sector : 16 * sector + COLS, 128 * line : 128 * line + 128
            ]
    send[...] = stage[...].astype(BF16)


def prepare_weights(ids_ref, shift_ref, embed, query_ref, wk, slot_w, keys_scr, bias_scr, query_scr):
    def place(slot, carry):
        start = pl.multiple_of(slot * PIX, PIX)
        slot_w[pl.ds(start, PIX), :] = embed[ids_ref[slot]]
        return carry

    lax.fori_loop(0, FIELDS, place, 0)
    swap = shift_ref[1] > shift_ref[0]
    query = query_ref[...].astype(F32)
    swapped = jnp.concatenate([query[2:], query[:2]], axis=0)
    query = jnp.where(swap, swapped, query)
    level = (iota((256, D), 0) // GROUP) % LEVELS
    spread = jnp.zeros((256, D), F32)
    for lev in range(LEVELS):
        spread = jnp.where(level == lev, query[lev : lev + 1, :], spread)
    query_scr[...] = spread[:16]
    own_head = iota((256, D), 1) // HEAD == iota((256, D), 0) // 16
    masked = jnp.where(own_head, spread, 0.0).astype(BF16)
    keys_scr[...] = lax.dot_general(
        wk[...], masked, NT, preferred_element_type=F32
    ).astype(BF16)
    same = iota((256, 256), 0) // FIELDS == iota((256, 256), 1) % GROUP
    bias_scr[...] = jnp.where(same, 0.0, MASKED)


def embed_line(line, part, line_pixels, slot_w, normed_scr):
    own_slot = iota((1, 16, 256), 2) // PIX == iota((1, 16, 256), 1)
    pixels = line_pixels[line][:COLS]
    spread = jnp.where(own_slot, pixels[:, None, :], 0.0).astype(BF16)
    weight = slot_w[pl.ds(pl.multiple_of(256 * part, 256), 256), :]
    tokens = dot(spread.reshape(COLS * 16, 256), weight)
    normed = layer_norm(tokens).astype(BF16)
    slots = pl.ds(pl.multiple_of(16 * part, 16), 16)
    normed_scr[pl.ds(line * COLS, COLS), slots, :] = normed.reshape(COLS, 16, D)


def merge_quad(quad, keys_scr, bias_scr, normed_scr, pooled_scr):
    normed = normed_scr[pl.ds(quad * GROUP, GROUP)].reshape(GROUP * FIELDS, D)
    scores = dot(normed, keys_scr[...]) * EXP2_SCALE + bias_scr[...]
    lifted = jnp.exp2(scores - jnp.max(scores, axis=0, keepdims=True))
    weights = (lifted * (1.0 / jnp.sum(lifted, axis=0, keepdims=True))).astype(BF16)
    pooled = lax.dot_general(weights, normed, TN, preferred_element_type=F32).astype(BF16)
    start = pl.multiple_of(quad * 16, 16)
    pooled_scr[:, pl.ds(start, 16), :] = pooled.reshape(HEADS, 16, D)


def project(chunk, pooled_scr, value_scr, query_scr):
    start = pl.multiple_of(chunk * 2 * CHUNK, 2 * CHUNK)
    halves = []
    for half in range(2):
        total = jnp.zeros((2 * CHUNK, 256), F32)
        for head in range(8 * half, 8 * half + 8):
            total = total + dot(pooled_scr[head, pl.ds(start, 2 * CHUNK), :], value_scr[head])
        halves.append(total)
    projected = jnp.concatenate(halves, axis=-1).reshape(2 * QUADS, 16, D)
    return projected + query_scr[...][None]


def quads_of(tokens, last):
    width = tokens.shape[-1]
    tokens = tokens.reshape(tokens.shape[0] // 8, 8, width)
    picked = [q for q in range(tokens.shape[0]) if (q % QUADS == QUADS - 1) == last]
    return jnp.concatenate([tokens[q] for q in picked], axis=0)


def with_last_column(rest, own, received):
    is_last = iota(own.shape, 0) % GROUP == GROUP - 1
    last = jnp.where(is_last, received, own)
    pieces = []
    for r in range(own.shape[0] // 8):
        pieces += [rest[16 * r : 16 * r + 16], last[8 * r : 8 * r + 8]]
    return jnp.concatenate(pieces, axis=0)


def whole_kernel(
    ids_ref, shift_ref, window_ref, fields_ref, query_ref, embed_h, wk_h, wv_h, qkv_h, wo_h, out_ref,
    embed, wk, wv, qkv, wo, slot_w, keys_scr, bias_scr, normed_scr, pooled_scr, query_scr,
    stage, send, recv, line_pixels, latents, slab, edge_send, edge_recv, col_recv, up_recv, down_recv,
    encoded, back_edge_recv, back_recv,
    load_sem, pix_send_sem, pix_recv_sem, col_send_sem, col_recv_sem, row_send_sem, row_recv_sem,
    back_send_sem, back_recv_sem, extra_up, extra_down, extra_send_sem, extra_recv_sem,
    value_scr,
):
    sector = lax.axis_index("var")
    sectors = lax.axis_size("var")
    band = lax.axis_index("lat")
    bands = lax.axis_size("lat")
    right = lax.rem(sector + 1, sectors)
    left = lax.rem(sector + sectors - 1, sectors)
    is_first = sector == 0
    is_last = sector == sectors - 1
    is_end = is_first | is_last
    has_left = jnp.logical_not(is_first)
    has_right = jnp.logical_not(is_last)
    has_up = band > 0
    has_down = band < bands - 1

    barrier = pltpu.get_barrier_semaphore()
    for k in range(1, sectors):
        pl.semaphore_signal(
            barrier, inc=1, device_id={"var": lax.rem(sector + k, sectors)}, device_id_type=MESH
        )

    @pl.when(has_up)
    def _():
        pl.semaphore_signal(barrier, inc=1, device_id={"lat": band - 1}, device_id_type=MESH)

    @pl.when(has_down)
    def _():
        pl.semaphore_signal(barrier, inc=1, device_id={"lat": band + 1}, device_id_type=MESH)

    loads = [
        pltpu.make_async_copy(src, dst, load_sem.at[i])
        for i, (src, dst) in enumerate(
            [(embed_h, embed), (wk_h, wk), (wv_h, wv), (qkv_h, qkv), (wo_h, wo)]
        )
    ]
    for load in loads:
        load.start()

    pick_pixels(fields_ref[...], stage, send)

    @pl.when(jnp.logical_not(has_up))
    def _():
        up_recv[...] = jnp.zeros_like(up_recv)

    @pl.when(jnp.logical_not(has_down))
    def _():
        down_recv[...] = jnp.zeros_like(down_recv)

    @pl.when((band == 0) & is_end)
    def _():
        extra_up[...] = jnp.zeros_like(extra_up)

    @pl.when((band == bands - 1) & is_end)
    def _():
        extra_down[...] = jnp.zeros_like(extra_down)

    @pl.when(is_first)
    def _():
        edge_recv[...] = jnp.zeros_like(edge_recv)

    @pl.when(is_last)
    def _():
        col_recv[...] = jnp.zeros_like(col_recv)

    neighbours = jnp.where(has_up, 1, 0) + jnp.where(has_down, 1, 0)
    pl.semaphore_wait(barrier, sectors - 1 + neighbours)

    def pixel_copy(k, peer, slot):
        return remote(
            send.at[peer], recv.at[slot], pix_send_sem.at[k], pix_recv_sem.at[k], var=peer
        )

    for k in SEND_ORDER:
        pixel_copy(k, lax.rem(sector + k, sectors), sector).start()
    recv[sector] = send[sector]

    loads[0].wait()
    loads[1].wait()
    prepare_weights(
        ids_ref, shift_ref, embed, query_ref, wk, slot_w, keys_scr, bias_scr, query_scr
    )
    loads[2].wait()
    split_values(wv, value_scr)

    def one_part(turn, carry):
        own = sector // 2
        part = lax.rem(own // 2 + turn // 2, 2) * 2 + lax.rem(own % 2 + turn % 2, 2)
        for side in range(2):
            source = part * 2 + side

            @pl.when(source != sector)
            def _():
                pixel_copy(lax.rem(sector + sectors - source, sectors), source, source).wait_recv()

            stage[side] = recv[source].astype(F32)
            for line in range(ROWS):
                line_pixels[line, 0:COLS, 128 * side : 128 * side + 128] = stage[
                    side, COLS * line : COLS * line + COLS, :
                ]

        def lines(step, carry):
            for k in range(EMBED_STEP):
                embed_line(step * EMBED_STEP + k, part, line_pixels, slot_w, normed_scr)
            return carry

        lax.fori_loop(0, ROWS // EMBED_STEP, lines, 0)
        return carry

    lax.fori_loop(0, 4, one_part, 0)

    shift = jnp.minimum(shift_ref[0], shift_ref[1])

    def column_copies(chunk):
        quads = pl.ds(pl.multiple_of(chunk * 16, 16), 16)
        tokens = pl.ds(pl.multiple_of(chunk * CHUNK, 16), CHUNK)
        return (
            remote(
                edge_send.at[quads], edge_recv.at[quads],
                col_send_sem.at[0, chunk], col_recv_sem.at[0, chunk], var=right,
            ),
            remote(
                latents.at[1, tokens], col_recv.at[tokens],
                col_send_sem.at[1, chunk], col_recv_sem.at[1, chunk], var=left,
            ),
        )

    def extra_copies(chunk):
        quads = pl.ds(pl.multiple_of(chunk * 16, 16), 16)
        tokens = pl.ds(pl.multiple_of(chunk * CHUNK, 16), CHUNK)
        copies = []
        for end, src, part in ((is_first, latents.at[1, tokens], tokens), (is_last, edge_send.at[quads], quads)):
            copies.append((end & has_up, remote(
                src, extra_down.at[part], extra_send_sem.at[0, chunk], extra_recv_sem.at[0, chunk], lat=band - 1
            )))
            copies.append((end & has_down, remote(
                src, extra_up.at[part], extra_send_sem.at[1, chunk], extra_recv_sem.at[1, chunk], lat=band + 1
            )))
        return copies

    def take_extra():
        for chunk in range(CHUNKS):
            for i, (_, copy) in enumerate(extra_copies(chunk)):
                end = is_first if i < 2 else is_last
                pl.when(end & (has_down if i % 2 == 0 else has_up))(functools.partial(wait_received, copy))

    def row_copies(pair, chunk):
        (up_start, up_count), (down_start, down_count) = UP_PARTS[chunk], DOWN_PARTS[chunk]
        up_part, down_part = pl.ds(up_start, up_count), pl.ds(down_start, down_count)
        upward = remote(
            slab.at[pair, up_part], down_recv.at[pair, up_part],
            row_send_sem.at[pair, 0, chunk], row_recv_sem.at[pair, 0, chunk], lat=band - 1,
        )
        downward = remote(
            slab.at[pair, down_part], up_recv.at[pair, down_part],
            row_send_sem.at[pair, 1, chunk], row_recv_sem.at[pair, 1, chunk], lat=band + 1,
        )
        return upward, downward

    def send_rows(pair, chunk):
        upward, downward = row_copies(pair, chunk)

        @pl.when(has_up)
        def _():
            upward.start()

        @pl.when(has_down)
        def _():
            downward.start()

    def take_rows(pair):
        for chunk in range(CHUNKS):
            upward, downward = row_copies(pair, chunk)

            @pl.when(has_down)
            def _():
                upward.wait_recv()

            @pl.when(has_up)
            def _():
                downward.wait_recv()

    def share_rows(chunk):
        edge_copy, col_copy = column_copies(chunk)
        tokens = slice(CHUNK * chunk, CHUNK * chunk + CHUNK)
        quads = slice(16 * chunk, 16 * chunk + 16)
        pl.when(has_right)(lambda: wait_received(col_copy))
        column = column_of(iota((CHUNK, D), 0))
        slab[1, tokens] = jnp.where(
            column < shift, col_recv[tokens].astype(F32), latents[1, tokens].astype(F32)
        ).astype(BF16)
        send_rows(1, chunk)
        pl.when(has_left)(lambda: wait_received(edge_copy))
        own = latents[0, tokens].astype(F32)
        slab[0, tokens] = with_last_column(
            quads_of(own, False), quads_of(own, True), edge_recv[quads].astype(F32)
        ).astype(BF16)
        send_rows(0, chunk)


    def one_chunk(chunk, carry):
        def quads(step, carry):
            for k in range(MERGE_STEP):
                quad = chunk * 2 * QUADS + step * MERGE_STEP + k
                merge_quad(quad, keys_scr, bias_scr, normed_scr, pooled_scr)
            return carry

        lax.fori_loop(0, 2 * QUADS // MERGE_STEP, quads, 0)
        fresh = project(chunk, pooled_scr, value_scr, query_scr)
        start = pl.multiple_of(chunk * CHUNK, 16)
        for pair in range(2):
            tokens = fresh[:, 8 * pair : 8 * pair + 8].reshape(CHUNK, D)
            latents[pair, pl.ds(start, CHUNK), :] = tokens.astype(BF16)
            if pair == 0:
                quads = pl.ds(pl.multiple_of(chunk * 16, 16), 16)
                edge_send[quads, :] = quads_of(tokens, True).astype(BF16)
        edge_copy, col_copy = column_copies(chunk)
        pl.when(has_right)(lambda: start_copy(edge_copy))
        pl.when(has_left)(lambda: start_copy(col_copy))
        for where, copy in extra_copies(chunk):
            pl.when(where)(functools.partial(start_copy, copy))
        for ready in range(CHUNKS - 1):
            @pl.when(chunk == ready + 1)
            def _():
                share_rows(ready)

        return carry

    lax.fori_loop(0, CHUNKS, one_chunk, 0)
    first = band * ROWS - (WIN_LAT - 1)
    total_rows = window_ref.shape[0]

    def row_ident(k):
        row = first + k
        inside = (row >= 0) & (row < total_rows)
        return jnp.where(inside, window_ref[jnp.clip(row, 0, total_rows - 1)], -1)

    key_token = iota((1, KEYS), 1)
    query_token = iota((OWN, 1), 0)
    key_row = jnp.full((1, KEYS), -1, jnp.int32)
    query_row = jnp.full((OWN, 1), -1, jnp.int32)
    for k in range(ROWS + 2 * (WIN_LAT - 1)):
        ident = row_ident(k)
        key_row = jnp.where(key_token // LINE == k, ident, key_row)
        if 0 <= k - (WIN_LAT - 1) < ROWS:
            query_row = jnp.where(query_token // LINE == k - (WIN_LAT - 1), ident, query_row)

    loads[3].wait()
    loads[4].wait()
    def around(own_part, halo_part):
        edge = halo_part.shape[0] // 2
        return jnp.concatenate([halo_part[:edge], own_part, halo_part[edge:]], axis=0).astype(BF16)

    def attend_extra(own, up, down, same):
        own_qkv = dot(layer_norm(own).astype(BF16), qkv[...])
        halo = jnp.concatenate([up.astype(F32), down.astype(F32)], axis=0)
        halo = dot(layer_norm(halo).astype(BF16), qkv[:, D:])
        keys = around(own_qkv[:, D : 2 * D], halo[:, :D])
        values = around(own_qkv[:, 2 * D :], halo[:, D:])
        mixed = attention(own_qkv[:, :D], keys, values, jnp.where(same, 0.0, MASKED))
        return (own + dot(mixed, wo[...])).astype(BF16)

    def window_bias(pair):
        def wrapped(token):
            if pair == 0:
                return jnp.where((column_of(token) == COLS - 1) & (sector == 0), 1, 0)
            return jnp.where((column_of(token) < shift) & (sector == sectors - 1), 1, 0)

        same = (query_row * 2 + wrapped(query_token)) == (key_row * 2 + wrapped(key_token))
        return jnp.where(same, 0.0, MASKED)

    biases = [window_bias(pair)[:, EDGE : EDGE + NEAR] for pair in range(2)]
    share_rows(CHUNKS - 1)
    near = {}
    for pair in (1, 0):
        own = slab[pair].astype(F32)
        own_qkv = dot(layer_norm(own).astype(BF16), qkv[...])
        queries, keys, values = own_qkv[:, :D], own_qkv[:, D : 2 * D], own_qkv[:, 2 * D :]
        state = attend_near(
            queries, keys[:NEAR].astype(BF16), values[:NEAR].astype(BF16), biases[pair]
        )
        near[pair] = own, queries, keys[NEAR:], values[NEAR:], state

    take_extra()

    @pl.when(is_first)
    def _():
        below = [jnp.where(column_of(token) < shift, 1, 0) for token in (query_token, key_token)]
        same = (query_row * 2 + below[0]) == (key_row * 2 + below[1])
        back_recv[...] = attend_extra(
            latents[1].astype(F32), extra_up[OWN - EDGE :], extra_down[:EDGE], same
        )

    @pl.when(is_last)
    def _():
        ident = [jnp.full((48, 1), -1, jnp.int32), jnp.full((1, 128), -1, jnp.int32)]
        token = [iota((48, 1), 0), iota((1, 128), 1)]
        for k in range(ROWS + 2 * (WIN_LAT - 1)):
            ident[1] = jnp.where(token[1] // 8 == k, row_ident(k), ident[1])
            ident[0] = jnp.where(token[0] // 8 == k - (WIN_LAT - 1), row_ident(k), ident[0])
        side = [jnp.where(t % GROUP == GROUP - 1, 1, 0) for t in token]
        same = (ident[0] * 2 + side[0]) == (ident[1] * 2 + side[1])
        back_edge_recv[...] = attend_extra(
            edge_send[...].astype(F32), extra_up[0:48].astype(F32)[8:], extra_down[0:48].astype(F32)[:40], same
        )

    def attend_window(pair):
        own, queries, keys, values, state = near[pair]
        take_rows(pair)
        halo = jnp.concatenate(
            [up_recv[pair].astype(F32)[OWN - EDGE :], down_recv[pair].astype(F32)[:EDGE]], axis=0
        )
        halo = dot(layer_norm(halo).astype(BF16), qkv[:, D:])
        keys, values = around(keys, halo[:, :D]), around(values, halo[:, D:])
        far_token = iota((1, 2 * EDGE + OWN - NEAR), 1)
        far_token = jnp.where(far_token < EDGE, far_token, far_token + NEAR)
        far_row = jnp.full(far_token.shape, -1, jnp.int32)
        for k in range(ROWS + 2 * (WIN_LAT - 1)):
            far_row = jnp.where(far_token // LINE == k, row_ident(k), far_row)

        def wrapped(token):
            if pair == 0:
                return jnp.where((column_of(token) == COLS - 1) & (sector == 0), 1, 0)
            return jnp.where((column_of(token) < shift) & (sector == sectors - 1), 1, 0)

        same = (query_row * 2 + wrapped(query_token)) == (far_row * 2 + wrapped(far_token))
        mixed = attend_far(queries, keys, values, jnp.where(same, 0.0, MASKED), state)
        return own + dot(mixed, wo[...])

    backs = []
    encoded[1] = attend_window(1).astype(BF16)
    back = remote(encoded.at[1], back_recv, back_send_sem.at[0], back_recv_sem.at[0], var=right)
    pl.when(has_right)(functools.partial(start_copy, back))
    backs.append(back)
    done = attend_window(0)
    encoded[0, 0:48] = quads_of(done, True).astype(BF16)
    back = remote(
        encoded.at[0, pl.ds(0, 48)], back_edge_recv, back_send_sem.at[1], back_recv_sem.at[1], var=left
    )
    pl.when(has_left)(functools.partial(start_copy, back))
    backs.append(back)
    first_rest = quads_of(done, False)

    swap = jnp.where(shift_ref[1] > shift_ref[0], 1, 0)
    row = iota((2 * OWN, OWN), 0)
    level = row % LEVELS
    place = row // 48 * LINE + row % 48 // 16 * 8 + level % 2 * GROUP + row % 16 // LEVELS
    hit = place == iota((2 * OWN, OWN), 1)
    orders = [
        jnp.where(hit & (level // 2 == (swap if pair == 0 else 1 - swap)), 1.0, 0.0).astype(BF16)
        for pair in range(2)
    ]
    pl.when(has_right)(lambda: wait_received(backs[1]))
    first_pair = with_last_column(
        first_rest, encoded[0, 0:48].astype(F32), back_edge_recv[...].astype(F32)
    )
    result = dot(orders[0], first_pair.astype(BF16))
    pl.when(has_left)(lambda: wait_received(backs[0]))
    column = column_of(iota((OWN, D), 0))
    second_pair = jnp.where(column < shift, back_recv[...].astype(F32), encoded[1].astype(F32))
    result = result + dot(orders[1], second_pair.astype(BF16))
    out_ref[...] = result.reshape(ROWS, COLS, LEVELS, D).astype(BF16)

    for k in range(1, sectors):
        pixel_copy(k, lax.rem(sector + k, sectors), sector).wait_send()
    for chunk in range(CHUNKS):
        edge_copy, col_copy = column_copies(chunk)
        pl.when(has_right)(functools.partial(wait_sent, edge_copy))
        pl.when(has_left)(functools.partial(wait_sent, col_copy))
        for where, copy in extra_copies(chunk):
            pl.when(where)(functools.partial(wait_sent, copy))
        for pair in range(2):
            upward, downward = row_copies(pair, chunk)

            @pl.when(has_up)
            def _():
                upward.wait_send()

            @pl.when(has_down)
            def _():
                downward.wait_send()

    for back, where in zip(backs, (has_right, has_left)):
        pl.when(where)(functools.partial(wait_sent, back))


def shards(
    fields, field_ids, embed_w, lat_query, perc_wk, perc_wv, swin_qkv, swin_wo, row_window, lon_shift
):
    vmem = pl.BlockSpec(memory_space=pltpu.VMEM)
    smem = pl.BlockSpec(memory_space=pltpu.SMEM)
    hbm = pl.BlockSpec(memory_space=pltpu.HBM)
    encoded = pl.pallas_call(
        whole_kernel,
        out_shape=jax.ShapeDtypeStruct((ROWS, COLS, LEVELS, D), BF16),
        in_specs=[smem] * 3 + [vmem] * 2 + [hbm] * 5,
        out_specs=vmem,
        scratch_shapes=[
            pltpu.VMEM((FIELDS, PIX, D), BF16),
            pltpu.VMEM((D, D), BF16),
            pltpu.VMEM((D, D), BF16),
            pltpu.VMEM((D, 3 * D), BF16),
            pltpu.VMEM((D, D), BF16),
            pltpu.VMEM((FIELDS * PIX, D), BF16),
            pltpu.VMEM((D, 256), BF16),
            pltpu.VMEM((256, 256), F32),
            pltpu.VMEM((ROWS * COLS, FIELDS, D), BF16),
            pltpu.VMEM((HEADS, 2 * OWN, D), BF16),
            pltpu.VMEM((16, D), F32),
            pltpu.VMEM((8, 80, 128), F32),
            pltpu.VMEM((8, 80, 128), BF16),
            pltpu.VMEM((8, 80, 128), BF16),
            pltpu.VMEM((ROWS, 16, 256), F32),
            pltpu.VMEM((2, OWN, D), BF16),
            pltpu.VMEM((2, OWN, D), BF16),
            pltpu.VMEM((48, D), BF16),
            pltpu.VMEM((48, D), BF16),
            pltpu.VMEM((OWN, D), BF16),
            pltpu.VMEM((2, OWN, D), BF16),
            pltpu.VMEM((2, OWN, D), BF16),
            pltpu.VMEM((2, OWN, D), BF16),
            pltpu.VMEM((48, D), BF16),
            pltpu.VMEM((OWN, D), BF16),
            pltpu.SemaphoreType.DMA((5,)),
            pltpu.SemaphoreType.DMA((8,)),
            pltpu.SemaphoreType.DMA((8,)),
            pltpu.SemaphoreType.DMA((2, CHUNKS)),
            pltpu.SemaphoreType.DMA((2, CHUNKS)),
            pltpu.SemaphoreType.DMA((2, 2, CHUNKS)),
            pltpu.SemaphoreType.DMA((2, 2, CHUNKS)),
            pltpu.SemaphoreType.DMA((2,)),
            pltpu.SemaphoreType.DMA((2,)),
            pltpu.VMEM((OWN, D), BF16),
            pltpu.VMEM((OWN, D), BF16),
            pltpu.SemaphoreType.DMA((2, CHUNKS)),
            pltpu.SemaphoreType.DMA((2, CHUNKS)),
            pltpu.VMEM((HEADS, D, 256), BF16),
        ],
        compiler_params=pltpu.CompilerParams(
            vmem_limit_bytes=63 << 20, collective_id=0, has_side_effects=True
        ),
        name="whole",
    )(
        field_ids, lon_shift, row_window, fields, lat_query, embed_w, perc_wk, perc_wv, swin_qkv, swin_wo
    )
    return jnp.transpose(encoded, (2, 0, 1, 3))


def solution(mesh):
    in_specs = (P("var", "lat", None), P(), P(), P(), P(), P(), P(), P(), P(), P())
    out_specs = P(None, "lat", "var", None)
    return jax.shard_map(shards, mesh=mesh, in_specs=in_specs, out_specs=out_specs, check_vma=False)
```
